32 devices in a mesh: parts: 2 (over x), tok: 16 (over z, y, core).
Axes of the slice: x: 2, y: 2, z: 4, core: 2. Of those that a mesh axis runs over, the one named last changes fastest.
Arguments:
- queries: bfloat16 [4096, 4096], P(('parts', 'tok')), parts along dimension 0, may hold values from -30 to 30
- keys: bfloat16 [4096, 512], P(('parts', 'tok')), parts along dimension 0, may hold values from -4 to 4
- values: bfloat16 [4096, 512], P(('parts', 'tok')), parts along dimension 0, may hold values from -5 to 5
- outputs: bfloat16 [4096, 4096], P(('parts', 'tok')), parts along dimension 0, may hold values from -3 to 3
- out_grad: bfloat16 [4096, 4096], P(('parts', 'tok')), parts along dimension 0, may hold values from -6 to 6
- ancestors: int32 [32, 10], P('parts'), parts along dimension 0, may hold values from -1 to 14, as said below
Outputs:
- query_grad: bfloat16 [4096, 4096], P(('parts', 'tok')), parts along dimension 0
- key_grad: bfloat16 [4096, 512], P(('parts', 'tok')), parts along dimension 0
- value_grad: bfloat16 [4096, 512], P(('parts', 'tok')), parts along dimension 0
The draws below stay inside these ranges and needn't reach their ends.
There are 2 independent parts, one for each index of `parts`. The reference program is written for one: setup_inputs(seed, part) draws one part's arguments, and reference() takes and returns one part's arrays. A program takes and returns all parts, laid end to end along the dimension named above; each array names one. Nothing has to cross between parts.
Inputs may be any that keep to these rules, and one draw needn't show every extreme that they name: Row t lists the ancestor tiles of tile t, from its parent up to tile 0, each once, then -1 to the end. Every listed tile is earlier than t; tile 0 is an ancestor of every other tile and has none; some tile has exactly 10 ancestors.
All inputs are finite; a program needn't handle non-finite values.
Results may differ from the reference program's by a relative error of at most 0.0053.
Values may be sent and summed in bfloat16 or wider, within the bound.
No kernel may reach another device: no remote copies, remote signals or barrier semaphores. Data moves between devices by JAX's collectives and lax.ppermute only.
A program may use at most 128 MiB of HBM per device.

```python
import jax
import jax.numpy as jnp
from jax import lax

QH = 32
KVH = 4
HD = 128
TILE = 128
NT = 16
TOKENS = 2048
DEPTH = 10


def draw_queries(key, part):
    result = jnp.clip(jax.random.normal(jax.random.fold_in(key, 1), (TOKENS, QH, HD), jnp.float32), -4.0, 4.0)
    return result.reshape(TOKENS, QH * HD).astype(jnp.bfloat16)


def draw_keys(key, part):
    result = jnp.clip(jax.random.normal(jax.random.fold_in(key, 2), (TOKENS, KVH, HD), jnp.float32), -4.0, 4.0)
    return result.reshape(TOKENS, KVH * HD).astype(jnp.bfloat16)


def draw_ancestors(key, part):
    base_key = jax.random.fold_in(key, 23)
    chain_key, coin_key, pick_key = jax.random.split(base_key, 3)
    ranking = jnp.argsort(jax.random.randint(chain_key, (NT - 1,), 0, 1 << 30), stable=True).astype(jnp.int32) + 1
    chain = jnp.sort(ranking[:DEPTH]).astype(jnp.int32)
    in_chain = jnp.zeros((NT,), jnp.bool_).at[chain].set(True)
    chain_parent = jnp.zeros((NT,), jnp.int32).at[chain].set(jnp.concatenate([jnp.zeros((1,), jnp.int32), chain[:-1]]))
    coins = jax.random.randint(coin_key, (NT,), 0, 2)
    picks = jax.random.randint(pick_key, (NT,), 0, 1 << 30)

    def place(index, state):
        parents, depths = state
        guess = jnp.where(coins[index] == 1, index - 1, picks[index] % index).astype(jnp.int32)
        guess = jnp.where(depths[guess] >= DEPTH, parents[guess], guess)
        chosen_parent = jnp.where(in_chain[index], chain_parent[index], guess)
        return (parents.at[index].set(chosen_parent), depths.at[index].set(depths[chosen_parent] + 1))
    parents, depths = lax.fori_loop(1, NT, place, (jnp.full((NT,), -1, jnp.int32), jnp.zeros((NT,), jnp.int32)))
    columns = []
    current = parents
    for level in range(DEPTH):
        columns.append(current)
        current = jnp.where(current >= 0, parents[jnp.maximum(current, 0)], -1).astype(jnp.int32)
    return jnp.stack(columns, axis=1).astype(jnp.int32)


def levels(key, extent, cuts, low, largest):
    loudness, own = 1.0, jax.random.fold_in(key, 6)
    for dim, blocks in cuts:
        heights = jnp.exp(jax.random.uniform(jax.random.fold_in(own, dim), (blocks,), jnp.float32, low / len(cuts), largest / len(cuts)))
        loudness = loudness * jnp.repeat(heights, extent[dim] // blocks).reshape([-1 if axis == dim else 1 for axis in range(len(extent))])
    return loudness


def gaussian(stream_key, extent, spread, most, cuts=(), kind=jnp.bfloat16):
    values = spread * jax.random.normal(stream_key, extent, jnp.float32)
    if cuts:
        values = values * levels(stream_key, extent, cuts, -0.22, 0.18)
    return jnp.clip(values, -most, most).astype(kind)


def setup_inputs(seed: int = 0, part: int = 0) -> dict:
    key_of = jax.random.split(jax.random.key(seed), 7)
    part_splits = jax.random.split(jax.random.fold_in(key_of[6], part), 7)
    return {
        "queries": draw_queries(jax.random.fold_in(jax.random.fold_in(key_of[6], part), 71), part),
        "keys": draw_keys(jax.random.fold_in(jax.random.fold_in(key_of[6], part), 71), part),
        "values": gaussian(part_splits[2], (TOKENS, KVH * HD), 1.0, 5.0, ((0, 16),)),
        "outputs": gaussian(part_splits[3], (TOKENS, QH * HD), 0.5, 3.0, ((0, 16),)),
        "out_grad": gaussian(part_splits[4], (TOKENS, QH * HD), 1.0, 6.0, ((0, 16),)),
        "ancestors": draw_ancestors(jax.random.fold_in(jax.random.fold_in(key_of[6], part), 71), part),
    }


def reference(queries, keys, values, outputs, out_grad, ancestors):
    tile_count = ancestors.shape[0]
    slot_count = ancestors.shape[1] + 1
    groups = QH // KVH
    softmax_scale = HD ** -0.5
    query_tiles = queries.reshape(tile_count, TILE, KVH, groups, HD)
    output_tiles = outputs.reshape(tile_count, TILE, KVH, groups, HD)
    grad_tiles = out_grad.reshape(tile_count, TILE, KVH, groups, HD)
    key_tiles = keys.reshape(tile_count, TILE, KVH, HD)
    value_tiles = values.reshape(tile_count, TILE, KVH, HD)
    own_tiles = jnp.arange(tile_count, dtype=jnp.int32)[:, None]
    key_lists = jnp.concatenate([ancestors.astype(jnp.int32), own_tiles], axis=1)
    causal = jnp.arange(TILE)[:, None] >= jnp.arange(TILE)[None, :]
    not_self = jnp.arange(slot_count) != slot_count - 1

    def scan_step(carry, tile_index):
        key_acc, value_acc = carry
        tile_row = key_lists[tile_index]
        is_live = tile_row >= 0
        safe_tiles = jnp.maximum(tile_row, 0).astype(jnp.int32)
        key_block = key_tiles[safe_tiles].astype(jnp.float32)
        value_block = value_tiles[safe_tiles].astype(jnp.float32)
        query_block = query_tiles[tile_index].astype(jnp.float32)
        output_block = output_tiles[tile_index].astype(jnp.float32)
        grad_block = grad_tiles[tile_index].astype(jnp.float32)
        scores = jnp.einsum("ikgd,sjkd->kgisj", query_block, key_block) * softmax_scale
        key_mask = is_live[None, :, None] & (not_self[None, :, None] | causal[:, None, :])
        scores = jnp.where(key_mask, scores, -jnp.inf)
        row_max = jnp.max(scores, axis=(3, 4), keepdims=True)
        log_total = row_max + jnp.log(jnp.sum(jnp.exp(scores - row_max), axis=(3, 4), keepdims=True))
        attn_probs = jnp.exp(scores - log_total)
        probs_low = lax.optimization_barrier(attn_probs.astype(jnp.bfloat16)).astype(jnp.float32)
        grad_probs = jnp.einsum("ikgd,sjkd->kgisj", grad_block, value_block)
        row_delta = jnp.transpose(jnp.sum(grad_block * output_block, axis=-1), (1, 2, 0))[..., None, None]
        grad_scores = lax.optimization_barrier((attn_probs * (grad_probs - row_delta)).astype(jnp.bfloat16)).astype(jnp.float32)
        query_grad = (jnp.einsum("kgisj,sjkd->ikgd", grad_scores, key_block) * softmax_scale).astype(jnp.bfloat16)
        key_part = jnp.einsum("kgisj,ikgd->sjkd", grad_scores, query_block)
        value_part = jnp.einsum("kgisj,ikgd->sjkd", probs_low, grad_block)
        keep_mask = is_live[:, None, None, None]
        key_acc = key_acc.at[safe_tiles].add(jnp.where(keep_mask, key_part, 0.0))
        value_acc = value_acc.at[safe_tiles].add(jnp.where(keep_mask, value_part, 0.0))
        return (key_acc, value_acc), query_grad

    zeros_acc = jnp.zeros((tile_count, TILE, KVH, HD), jnp.float32)
    (key_acc, value_acc), query_grad = lax.scan(scan_step, (zeros_acc, zeros_acc), jnp.arange(tile_count, dtype=jnp.int32))
    token_count = tile_count * TILE
    key_grad = (key_acc * softmax_scale).astype(jnp.bfloat16).reshape(token_count, KVH * HD)
    value_grad = value_acc.astype(jnp.bfloat16).reshape(token_count, KVH * HD)
    return (query_grad.reshape(token_count, QH * HD), key_grad, value_grad)
```

```python
import functools
import math

import jax
import jax.numpy as jnp
from jax import lax
from jax.experimental import pallas as pl
from jax.experimental.pallas import tpu as pltpu
from jax.sharding import PartitionSpec as P

QH = 32
KVH = 4
HD = 128
TILE = 128
GROUP = QH // KVH
LOCAL = KVH // 2
ROWS = GROUP * TILE
PAIR = 2 * TILE
COLS = 2
SCALE = HD ** (-0.5)
LOG2E = 1.0 / math.log(2.0)
MASKED = -1e30
NT_DIMS = (((1,), (1,)), ((), ()))


def delta_kernel(out_ref, grad_ref, delta_ref):
    for head in range(QH):
        cols = slice(head * HD, (head + 1) * HD)
        product = out_ref[:, cols].astype(jnp.float32) * grad_ref[:, cols].astype(jnp.float32)
        delta_ref[head : head + 1, :] = jnp.sum(product.T, axis=0, keepdims=True)


def row_deltas(outputs, out_grad):
    return pl.pallas_call(
        delta_kernel,
        out_shape=jax.ShapeDtypeStruct((QH, TILE), jnp.float32),
        name="row_deltas",
    )(outputs, out_grad)


def backward_kernel(depth, steps, me_ref, anc_ref, q_own, q_peer, g_own, g_peer, d_own, d_peer, *rest):
    arrivals = rest[: 2 * steps]
    dq_own, dq_peer, near_ref, far_ref = rest[2 * steps : 2 * steps + 4]
    (k_all, v_all, q_all, g_all, delta, probs, chunk_max, total, dk_acc, dv_acc, dq_acc) = rest[
        2 * steps + 4 :
    ]
    me = me_ref[0]
    core = me & 1
    chip = me >> 1
    level = chip // COLS
    column = chip % COLS

    for index, arrival in enumerate(arrivals):
        for half in range(2):
            rows = slice(half * TILE, (half + 1) * TILE)
            k_all[2 * index + half] = arrival[rows, :HD]
            v_all[2 * index + half] = arrival[rows, HD:]
    for u, (q_ref, g_ref, d_ref) in enumerate(((q_own, g_own, d_own), (q_peer, g_peer, d_peer))):
        for head in range(GROUP):
            rows = slice(head * TILE, (head + 1) * TILE)
            cols = slice(head * HD, (head + 1) * HD)
            q_all[u, rows, :] = q_ref[:, cols]
            g_all[u, rows, :] = g_ref[:, cols]
            delta[u, :, rows] = d_ref[head : head + 1, :]
    dk_acc[...] = jnp.zeros_like(dk_acc)
    dv_acc[...] = jnp.zeros_like(dv_acc)

    def slot_of(tile):
        other = tile >> 1
        shift = level - other // COLS
        beside = column ^ (other % COLS)
        return (shift * COLS + beside) * 2 + ((tile & 1) ^ core)

    def one_tile(u, carry):
        tile = 2 * chip + (core ^ u)
        live = jnp.int32(1)
        for slot in range(depth):
            live += (anc_ref[tile, slot] >= 0).astype(jnp.int32)
        own_slot = slot_of(tile)
        chunks = (live + 1) // 2

        def slots(chunk):
            if isinstance(chunk, int) and chunk == 0:
                first = own_slot
            else:
                first = slot_of(anc_ref[tile, 2 * chunk - 1])
            good = 2 * chunk + 1 < live
            second = jnp.where(
                good, slot_of(anc_ref[tile, jnp.minimum(2 * chunk, depth - 1)]), own_slot
            )
            return first, second, good

        def scores_chunk(chunk):
            is_first = isinstance(chunk, int) and chunk == 0
            first, second, good = slots(chunk)
            key_block = jnp.concatenate([k_all[first], k_all[second]], axis=0)
            for pair in range(GROUP // 2):
                rows = slice(pair * PAIR, (pair + 1) * PAIR)
                raw = lax.dot_general(
                    key_block, q_all[u, rows, :], NT_DIMS, preferred_element_type=jnp.float32
                ) * (SCALE * LOG2E)
                top, low = raw[:TILE], raw[TILE:]
                if is_first:
                    key_pos = lax.broadcasted_iota(jnp.int32, (TILE, PAIR), 0)
                    query_pos = lax.broadcasted_iota(jnp.int32, (TILE, PAIR), 1) & (TILE - 1)
                    top = jnp.where(key_pos <= query_pos, top, MASKED)
                low = jnp.where(good, low, MASKED)
                block_max = jnp.maximum(
                    jnp.max(top, axis=0, keepdims=True), jnp.max(low, axis=0, keepdims=True)
                )
                if is_first:
                    new_max = block_max
                else:
                    old_max = chunk_max[chunk - 1, :, rows]
                    new_max = jnp.maximum(old_max, block_max)
                top = jnp.exp2(top - new_max)
                low = jnp.exp2(low - new_max)
                block_sum = jnp.sum(top, axis=0, keepdims=True) + jnp.sum(
                    low, axis=0, keepdims=True
                )
                if not is_first:
                    block_sum += total[:, rows] * jnp.exp2(old_max - new_max)
                total[:, rows] = block_sum
                chunk_max[chunk, :, rows] = new_max
                probs[chunk, :TILE, rows] = top
                probs[chunk, TILE:, rows] = low

        scores_chunk(0)

        def scores_loop(chunk, carry):
            scores_chunk(chunk)
            return carry

        lax.fori_loop(1, chunks, scores_loop, 0)
        final_max = chunk_max[chunks - 1]
        inverse = 1.0 / total[...]
        dq_acc[...] = jnp.zeros_like(dq_acc)

        def grads_loop(chunk, carry):
            first = jnp.where(
                chunk == 0, own_slot, slot_of(anc_ref[tile, jnp.maximum(2 * chunk - 1, 0)])
            )
            good = 2 * chunk + 1 < live
            second = jnp.where(
                good, slot_of(anc_ref[tile, jnp.minimum(2 * chunk, depth - 1)]), own_slot
            )
            key_block = jnp.concatenate([k_all[first], k_all[second]], axis=0)
            value_block = jnp.concatenate([v_all[first], v_all[second]], axis=0)
            key_turned = key_block.T
            factor = jnp.exp2(chunk_max[chunk] - final_max) * inverse
            dk = jnp.zeros((PAIR, HD), jnp.float32)
            dv = jnp.zeros((PAIR, HD), jnp.float32)
            for pair in range(GROUP // 2):
                rows = slice(pair * PAIR, (pair + 1) * PAIR)
                query_block = q_all[u, rows, :]
                grad_block = g_all[u, rows, :]
                grad_probs = lax.dot_general(
                    value_block, grad_block, NT_DIMS, preferred_element_type=jnp.float32
                )
                attn = probs[chunk, :, rows] * factor[:, rows]
                attn_low = attn.astype(jnp.bfloat16)
                grad_scores = (attn * (grad_probs - delta[u, :, rows])).astype(jnp.bfloat16)
                dv += jnp.dot(attn_low, grad_block, preferred_element_type=jnp.float32)
                dk += jnp.dot(grad_scores, query_block, preferred_element_type=jnp.float32)
                dq_acc[:, rows] += jnp.dot(
                    key_turned, grad_scores, preferred_element_type=jnp.float32
                )
            dk_acc[first] += dk[:TILE]
            dk_acc[second] += dk[TILE:]
            dv_acc[first] += dv[:TILE]
            dv_acc[second] += dv[TILE:]
            return carry

        lax.fori_loop(0, chunks, grads_loop, 0)

        def put(dq_ref):
            for head in range(GROUP):
                cols = slice(head * TILE, (head + 1) * TILE)
                dq_ref[:, cols] = (dq_acc[:, cols] * SCALE).T.astype(jnp.bfloat16)

        @pl.when(u == 0)
        def _():
            put(dq_own)

        @pl.when(u == 1)
        def _():
            put(dq_peer)

        return carry

    lax.fori_loop(0, 2, one_tile, 0)

    for shift in range(steps):
        for half in range(2):
            rows = slice(half * TILE, (half + 1) * TILE)
            slot = shift * 4 + half
            near_ref[shift, rows, :HD] = dk_acc[slot]
            near_ref[shift, rows, HD:] = dv_acc[slot]
            far_ref[shift, rows, :HD] = dk_acc[slot + 2].astype(jnp.bfloat16)
            far_ref[shift, rows, HD:] = dv_acc[slot + 2].astype(jnp.bfloat16)


def head_backward(local, me, ancestors, q_pair, g_pair, d_pair, arrivals):
    steps = len(arrivals) // 2
    depth = ancestors.shape[1]
    max_chunks = (depth + 2) // 2
    slots = 4 * steps

    def pick(me_ref):
        return (me_ref[0] & 1) * LOCAL + local

    wide = pl.BlockSpec((TILE, ROWS), lambda i, me_ref, anc_ref: (0, pick(me_ref)))
    small = pl.BlockSpec((GROUP, TILE), lambda i, me_ref, anc_ref: (pick(me_ref), 0))
    whole = pl.BlockSpec((PAIR, 2 * HD), lambda i, *_: (0, 0))
    return pl.pallas_call(
        functools.partial(backward_kernel, depth, steps),
        grid_spec=pltpu.PrefetchScalarGridSpec(
            num_scalar_prefetch=2,
            grid=(1,),
            in_specs=[wide] * 4 + [small] * 2 + [whole] * len(arrivals),
            out_specs=[
                pl.BlockSpec((TILE, ROWS), lambda i, *_: (0, 0)),
                pl.BlockSpec((TILE, ROWS), lambda i, *_: (0, 0)),
                pl.BlockSpec((steps, PAIR, 2 * HD), lambda i, *_: (0, 0, 0)),
                pl.BlockSpec((steps, PAIR, 2 * HD), lambda i, *_: (0, 0, 0)),
            ],
            scratch_shapes=[
                pltpu.VMEM((slots, TILE, HD), jnp.bfloat16),
                pltpu.VMEM((slots, TILE, HD), jnp.bfloat16),
                pltpu.VMEM((2, ROWS, HD), jnp.bfloat16),
                pltpu.VMEM((2, ROWS, HD), jnp.bfloat16),
                pltpu.VMEM((2, 1, ROWS), jnp.float32),
                pltpu.VMEM((max_chunks, PAIR, ROWS), jnp.float32),
                pltpu.VMEM((max_chunks, 1, ROWS), jnp.float32),
                pltpu.VMEM((1, ROWS), jnp.float32),
                pltpu.VMEM((slots, TILE, HD), jnp.float32),
                pltpu.VMEM((slots, TILE, HD), jnp.float32),
                pltpu.VMEM((HD, ROWS), jnp.float32),
            ],
        ),
        out_shape=[
            jax.ShapeDtypeStruct((TILE, ROWS), jnp.bfloat16),
            jax.ShapeDtypeStruct((TILE, ROWS), jnp.bfloat16),
            jax.ShapeDtypeStruct((steps, PAIR, 2 * HD), jnp.float32),
            jax.ShapeDtypeStruct((steps, PAIR, 2 * HD), jnp.bfloat16),
        ],
        compiler_params=pltpu.CompilerParams(vmem_limit_bytes=48 * 1024 * 1024),
        name="tree_backward",
    )(me, ancestors, *q_pair, *g_pair, *d_pair, *arrivals)


def per_device(tok_count, queries, keys, values, outputs, out_grad, ancestors):
    steps = tok_count // (2 * COLS)
    width = 2 * COLS
    index = lax.axis_index("tok")
    core = index % 2
    me = index.reshape(1).astype(jnp.int32)

    swap = [(t, t ^ 1) for t in range(tok_count)]

    def to_peer(x):
        return lax.ppermute(x, "tok", swap)

    def up(x, shift):
        return lax.ppermute(
            x, "tok", [(t, t + shift * width) for t in range(tok_count - shift * width)]
        )

    def down(x, shift):
        return lax.ppermute(
            x, "tok", [(t + shift * width, t) for t in range(tok_count - shift * width)]
        )

    def beside(x, lowest, first=0, last=1):
        return lax.ppermute(
            x,
            "tok",
            [
                (t, t ^ 2)
                for t in range(lowest * width, tok_count)
                if first <= (t >> 1) % COLS <= last
            ],
        )

    def columns(x, who, count):
        return lax.dynamic_slice_in_dim(x, who * count, count, 1)

    half_cols = LOCAL * HD
    kv_peer = to_peer(
        jnp.concatenate(
            [columns(keys, 1 - core, half_cols), columns(values, 1 - core, half_cols)], axis=1
        )
    )
    kv_own = jnp.concatenate([columns(keys, core, half_cols), columns(values, core, half_cols)], axis=1)
    q_pair = (queries, to_peer(queries))
    g_pair = (out_grad, to_peer(out_grad))
    deltas = row_deltas(outputs, out_grad)
    d_pair = (deltas, to_peer(deltas))

    gathered = []
    for local in range(LOCAL):
        payload = jnp.concatenate(
            [
                jnp.concatenate(
                    [
                        part[:, local * HD : (local + 1) * HD],
                        part[:, half_cols + local * HD : half_cols + (local + 1) * HD],
                    ],
                    axis=1,
                )
                for part in (kv_own, kv_peer)
            ],
            axis=0,
        )
        arrivals = [payload, beside(payload, 0, 0, 0)]
        for shift in range(1, steps):
            moved = up(payload, shift)
            arrivals += [moved, beside(moved, shift)]
        gathered.append(arrivals)

    dq_own, dq_peer, sums = [], [], []
    for local in range(LOCAL):
        own, peer, near, far = head_backward(
            local, me, ancestors, q_pair, g_pair, d_pair, gathered[local]
        )
        dq_own.append(own)
        dq_peer.append(to_peer(peer))
        acc = near[0] + beside(far[0], 0, 1, 1).astype(jnp.float32)
        for shift in range(steps - 1, 0, -1):
            joint = near[shift] + beside(far[shift], shift).astype(jnp.float32)
            acc += down(joint.astype(jnp.bfloat16), shift).astype(jnp.float32)
        scaled = jnp.concatenate([acc[:, :HD] * SCALE, acc[:, HD:]], axis=1).astype(jnp.bfloat16)
        sums.append((scaled[:TILE], to_peer(scaled[TILE:])))

    def in_order(own, other):
        return jnp.where(
            core == 0,
            jnp.concatenate(own + other, axis=1),
            jnp.concatenate(other + own, axis=1),
        )

    return (
        in_order(dq_own, dq_peer),
        in_order([s[0][:, :HD] for s in sums], [s[1][:, :HD] for s in sums]),
        in_order([s[0][:, HD:] for s in sums], [s[1][:, HD:] for s in sums]),
    )


def solution(mesh):
    return jax.shard_map(
        functools.partial(per_device, mesh.shape["tok"]),
        mesh=mesh,
        in_specs=(
            P(("parts", "tok"), None),
            P(("parts", "tok"), None),
            P(("parts", "tok"), None),
            P(("parts", "tok"), None),
            P(("parts", "tok"), None),
            P("parts", None),
        ),
        out_specs=(P(("parts", "tok"), None), P(("parts", "tok"), None), P(("parts", "tok"), None)),
        check_vma=False,
    )
```

```python
import functools
import math

import jax
import jax.numpy as jnp
from jax import lax
from jax.experimental import pallas as pl
from jax.experimental.pallas import tpu as pltpu
from jax.sharding import Mesh
from jax.sharding import PartitionSpec as P

QH = 32
KVH = 4
HD = 128
TILE = 128
GROUP = QH // KVH
ROWS = GROUP * TILE
PAIR = 2 * TILE
QUAD = 4
LEVEL = QUAD * TILE
SCALE = HD ** (-0.5)
SCALE2 = SCALE / math.log(2.0)
MASKED = -1e30
NT_DIMS = (((1,), (1,)), ((), ()))
PARAMS = pltpu.CompilerParams(vmem_limit_bytes=48 * 1024 * 1024)


def delta_kernel(out_ref, grad_ref, delta_ref):
    for head in range(QH):
        cols = slice(head * HD, (head + 1) * HD)
        product = out_ref[:, cols].astype(jnp.float32) * grad_ref[:, cols].astype(jnp.float32)
        delta_ref[head : head + 1, :] = jnp.sum(product.T, axis=0, keepdims=True)


def row_deltas(outputs, out_grad):
    return pl.pallas_call(
        delta_kernel,
        out_shape=jax.ShapeDtypeStruct((QH, TILE), jnp.float32),
        name="row_deltas",
    )(outputs, out_grad)


def live_counts(anc_ref, me, u, depth):
    tile = me ^ u
    cut = ((me >> 2) - 1) * QUAD
    near, live = jnp.int32(1), jnp.int32(1)
    for slot in range(depth):
        entry = anc_ref[tile, slot]
        live += (entry >= 0).astype(jnp.int32)
        near += ((entry >= 0) & (entry >= cut)).astype(jnp.int32)
    return tile, near, live


def chunk_slots(anc_ref, me, tile, depth, start, stop, lowest):
    def slot_of(entry):
        seen = jnp.where(entry == 0, tile, anc_ref[tile, jnp.clip(entry - 1, 0, depth - 1)])
        return ((me >> 2) - (seen >> 2) - lowest) * QUAD + ((seen ^ me) & (QUAD - 1))

    good = start + 1 < stop
    first = slot_of(start)
    return first, jnp.where(good, slot_of(start + 1), first), good


def slot_rows(slot):
    return pl.ds(pl.multiple_of(slot * TILE, TILE), TILE)


def two_tiles(ref, first, second):
    return jnp.concatenate([ref[slot_rows(first), :], ref[slot_rows(second), :]], axis=0)


def two_heads(ref, u, pair):
    left = ref[u, :, 2 * pair * HD : (2 * pair + 1) * HD]
    right = ref[u, :, (2 * pair + 1) * HD : (2 * pair + 2) * HD]
    return jnp.concatenate([left, right], axis=0)


def causal_mask():
    key_pos = lax.broadcasted_iota(jnp.int32, (TILE, PAIR), 0)
    query_pos = lax.broadcasted_iota(jnp.int32, (TILE, PAIR), 1) & (TILE - 1)
    return key_pos <= query_pos


def gather_queries(scratch, own, peer, side):
    scratch[0] = own[...]
    scratch[1] = peer[...]
    scratch[2] = side[:TILE, :]
    scratch[3] = side[TILE:, :]


def stats_kernel(depth, steps, me_ref, anc_ref, q_own, q_peer, q_side, *rest):
    k_refs = rest[:steps]
    lse_ref, q_all, k_all, top_max, total = rest[steps:]
    me = me_ref[0]
    gather_queries(q_all, q_own, q_peer, q_side)
    for shift, k_ref in enumerate(k_refs):
        k_all[shift * LEVEL : (shift + 1) * LEVEL, :] = k_ref[...]

    def one_tile(u, carry):
        tile, _, live = live_counts(anc_ref, me, u, depth)

        def chunk_stats(index, is_first):
            first, second, good = chunk_slots(anc_ref, me, tile, depth, 2 * index, live, 0)
            key_block = two_tiles(k_all, first, second)
            for pair in range(GROUP // 2):
                rows = slice(pair * PAIR, (pair + 1) * PAIR)
                raw = lax.dot_general(
                    key_block,
                    two_heads(q_all, u, pair),
                    NT_DIMS,
                    preferred_element_type=jnp.float32,
                )
                top, low = raw[:TILE], raw[TILE:]
                if is_first:
                    top = jnp.where(causal_mask(), top, MASKED)
                low_max = jnp.max(low, axis=0, keepdims=True)
                new_max = jnp.maximum(
                    jnp.max(top, axis=0, keepdims=True), jnp.where(good, low_max, MASKED)
                )
                if not is_first:
                    old_max = top_max[:, rows]
                    new_max = jnp.maximum(old_max, new_max)
                low_base = jnp.where(good, new_max, -MASKED)
                new_sum = jnp.sum(
                    jnp.exp2((top - new_max) * SCALE2), axis=0, keepdims=True
                ) + jnp.sum(jnp.exp2((low - low_base) * SCALE2), axis=0, keepdims=True)
                if not is_first:
                    new_sum += total[:, rows] * jnp.exp2((old_max - new_max) * SCALE2)
                top_max[:, rows] = new_max
                total[:, rows] = new_sum

        chunk_stats(0, True)

        def step(index, carry):
            chunk_stats(index, False)
            return carry

        lax.fori_loop(1, (live + 1) // 2, step, 0)
        lse_ref[u] = top_max[...] * SCALE2 + jnp.log2(total[...])
        return carry

    lax.fori_loop(0, QUAD, one_tile, 0)


def grads_kernel(depth, near_part, steps, me_ref, anc_ref, q_own, q_peer, q_side, g_own, g_peer, g_side, d_own, d_peer, d_side, lse_ref, *rest):
    kv_refs = rest[: 2 * steps]
    rest = rest[2 * steps :]
    if near_part:
        dq_in, dq_own, dq_peer, dq_side = rest[:4]
        rest = rest[4:]
    else:
        dq_acc = rest[0]
        rest = rest[1:]
    partial_refs = rest[:steps]
    q_all, g_all, delta, k_all, v_all, dk_acc, dv_acc = rest[steps : steps + 7]
    if near_part:
        dq_acc = rest[steps + 7]
    lowest = 0 if near_part else 2
    me = me_ref[0]
    gather_queries(q_all, q_own, q_peer, q_side)
    gather_queries(g_all, g_own, g_peer, g_side)
    for head in range(GROUP):
        cols = slice(head * TILE, (head + 1) * TILE)
        delta[0, :, cols] = d_own[head : head + 1, :]
        delta[1, :, cols] = d_peer[head : head + 1, :]
        delta[2, :, cols] = d_side[head : head + 1, :]
        delta[3, :, cols] = d_side[GROUP + head : GROUP + head + 1, :]
    for shift in range(steps):
        k_all[shift * LEVEL : (shift + 1) * LEVEL, :] = kv_refs[shift][...]
        v_all[shift * LEVEL : (shift + 1) * LEVEL, :] = kv_refs[steps + shift][...]
    dk_acc[...] = jnp.zeros_like(dk_acc)
    dv_acc[...] = jnp.zeros_like(dv_acc)

    def one_tile(u, carry):
        tile, near, live = live_counts(anc_ref, me, u, depth)
        start, stop = (0, near) if near_part else (near, live)
        if near_part:
            dq_acc[u] = dq_in[u]
        else:
            dq_acc[u] = jnp.zeros((HD, ROWS), jnp.float32)

        def chunk_grads(index, is_first):
            first, second, good = chunk_slots(
                anc_ref, me, tile, depth, start + 2 * index, stop, lowest
            )
            key_block = two_tiles(k_all, first, second)
            value_block = two_tiles(v_all, first, second)
            key_turned = key_block.T
            dk = jnp.zeros((PAIR, HD), jnp.float32)
            dv = jnp.zeros((PAIR, HD), jnp.float32)
            for pair in range(GROUP // 2):
                rows = slice(pair * PAIR, (pair + 1) * PAIR)
                query_block = two_heads(q_all, u, pair)
                grad_block = two_heads(g_all, u, pair)
                raw = lax.dot_general(
                    key_block, query_block, NT_DIMS, preferred_element_type=jnp.float32
                )
                grad_probs = lax.dot_general(
                    value_block, grad_block, NT_DIMS, preferred_element_type=jnp.float32
                )
                lse = lse_ref[u, :, rows]
                away = delta[u, :, rows]
                lows, scores = [], []
                for part in range(2):
                    half = slice(part * TILE, (part + 1) * TILE)
                    base = lse if part == 0 else jnp.where(good, lse, -MASKED)
                    attn = jnp.exp2(raw[half] * SCALE2 - base)
                    if is_first and part == 0:
                        attn = jnp.where(causal_mask(), attn, 0.0)
                    lows.append(attn.astype(jnp.bfloat16))
                    scores.append((attn * (grad_probs[half] - away)).astype(jnp.bfloat16))
                attn_low = jnp.concatenate(lows, axis=0)
                grad_scores = jnp.concatenate(scores, axis=0)
                dv += jnp.dot(attn_low, grad_block, preferred_element_type=jnp.float32)
                dk += jnp.dot(grad_scores, query_block, preferred_element_type=jnp.float32)
                dq_acc[u, :, rows] += jnp.dot(
                    key_turned, grad_scores, preferred_element_type=jnp.float32
                )
            dk_acc[slot_rows(first), :] += dk[:TILE]
            dk_acc[slot_rows(second), :] += dk[TILE:]
            dv_acc[slot_rows(first), :] += dv[:TILE]
            dv_acc[slot_rows(second), :] += dv[TILE:]

        def step(index, carry):
            chunk_grads(index, False)
            return carry

        if near_part:
            chunk_grads(0, True)
        lax.fori_loop(1 if near_part else 0, (stop - start + 1) // 2, step, 0)
        return carry

    lax.fori_loop(0, QUAD, one_tile, 0)

    if near_part:
        for u in range(QUAD):
            for head in range(GROUP):
                cols = slice(head * HD, (head + 1) * HD)
                turned = (dq_acc[u, :, cols] * SCALE).T.astype(jnp.bfloat16)
                if u == 0:
                    dq_own[:, cols] = turned
                elif u == 1:
                    dq_peer[:, cols] = turned
                else:
                    dq_side[(u - 2) * TILE : (u - 1) * TILE, cols] = turned
    for shift, out_ref in enumerate(partial_refs):
        rows = slice(shift * LEVEL, (shift + 1) * LEVEL)
        out_ref[:, :HD] = dk_acc[rows, :].astype(out_ref.dtype)
        out_ref[:, HD:] = dv_acc[rows, :].astype(out_ref.dtype)


def fixed(shape):
    return pl.BlockSpec(shape, lambda i, *_: (0,) * len(shape))


def own_head(me_ref):
    return ((me_ref[0] & 1) << 1) | ((me_ref[0] >> 1) & 1)


WIDE = pl.BlockSpec((TILE, ROWS), lambda i, me_ref, anc_ref: (0, own_head(me_ref)))
SMALL = pl.BlockSpec((GROUP, TILE), lambda i, me_ref, anc_ref: (own_head(me_ref), 0))
SIDE = fixed((PAIR, ROWS))
LSE = fixed((QUAD, 1, ROWS))
KEYS = fixed((LEVEL, HD))
SUMS = fixed((LEVEL, 2 * HD))
DQ = fixed((QUAD, HD, ROWS))


def statistics(me, ancestors, q_set, k_list):
    steps = len(k_list)
    return pl.pallas_call(
        functools.partial(stats_kernel, ancestors.shape[1], steps),
        grid_spec=pltpu.PrefetchScalarGridSpec(
            num_scalar_prefetch=2,
            grid=(1,),
            in_specs=[WIDE, WIDE, SIDE] + [KEYS] * steps,
            out_specs=LSE,
            scratch_shapes=[
                pltpu.VMEM((QUAD, TILE, ROWS), jnp.bfloat16),
                pltpu.VMEM((steps * LEVEL, HD), jnp.bfloat16),
                pltpu.VMEM((1, ROWS), jnp.float32),
                pltpu.VMEM((1, ROWS), jnp.float32),
            ],
        ),
        out_shape=jax.ShapeDtypeStruct((QUAD, 1, ROWS), jnp.float32),
        compiler_params=PARAMS,
        name="statistics",
    )(me, ancestors, *q_set, *k_list)


def gradients(me, ancestors, q_set, g_set, d_set, lse, k_list, v_list, dq_far=None):
    steps = len(k_list)
    near_part = dq_far is not None
    if near_part:
        dq_specs = [WIDE_OUT, WIDE_OUT, SIDE]
        dq_shapes = [
            jax.ShapeDtypeStruct((TILE, ROWS), jnp.bfloat16),
            jax.ShapeDtypeStruct((TILE, ROWS), jnp.bfloat16),
            jax.ShapeDtypeStruct((PAIR, ROWS), jnp.bfloat16),
        ]
        kinds = [jnp.float32] + [jnp.bfloat16] * (steps - 1)
    else:
        dq_specs = [DQ]
        dq_shapes = [jax.ShapeDtypeStruct((QUAD, HD, ROWS), jnp.float32)]
        kinds = [jnp.bfloat16] * steps
    scratch = [
        pltpu.VMEM((QUAD, TILE, ROWS), jnp.bfloat16),
        pltpu.VMEM((QUAD, TILE, ROWS), jnp.bfloat16),
        pltpu.VMEM((QUAD, 1, ROWS), jnp.float32),
        pltpu.VMEM((steps * LEVEL, HD), jnp.bfloat16),
        pltpu.VMEM((steps * LEVEL, HD), jnp.bfloat16),
        pltpu.VMEM((steps * LEVEL, HD), jnp.float32),
        pltpu.VMEM((steps * LEVEL, HD), jnp.float32),
    ]
    if near_part:
        scratch.append(pltpu.VMEM((QUAD, HD, ROWS), jnp.float32))
    return pl.pallas_call(
        functools.partial(grads_kernel, ancestors.shape[1], near_part, steps),
        grid_spec=pltpu.PrefetchScalarGridSpec(
            num_scalar_prefetch=2,
            grid=(1,),
            in_specs=[WIDE, WIDE, SIDE, WIDE, WIDE, SIDE, SMALL, SMALL, fixed((2 * GROUP, TILE)), LSE]
            + [KEYS] * (2 * steps)
            + ([DQ] if near_part else []),
            out_specs=dq_specs + [SUMS] * steps,
            scratch_shapes=scratch,
        ),
        out_shape=dq_shapes + [jax.ShapeDtypeStruct((LEVEL, 2 * HD), kind) for kind in kinds],
        compiler_params=PARAMS,
        name="near_grads" if near_part else "far_grads",
    )(
        me,
        ancestors,
        *q_set,
        *g_set,
        *d_set,
        lse,
        *k_list,
        *v_list,
        *([dq_far] if near_part else []),
    )


WIDE_OUT = fixed((TILE, ROWS))


def per_device(steps, queries, keys, values, outputs, out_grad, ancestors):
    level, side, core = (lax.axis_index(name) for name in ("level", "side", "core"))
    me = (QUAD * level + 2 * side + core).reshape(1).astype(jnp.int32)

    def to_peer(x):
        return lax.ppermute(x, "core", [(0, 1), (1, 0)])

    def to_side(x):
        return lax.ppermute(x, "side", [(0, 1), (1, 0)])

    def up(x, shift):
        return lax.ppermute(x, "level", [(z, z + shift) for z in range(steps - shift)])

    def down(x, shift):
        return lax.ppermute(x, "level", [(z + shift, z) for z in range(steps - shift)])

    def columns(x, who, count):
        return lax.dynamic_slice_in_dim(x, who * count, count, 1)

    def head_rows(x, who):
        return lax.dynamic_slice_in_dim(x, who * GROUP, GROUP, 0)

    side_head = 2 * core + 1 - side
    half = 2 * HD
    kv_peer = to_peer(
        jnp.concatenate([columns(keys, 1 - core, half), columns(values, 1 - core, half)], axis=1)
    )
    q_peer = to_peer(queries)
    g_peer = to_peer(out_grad)
    k_chip = jnp.concatenate([columns(keys, core, half), kv_peer[:, :half]], axis=0)
    v_chip = jnp.concatenate([columns(values, core, half), kv_peer[:, half:]], axis=0)
    kv_side = to_side(
        jnp.concatenate([columns(k_chip, 1 - side, HD), columns(v_chip, 1 - side, HD)], axis=1)
    )
    k_level = jnp.concatenate([columns(k_chip, side, HD), kv_side[:, :HD]], axis=0)
    v_level = jnp.concatenate([columns(v_chip, side, HD), kv_side[:, HD:]], axis=0)
    k_list = [k_level] + [up(k_level, shift) for shift in range(1, steps)]

    def both(own, peer):
        return jnp.concatenate([columns(own, side_head, ROWS), columns(peer, side_head, ROWS)], axis=0)

    q_set = (queries, q_peer, to_side(both(queries, q_peer)))
    v_list = [v_level] + [up(v_level, shift) for shift in range(1, steps)]
    g_set = (out_grad, g_peer, to_side(both(out_grad, g_peer)))
    deltas = row_deltas(outputs, out_grad)
    d_peer = to_peer(deltas)
    d_side = to_side(
        jnp.concatenate([head_rows(deltas, side_head), head_rows(d_peer, side_head)], axis=0)
    )
    d_set = (deltas, d_peer, d_side)

    lse = statistics(me, ancestors, q_set, k_list)
    dq_far, *far = gradients(me, ancestors, q_set, g_set, d_set, lse, k_list[2:], v_list[2:])
    back = [down(far[shift - 2], shift) for shift in range(2, steps)]
    dq_own, dq_peer, dq_side, total, near = gradients(
        me, ancestors, q_set, g_set, d_set, lse, k_list[:2], v_list[:2], dq_far
    )
    back.append(down(near, 1))
    dq_side = to_side(dq_side)
    dq_diag = to_peer(dq_side[TILE:])
    dq_peer = to_peer(dq_peer)

    for part in back:
        total += part.astype(jnp.float32)
    scaled = jnp.concatenate([total[:, :HD] * SCALE, total[:, HD:]], axis=1).astype(jnp.bfloat16)
    kv_side = to_side(scaled[PAIR:])
    kv_peer = to_peer(jnp.concatenate([scaled[TILE:PAIR], kv_side[TILE:]], axis=1))

    def in_order(own, beside, peer, diagonal):
        here = jnp.where(
            side == 0,
            jnp.concatenate([own, beside], axis=1),
            jnp.concatenate([beside, own], axis=1),
        )
        there = jnp.where(
            side == 0,
            jnp.concatenate([peer, diagonal], axis=1),
            jnp.concatenate([diagonal, peer], axis=1),
        )
        return jnp.where(
            core == 0,
            jnp.concatenate([here, there], axis=1),
            jnp.concatenate([there, here], axis=1),
        )

    return (
        in_order(dq_own, dq_side[:TILE], dq_peer, dq_diag),
        in_order(scaled[:TILE, :HD], kv_side[:TILE, :HD], kv_peer[:, :HD], kv_peer[:, half : half + HD]),
        in_order(scaled[:TILE, HD:], kv_side[:TILE, HD:], kv_peer[:, HD:half], kv_peer[:, half + HD :]),
    )


def solution(mesh):
    parts, tok = mesh.shape["parts"], mesh.shape["tok"]
    quads = Mesh(
        mesh.devices.reshape(parts, tok // QUAD, 2, 2), ("parts", "level", "side", "core")
    )
    rows = P(("parts", "level", "side", "core"), None)
    return jax.shard_map(
        functools.partial(per_device, tok // QUAD),
        mesh=quads,
        in_specs=(rows, rows, rows, rows, rows, P("parts", None)),
        out_specs=(rows, rows, rows),
        check_vma=False,
    )
```

```python
import functools
import math

import jax
import jax.numpy as jnp
from jax import lax
from jax.experimental import pallas as pl
from jax.experimental.pallas import tpu as pltpu
from jax.sharding import Mesh
from jax.sharding import PartitionSpec as P

QH = 32
KVH = 4
HD = 128
TILE = 128
GROUP = QH // KVH
ROWS = GROUP * TILE
PAIR = 2 * TILE
QUAD = 4
LEVEL = QUAD * TILE
SCALE = HD ** (-0.5)
SCALE2 = SCALE / math.log(2.0)
MASKED = -1e30
NT_DIMS = (((1,), (1,)), ((), ()))
PARAMS = pltpu.CompilerParams(vmem_limit_bytes=28 * 1024 * 1024)


def delta_kernel(out_ref, grad_ref, delta_ref):
    for head in range(QH):
        cols = slice(head * HD, (head + 1) * HD)
        product = out_ref[:, cols].astype(jnp.float32) * grad_ref[:, cols].astype(jnp.float32)
        delta_ref[head : head + 1, :] = jnp.sum(product.T, axis=0, keepdims=True)


def row_deltas(outputs, out_grad):
    return pl.pallas_call(
        delta_kernel,
        out_shape=jax.ShapeDtypeStruct((QH, TILE), jnp.float32),
        name="row_deltas",
    )(outputs, out_grad)


def live_counts(anc_ref, me, u, depth):
    tile = me ^ u
    cut = ((me >> 2) - 1) * QUAD
    near, live = jnp.int32(1), jnp.int32(1)
    for slot in range(depth):
        entry = anc_ref[tile, slot]
        live += (entry >= 0).astype(jnp.int32)
        near += ((entry >= 0) & (entry >= cut)).astype(jnp.int32)
    return tile, near, live


def chunk_slots(anc_ref, me, tile, depth, start, stop, lowest):
    def slot_of(entry):
        seen = jnp.where(entry == 0, tile, anc_ref[tile, jnp.clip(entry - 1, 0, depth - 1)])
        return ((me >> 2) - (seen >> 2) - lowest) * QUAD + ((seen ^ me) & (QUAD - 1))

    good = start + 1 < stop
    first = slot_of(start)
    return first, jnp.where(good, slot_of(start + 1), first), good


def slot_rows(slot):
    return pl.ds(pl.multiple_of(slot * TILE, TILE), TILE)


def two_tiles(ref, first, second):
    return jnp.concatenate([ref[slot_rows(first), :], ref[slot_rows(second), :]], axis=0)


def two_heads(ref, u, pair):
    left = ref[u, :, 2 * pair * HD : (2 * pair + 1) * HD]
    right = ref[u, :, (2 * pair + 1) * HD : (2 * pair + 2) * HD]
    return jnp.concatenate([left, right], axis=0)


def causal_mask():
    key_pos = lax.broadcasted_iota(jnp.int32, (TILE, PAIR), 0)
    query_pos = lax.broadcasted_iota(jnp.int32, (TILE, PAIR), 1) & (TILE - 1)
    return key_pos <= query_pos


def gather_queries(scratch, own, peer, side):
    scratch[0] = own[...]
    scratch[1] = peer[...]
    scratch[2] = side[:TILE, :]
    scratch[3] = side[TILE:, :]


def stats_kernel(depth, steps, me_ref, anc_ref, q_own, q_peer, q_side, *rest):
    k_refs = rest[:steps]
    lse_ref, q_all, k_all, top_max, total = rest[steps:]
    me = me_ref[0]
    gather_queries(q_all, q_own, q_peer, q_side)
    for shift, k_ref in enumerate(k_refs):
        k_all[shift * LEVEL : (shift + 1) * LEVEL, :] = k_ref[...]

    def one_tile(u, carry):
        tile, _, live = live_counts(anc_ref, me, u, depth)

        def chunk_stats(index, is_first):
            first, second, good = chunk_slots(anc_ref, me, tile, depth, 2 * index, live, 0)
            key_block = two_tiles(k_all, first, second)
            for pair in range(GROUP // 2):
                rows = slice(pair * PAIR, (pair + 1) * PAIR)
                raw = lax.dot_general(
                    key_block,
                    two_heads(q_all, u, pair),
                    NT_DIMS,
                    preferred_element_type=jnp.float32,
                )
                top, low = raw[:TILE], raw[TILE:]
                if is_first:
                    top = jnp.where(causal_mask(), top, MASKED)
                low_max = jnp.max(low, axis=0, keepdims=True)
                new_max = jnp.maximum(
                    jnp.max(top, axis=0, keepdims=True), jnp.where(good, low_max, MASKED)
                )
                if not is_first:
                    old_max = top_max[:, rows]
                    new_max = jnp.maximum(old_max, new_max)
                low_base = jnp.where(good, new_max, -MASKED)
                new_sum = jnp.sum(
                    jnp.exp2((top - new_max) * SCALE2), axis=0, keepdims=True
                ) + jnp.sum(jnp.exp2((low - low_base) * SCALE2), axis=0, keepdims=True)
                if not is_first:
                    new_sum += total[:, rows] * jnp.exp2((old_max - new_max) * SCALE2)
                top_max[:, rows] = new_max
                total[:, rows] = new_sum

        chunk_stats(0, True)

        def step(index, carry):
            chunk_stats(index, False)
            return carry

        lax.fori_loop(1, (live + 1) // 2, step, 0)
        lse_ref[u] = top_max[...] * SCALE2 + jnp.log2(total[...])
        return carry

    lax.fori_loop(0, QUAD, one_tile, 0)


def grads_kernel(depth, near_part, steps, me_ref, anc_ref, q_own, q_peer, q_side, g_own, g_peer, g_side, d_own, d_peer, d_side, lse_ref, *rest):
    kv_refs = rest[: 2 * steps]
    rest = rest[2 * steps :]
    if near_part:
        dq_in, dq_own, dq_peer, dq_side = rest[:4]
        rest = rest[4:]
    else:
        dq_acc = rest[0]
        rest = rest[1:]
    partial_refs = rest[:steps]
    q_all, g_all, delta, k_all, v_all, dk_acc, dv_acc = rest[steps : steps + 7]
    if near_part:
        dq_acc = rest[steps + 7]
    lowest = 0 if near_part else 2
    me = me_ref[0]
    gather_queries(q_all, q_own, q_peer, q_side)
    gather_queries(g_all, g_own, g_peer, g_side)
    for head in range(GROUP):
        cols = slice(head * TILE, (head + 1) * TILE)
        delta[0, :, cols] = d_own[head : head + 1, :]
        delta[1, :, cols] = d_peer[head : head + 1, :]
        delta[2, :, cols] = d_side[head : head + 1, :]
        delta[3, :, cols] = d_side[GROUP + head : GROUP + head + 1, :]
    for shift in range(steps):
        k_all[shift * LEVEL : (shift + 1) * LEVEL, :] = kv_refs[shift][...]
        v_all[shift * LEVEL : (shift + 1) * LEVEL, :] = kv_refs[steps + shift][...]
    dk_acc[...] = jnp.zeros_like(dk_acc)
    dv_acc[...] = jnp.zeros_like(dv_acc)

    def one_tile(u, carry):
        tile, near, live = live_counts(anc_ref, me, u, depth)
        start, stop = (0, near) if near_part else (near, live)
        if near_part:
            dq_acc[u] = dq_in[u]
        else:
            dq_acc[u] = jnp.zeros((HD, ROWS), jnp.float32)

        def chunk_grads(index, is_first):
            first, second, good = chunk_slots(
                anc_ref, me, tile, depth, start + 2 * index, stop, lowest
            )
            key_block = two_tiles(k_all, first, second)
            value_block = two_tiles(v_all, first, second)
            key_turned = key_block.T
            dk = jnp.zeros((PAIR, HD), jnp.float32)
            dv = jnp.zeros((PAIR, HD), jnp.float32)
            for pair in range(GROUP // 2):
                rows = slice(pair * PAIR, (pair + 1) * PAIR)
                query_block = two_heads(q_all, u, pair)
                grad_block = two_heads(g_all, u, pair)
                raw = lax.dot_general(
                    key_block, query_block, NT_DIMS, preferred_element_type=jnp.float32
                )
                grad_probs = lax.dot_general(
                    value_block, grad_block, NT_DIMS, preferred_element_type=jnp.float32
                )
                lse = lse_ref[u, :, rows]
                away = delta[u, :, rows]
                lows, scores = [], []
                for part in range(2):
                    half = slice(part * TILE, (part + 1) * TILE)
                    base = lse if part == 0 else jnp.where(good, lse, -MASKED)
                    attn = jnp.exp2(raw[half] * SCALE2 - base)
                    if is_first and part == 0:
                        attn = jnp.where(causal_mask(), attn, 0.0)
                    lows.append(attn.astype(jnp.bfloat16))
                    scores.append((attn * (grad_probs[half] - away)).astype(jnp.bfloat16))
                attn_low = jnp.concatenate(lows, axis=0)
                grad_scores = jnp.concatenate(scores, axis=0)
                dv += jnp.dot(attn_low, grad_block, preferred_element_type=jnp.float32)
                dk += jnp.dot(grad_scores, query_block, preferred_element_type=jnp.float32)
                dq_acc[u, :, rows] += jnp.dot(
                    key_turned, grad_scores, preferred_element_type=jnp.float32
                )
            dk_acc[slot_rows(first), :] += dk[:TILE]
            dk_acc[slot_rows(second), :] += dk[TILE:]
            dv_acc[slot_rows(first), :] += dv[:TILE]
            dv_acc[slot_rows(second), :] += dv[TILE:]

        def step(index, carry):
            chunk_grads(index, False)
            return carry

        if near_part:
            chunk_grads(0, True)
        lax.fori_loop(1 if near_part else 0, (stop - start + 1) // 2, step, 0)
        return carry

    lax.fori_loop(0, QUAD, one_tile, 0)

    if near_part:
        for u in range(QUAD):
            for head in range(GROUP):
                cols = slice(head * HD, (head + 1) * HD)
                turned = (dq_acc[u, :, cols] * SCALE).T.astype(jnp.bfloat16)
                if u == 0:
                    dq_own[:, cols] = turned
                elif u == 1:
                    dq_peer[:, cols] = turned
                else:
                    dq_side[(u - 2) * TILE : (u - 1) * TILE, cols] = turned
    for shift, out_ref in enumerate(partial_refs):
        rows = slice(shift * LEVEL, (shift + 1) * LEVEL)
        out_ref[:, :HD] = dk_acc[rows, :].astype(out_ref.dtype)
        out_ref[:, HD:] = dv_acc[rows, :].astype(out_ref.dtype)


def work(ancestors, products):
    pairs = QUAD * (ancestors.shape[1] + 1)
    return pl.CostEstimate(
        flops=2 * products * pairs * GROUP * TILE * TILE * 2 * HD,
        transcendentals=pairs * GROUP * TILE * TILE,
        bytes_accessed=16 * 1024 * 1024,
    )


def fixed(shape):
    return pl.BlockSpec(shape, lambda i, *_: (0,) * len(shape))


def own_head(me_ref):
    return ((me_ref[0] & 1) << 1) | ((me_ref[0] >> 1) & 1)


WIDE = pl.BlockSpec((TILE, ROWS), lambda i, me_ref, anc_ref: (0, own_head(me_ref)))
SMALL = pl.BlockSpec((GROUP, TILE), lambda i, me_ref, anc_ref: (own_head(me_ref), 0))
SIDE = fixed((PAIR, ROWS))
LSE = fixed((QUAD, 1, ROWS))
KEYS = fixed((LEVEL, HD))
SUMS = fixed((LEVEL, 2 * HD))
DQ = fixed((QUAD, HD, ROWS))


def statistics(me, ancestors, q_set, k_list):
    steps = len(k_list)
    return pl.pallas_call(
        functools.partial(stats_kernel, ancestors.shape[1], steps),
        grid_spec=pltpu.PrefetchScalarGridSpec(
            num_scalar_prefetch=2,
            grid=(1,),
            in_specs=[WIDE, WIDE, SIDE] + [KEYS] * steps,
            out_specs=LSE,
            scratch_shapes=[
                pltpu.VMEM((QUAD, TILE, ROWS), jnp.bfloat16),
                pltpu.VMEM((steps * LEVEL, HD), jnp.bfloat16),
                pltpu.VMEM((1, ROWS), jnp.float32),
                pltpu.VMEM((1, ROWS), jnp.float32),
            ],
        ),
        out_shape=jax.ShapeDtypeStruct((QUAD, 1, ROWS), jnp.float32),
        compiler_params=PARAMS,
        cost_estimate=work(ancestors, 1),
        name="statistics",
    )(me, ancestors, *q_set, *k_list)


def gradients(me, ancestors, q_set, g_set, d_set, lse, k_list, v_list, dq_far=None):
    steps = len(k_list)
    near_part = dq_far is not None
    if near_part:
        dq_specs = [WIDE_OUT, WIDE_OUT, SIDE]
        dq_shapes = [
            jax.ShapeDtypeStruct((TILE, ROWS), jnp.bfloat16),
            jax.ShapeDtypeStruct((TILE, ROWS), jnp.bfloat16),
            jax.ShapeDtypeStruct((PAIR, ROWS), jnp.bfloat16),
        ]
        kinds = [jnp.float32] + [jnp.bfloat16] * (steps - 1)
    else:
        dq_specs = [DQ]
        dq_shapes = [jax.ShapeDtypeStruct((QUAD, HD, ROWS), jnp.float32)]
        kinds = [jnp.bfloat16] * steps
    scratch = [
        pltpu.VMEM((QUAD, TILE, ROWS), jnp.bfloat16),
        pltpu.VMEM((QUAD, TILE, ROWS), jnp.bfloat16),
        pltpu.VMEM((QUAD, 1, ROWS), jnp.float32),
        pltpu.VMEM((steps * LEVEL, HD), jnp.bfloat16),
        pltpu.VMEM((steps * LEVEL, HD), jnp.bfloat16),
        pltpu.VMEM((steps * LEVEL, HD), jnp.float32),
        pltpu.VMEM((steps * LEVEL, HD), jnp.float32),
    ]
    if near_part:
        scratch.append(pltpu.VMEM((QUAD, HD, ROWS), jnp.float32))
    return pl.pallas_call(
        functools.partial(grads_kernel, ancestors.shape[1], near_part, steps),
        grid_spec=pltpu.PrefetchScalarGridSpec(
            num_scalar_prefetch=2,
            grid=(1,),
            in_specs=[WIDE, WIDE, SIDE, WIDE, WIDE, SIDE, SMALL, SMALL, fixed((2 * GROUP, TILE)), LSE]
            + [KEYS] * (2 * steps)
            + ([DQ] if near_part else []),
            out_specs=dq_specs + [SUMS] * steps,
            scratch_shapes=scratch,
        ),
        out_shape=dq_shapes + [jax.ShapeDtypeStruct((LEVEL, 2 * HD), kind) for kind in kinds],
        compiler_params=PARAMS,
        cost_estimate=work(ancestors, 5),
        name="near_grads" if near_part else "far_grads",
    )(
        me,
        ancestors,
        *q_set,
        *g_set,
        *d_set,
        lse,
        *k_list,
        *v_list,
        *([dq_far] if near_part else []),
    )


WIDE_OUT = fixed((TILE, ROWS))


def pack_keys_kernel(me_ref, k_own, v_own, k_peer, v_peer, k_away, v_away, k_far, v_far, mine_ref, send_ref):
    mine_ref[:TILE, :HD] = k_own[...]
    mine_ref[:TILE, HD:] = v_own[...]
    mine_ref[TILE:, :HD] = k_peer[...]
    mine_ref[TILE:, HD:] = v_peer[...]
    send_ref[:TILE, :HD] = k_away[...]
    send_ref[:TILE, HD:] = v_away[...]
    send_ref[TILE:, :HD] = k_far[...]
    send_ref[TILE:, HD:] = v_far[...]


def side_head(me_ref):
    return own_head(me_ref) ^ 1


def pack_keys(me, keys, values, k_peer, v_peer):
    mine = pl.BlockSpec((TILE, HD), lambda i, me_ref: (0, own_head(me_ref)))
    away = pl.BlockSpec((TILE, HD), lambda i, me_ref: (0, side_head(me_ref)))
    return pl.pallas_call(
        pack_keys_kernel,
        grid_spec=pltpu.PrefetchScalarGridSpec(
            num_scalar_prefetch=1,
            grid=(1,),
            in_specs=[mine] * 4 + [away] * 4,
            out_specs=[fixed((PAIR, 2 * HD))] * 2,
        ),
        out_shape=[jax.ShapeDtypeStruct((PAIR, 2 * HD), jnp.bfloat16)] * 2,
        name="pack_keys",
    )(me, keys, values, k_peer, v_peer, keys, values, k_peer, v_peer)


def pack_queries_kernel(me_ref, q_own, q_peer, g_own, g_peer, q_ref, g_ref):
    q_ref[:TILE, :] = q_own[...]
    q_ref[TILE:, :] = q_peer[...]
    g_ref[:TILE, :] = g_own[...]
    g_ref[TILE:, :] = g_peer[...]


def pack_queries(me, queries, q_peer, out_grad, g_peer):
    away = pl.BlockSpec((TILE, ROWS), lambda i, me_ref: (0, side_head(me_ref)))
    return pl.pallas_call(
        pack_queries_kernel,
        grid_spec=pltpu.PrefetchScalarGridSpec(
            num_scalar_prefetch=1,
            grid=(1,),
            in_specs=[away] * 4,
            out_specs=[SIDE] * 2,
        ),
        out_shape=[jax.ShapeDtypeStruct((PAIR, ROWS), jnp.bfloat16)] * 2,
        name="pack_queries",
    )(me, queries, q_peer, out_grad, g_peer)


def pack_deltas_kernel(me_ref, d_own, d_peer, send_ref):
    send_ref[:GROUP, :] = d_own[...]
    send_ref[GROUP:, :] = d_peer[...]


def pack_deltas(me, deltas, d_peer):
    away = pl.BlockSpec((GROUP, TILE), lambda i, me_ref: (side_head(me_ref), 0))
    return pl.pallas_call(
        pack_deltas_kernel,
        grid_spec=pltpu.PrefetchScalarGridSpec(
            num_scalar_prefetch=1,
            grid=(1,),
            in_specs=[away] * 2,
            out_specs=fixed((2 * GROUP, TILE)),
        ),
        out_shape=jax.ShapeDtypeStruct((2 * GROUP, TILE), jnp.float32),
        name="pack_deltas",
    )(me, deltas, d_peer)


def add_sums_kernel(count, *refs):
    total_ref, parts = refs[0], refs[1 : 1 + count]
    own_ref, peer_ref, send_ref = refs[-3:]
    total = total_ref[...]
    for part in parts:
        total += part[...].astype(jnp.float32)
    scaled = jnp.concatenate([total[:, :HD] * SCALE, total[:, HD:]], axis=1).astype(jnp.bfloat16)
    own_ref[...] = scaled[:TILE]
    peer_ref[...] = scaled[TILE:PAIR]
    send_ref[...] = scaled[PAIR:]


def add_sums(total, parts, first_needed):
    here = pl.BlockSpec(memory_space=pltpu.VMEM)
    return pl.pallas_call(
        functools.partial(add_sums_kernel, len(parts)),
        in_specs=[here] * (1 + len(parts)) + [pl.BlockSpec(memory_space=pl.ANY)],
        out_specs=[here] * 3,
        out_shape=[
            jax.ShapeDtypeStruct((TILE, 2 * HD), jnp.bfloat16),
            jax.ShapeDtypeStruct((TILE, 2 * HD), jnp.bfloat16),
            jax.ShapeDtypeStruct((PAIR, 2 * HD), jnp.bfloat16),
        ],
        name="add_sums",
    )(total, *parts, first_needed)


def placed(me_ref, width):
    head = own_head(me_ref)
    return [pl.ds(pl.multiple_of((head ^ flip) * width, width), width) for flip in range(4)]


def place_queries_kernel(me_ref, own, side, peer, far, dq_ref):
    at = placed(me_ref, ROWS)
    dq_ref[:, at[0]] = own[...]
    dq_ref[:, at[1]] = side[:TILE, :]
    dq_ref[:, at[2]] = peer[...]
    dq_ref[:, at[3]] = far[...]


def place_queries(me, own, side, peer, far):
    return pl.pallas_call(
        place_queries_kernel,
        grid_spec=pltpu.PrefetchScalarGridSpec(
            num_scalar_prefetch=1,
            grid=(1,),
            in_specs=[WIDE_OUT, SIDE, WIDE_OUT, WIDE_OUT],
            out_specs=fixed((TILE, QH * HD)),
        ),
        out_shape=jax.ShapeDtypeStruct((TILE, QH * HD), jnp.bfloat16),
        name="place_queries",
    )(me, own, side, peer, far)


def place_keys_kernel(me_ref, own, side, peer, far, dk_ref, dv_ref):
    at = placed(me_ref, HD)
    for spot, part in zip(at, (own[...], side[:TILE, :], peer[...], far[...])):
        dk_ref[:, spot] = part[:, :HD]
        dv_ref[:, spot] = part[:, HD:]


def place_keys(me, own, side, peer, far):
    piece = fixed((TILE, 2 * HD))
    return pl.pallas_call(
        place_keys_kernel,
        grid_spec=pltpu.PrefetchScalarGridSpec(
            num_scalar_prefetch=1,
            grid=(1,),
            in_specs=[piece, fixed((PAIR, 2 * HD)), piece, piece],
            out_specs=[fixed((TILE, KVH * HD))] * 2,
        ),
        out_shape=[jax.ShapeDtypeStruct((TILE, KVH * HD), jnp.bfloat16)] * 2,
        name="place_keys",
    )(me, own, side, peer, far)


def per_device(steps, queries, keys, values, outputs, out_grad, ancestors):
    level, side, core = (lax.axis_index(name) for name in ("level", "side", "core"))
    me = (QUAD * level + 2 * side + core).reshape(1).astype(jnp.int32)

    def to_peer(x):
        return lax.ppermute(x, "core", [(0, 1), (1, 0)])

    def to_side(x):
        return lax.ppermute(x, "side", [(0, 1), (1, 0)])

    def up(x, shift):
        return lax.ppermute(x, "level", [(z, z + shift) for z in range(steps - shift)])

    def down(x, shift):
        return lax.ppermute(x, "level", [(z + shift, z) for z in range(steps - shift)])

    kv_chip, kv_send = pack_keys(me, keys, values, to_peer(keys), to_peer(values))
    kv_side = to_side(kv_send)
    k_level = jnp.concatenate([kv_chip[:, :HD], kv_side[:, :HD]], axis=0)
    v_level = jnp.concatenate([kv_chip[:, HD:], kv_side[:, HD:]], axis=0)
    k_list = [k_level] + [up(k_level, shift) for shift in range(1, steps)]
    q_peer, g_peer = to_peer(queries), to_peer(out_grad)
    q_send, g_send = pack_queries(me, queries, q_peer, out_grad, g_peer)
    q_set = (queries, q_peer, to_side(q_send))
    v_list = [v_level] + [up(v_level, shift) for shift in range(1, steps)]
    g_set = (out_grad, g_peer, to_side(g_send))
    deltas = row_deltas(outputs, out_grad)
    d_peer = to_peer(deltas)
    d_set = (deltas, d_peer, to_side(pack_deltas(me, deltas, d_peer)))

    lse = statistics(me, ancestors, q_set, k_list)
    dq_far, *far = gradients(me, ancestors, q_set, g_set, d_set, lse, k_list[2:], v_list[2:])
    back = [down(far[shift - 2], shift) for shift in range(2, steps)]
    dq_own, dq_peer, dq_side, total, near = gradients(
        me, ancestors, q_set, g_set, d_set, lse, k_list[:2], v_list[:2], dq_far
    )
    dq_side = to_side(dq_side)
    back.append(down(near, 1))
    dq_peer = to_peer(dq_peer)

    sum_own, sum_peer, sum_side = add_sums(total, back, dq_side)
    dq_far = to_peer(dq_side[TILE:])
    sum_peer = to_peer(sum_peer)
    sum_side = to_side(sum_side)
    sum_far = to_peer(sum_side[TILE:])
    return (
        place_queries(me, dq_own, dq_side, dq_peer, dq_far),
        *place_keys(me, sum_own, sum_side, sum_peer, sum_far),
    )


def solution(mesh):
    parts, tok = mesh.shape["parts"], mesh.shape["tok"]
    quads = Mesh(
        mesh.devices.reshape(parts, tok // QUAD, 2, 2), ("parts", "level", "side", "core")
    )
    rows = P(("parts", "level", "side", "core"), None)
    return jax.shard_map(
        functools.partial(per_device, tok // QUAD),
        mesh=quads,
        in_specs=(rows, rows, rows, rows, rows, P("parts", None)),
        out_specs=(rows, rows, rows),
        check_vma=False,
    )
```

```python
import functools
import math

import jax
import jax.numpy as jnp
from jax import lax
from jax.experimental import pallas as pl
from jax.experimental.pallas import tpu as pltpu
from jax.sharding import Mesh
from jax.sharding import PartitionSpec as P

QH = 32
KVH = 4
HD = 128
TILE = 128
GROUP = QH // KVH
ROWS = GROUP * TILE
PAIR = 2 * TILE
QUAD = 4
LEVEL = QUAD * TILE
SCALE = HD ** (-0.5)
SCALE2 = SCALE / math.log(2.0)
MASKED = -1e30
NT_DIMS = (((1,), (1,)), ((), ()))
PARAMS = pltpu.CompilerParams(vmem_limit_bytes=28 * 1024 * 1024)
SMALL_PARAMS = pltpu.CompilerParams(vmem_limit_bytes=16 * 1024 * 1024)


def delta_kernel(out_ref, grad_ref, after_ref, delta_ref):
    for head in range(QH):
        cols = slice(head * HD, (head + 1) * HD)
        product = out_ref[:, cols].astype(jnp.float32) * grad_ref[:, cols].astype(jnp.float32)
        delta_ref[head : head + 1, :] = jnp.sum(product.T, axis=0, keepdims=True)


def row_deltas(outputs, out_grad, after):
    return pl.pallas_call(
        delta_kernel,
        in_specs=[pl.BlockSpec(memory_space=pltpu.VMEM)] * 2 + [pl.BlockSpec(memory_space=pl.ANY)],
        out_shape=jax.ShapeDtypeStruct((QH, TILE), jnp.float32),
        compiler_params=SMALL_PARAMS,
        name="row_deltas",
    )(outputs, out_grad, after)


def live_counts(anc_ref, me, u, depth):
    tile = me ^ u
    cut = ((me >> 2) - 1) * QUAD
    near, live = jnp.int32(1), jnp.int32(1)
    for slot in range(depth):
        entry = anc_ref[tile, slot]
        live += (entry >= 0).astype(jnp.int32)
        near += ((entry >= 0) & (entry >= cut)).astype(jnp.int32)
    return tile, near, live


def chunk_slots(anc_ref, me, tile, depth, start, stop, lowest):
    def slot_of(entry):
        seen = jnp.where(entry == 0, tile, anc_ref[tile, jnp.clip(entry - 1, 0, depth - 1)])
        return ((me >> 2) - (seen >> 2) - lowest) * QUAD + ((seen ^ me) & (QUAD - 1))

    good = start + 1 < stop
    first = slot_of(start)
    return first, jnp.where(good, slot_of(start + 1), first), good


def slot_rows(slot):
    return pl.ds(pl.multiple_of(slot * TILE, TILE), TILE)


def two_tiles(ref, first, second):
    return jnp.concatenate([ref[slot_rows(first), :], ref[slot_rows(second), :]], axis=0)


def two_heads(ref, u, pair):
    left = ref[u, :, 2 * pair * HD : (2 * pair + 1) * HD]
    right = ref[u, :, (2 * pair + 1) * HD : (2 * pair + 2) * HD]
    return jnp.concatenate([left, right], axis=0)


def causal_mask():
    key_pos = lax.broadcasted_iota(jnp.int32, (TILE, PAIR), 0)
    query_pos = lax.broadcasted_iota(jnp.int32, (TILE, PAIR), 1) & (TILE - 1)
    return key_pos <= query_pos


def gather_queries(scratch, own, peer, side):
    scratch[0] = own[...]
    scratch[1] = peer[...]
    scratch[2] = side[:TILE, :]
    scratch[3] = side[TILE:, :]


def stats_kernel(depth, steps, me_ref, anc_ref, q_own, q_peer, q_side, *rest):
    k_refs = rest[:steps]
    lse_ref, q_all, k_all, top_max, total = rest[steps:]
    me = me_ref[0]
    gather_queries(q_all, q_own, q_peer, q_side)
    for shift, k_ref in enumerate(k_refs):
        k_all[shift * LEVEL : (shift + 1) * LEVEL, :] = k_ref[...]

    def one_tile(u, carry):
        tile, _, live = live_counts(anc_ref, me, u, depth)

        def chunk_stats(index, is_first):
            first, second, good = chunk_slots(anc_ref, me, tile, depth, 2 * index, live, 0)
            key_block = two_tiles(k_all, first, second)
            for pair in range(GROUP // 2):
                rows = slice(pair * PAIR, (pair + 1) * PAIR)
                raw = lax.dot_general(
                    key_block,
                    two_heads(q_all, u, pair),
                    NT_DIMS,
                    preferred_element_type=jnp.float32,
                )
                top, low = raw[:TILE], raw[TILE:]
                if is_first:
                    top = jnp.where(causal_mask(), top, MASKED)
                low_max = jnp.max(low, axis=0, keepdims=True)
                new_max = jnp.maximum(
                    jnp.max(top, axis=0, keepdims=True), jnp.where(good, low_max, MASKED)
                )
                if not is_first:
                    old_max = top_max[:, rows]
                    new_max = jnp.maximum(old_max, new_max)
                low_base = jnp.where(good, new_max, -MASKED)
                new_sum = jnp.sum(
                    jnp.exp2((top - new_max) * SCALE2), axis=0, keepdims=True
                ) + jnp.sum(jnp.exp2((low - low_base) * SCALE2), axis=0, keepdims=True)
                if not is_first:
                    new_sum += total[:, rows] * jnp.exp2((old_max - new_max) * SCALE2)
                top_max[:, rows] = new_max
                total[:, rows] = new_sum

        chunk_stats(0, True)

        def step(index, carry):
            chunk_stats(index, False)
            return carry

        lax.fori_loop(1, (live + 1) // 2, step, 0)
        lse_ref[u] = top_max[...] * SCALE2 + jnp.log2(total[...])
        return carry

    lax.fori_loop(0, QUAD, one_tile, 0)


def grads_kernel(depth, stage, steps, me_ref, anc_ref, q_own, q_peer, q_side, g_own, g_peer, g_side, d_own, d_peer, d_side, lse_ref, *rest):
    kv_refs, rest = rest[: 2 * steps], rest[2 * steps :]
    if stage != "far":
        dq_in, rest = rest[0], rest[1:]
    if stage == "own":
        dk_in, dv_in, rest = rest[0], rest[1], rest[2:]
    tiles = {"far": (0, 1, 2, 3), "side": (2, 3), "own": (0, 1)}[stage]
    lowest = 2 if stage == "far" else 0
    if stage == "far":
        dq_acc, partial_refs, rest = rest[0], rest[1 : 1 + steps], rest[1 + steps :]
    elif stage == "side":
        dq_side, dk_acc, dv_acc, rest = rest[0], rest[1], rest[2], rest[3:]
    else:
        dq_own, dq_peer, partial_refs, rest = rest[0], rest[1], rest[2 : 2 + steps], rest[2 + steps :]
    q_all, g_all, delta, k_all, v_all, rest = *rest[:5], rest[5:]
    if stage != "side":
        dk_acc, dv_acc, rest = rest[0], rest[1], rest[2:]
    if stage != "far":
        dq_acc = rest[0]
    me = me_ref[0]
    for place, u in enumerate(tiles):
        if u < 2:
            q_all[place] = (q_own, q_peer)[u][...]
            g_all[place] = (g_own, g_peer)[u][...]
        else:
            rows = slice((u - 2) * TILE, (u - 1) * TILE)
            q_all[place] = q_side[rows, :]
            g_all[place] = g_side[rows, :]
        for head in range(GROUP):
            cols = slice(head * TILE, (head + 1) * TILE)
            d_ref, row = ((d_own, 0), (d_peer, 0), (d_side, 0), (d_side, GROUP))[u]
            delta[place, :, cols] = d_ref[row + head : row + head + 1, :]
    for shift in range(steps):
        k_all[shift * LEVEL : (shift + 1) * LEVEL, :] = kv_refs[shift][...]
        v_all[shift * LEVEL : (shift + 1) * LEVEL, :] = kv_refs[steps + shift][...]
    if stage == "own":
        dk_acc[...] = dk_in[...]
        dv_acc[...] = dv_in[...]
    else:
        dk_acc[...] = jnp.zeros_like(dk_acc)
        dv_acc[...] = jnp.zeros_like(dv_acc)

    def one_tile(place, carry):
        u = tiles[0] + place
        tile, near, live = live_counts(anc_ref, me, u, depth)
        start, stop = (near, live) if stage == "far" else (0, near)
        if stage == "far":
            dq_acc[place] = jnp.zeros((HD, ROWS), jnp.float32)
        else:
            dq_acc[place] = dq_in[place]

        def chunk_grads(index, is_first):
            first, second, good = chunk_slots(
                anc_ref, me, tile, depth, start + 2 * index, stop, lowest
            )
            key_block = two_tiles(k_all, first, second)
            value_block = two_tiles(v_all, first, second)
            key_turned = key_block.T
            dk = jnp.zeros((PAIR, HD), jnp.float32)
            dv = jnp.zeros((PAIR, HD), jnp.float32)
            for pair in range(GROUP // 2):
                rows = slice(pair * PAIR, (pair + 1) * PAIR)
                query_block = two_heads(q_all, place, pair)
                grad_block = two_heads(g_all, place, pair)
                raw = lax.dot_general(
                    key_block, query_block, NT_DIMS, preferred_element_type=jnp.float32
                )
                grad_probs = lax.dot_general(
                    value_block, grad_block, NT_DIMS, preferred_element_type=jnp.float32
                )
                lse = lse_ref[u, :, rows]
                away = delta[place, :, rows]
                lows, scores = [], []
                for part in range(2):
                    half = slice(part * TILE, (part + 1) * TILE)
                    base = lse if part == 0 else jnp.where(good, lse, -MASKED)
                    attn = jnp.exp2(raw[half] * SCALE2 - base)
                    if is_first and part == 0:
                        attn = jnp.where(causal_mask(), attn, 0.0)
                    lows.append(attn.astype(jnp.bfloat16))
                    scores.append((attn * (grad_probs[half] - away)).astype(jnp.bfloat16))
                attn_low = jnp.concatenate(lows, axis=0)
                grad_scores = jnp.concatenate(scores, axis=0)
                dv += jnp.dot(attn_low, grad_block, preferred_element_type=jnp.float32)
                dk += jnp.dot(grad_scores, query_block, preferred_element_type=jnp.float32)
                dq_acc[place, :, rows] += jnp.dot(
                    key_turned, grad_scores, preferred_element_type=jnp.float32
                )
            dk_acc[slot_rows(first), :] += dk[:TILE]
            dk_acc[slot_rows(second), :] += dk[TILE:]
            dv_acc[slot_rows(first), :] += dv[:TILE]
            dv_acc[slot_rows(second), :] += dv[TILE:]

        def step(index, carry):
            chunk_grads(index, False)
            return carry

        if stage != "far":
            chunk_grads(0, True)
        lax.fori_loop(0 if stage == "far" else 1, (stop - start + 1) // 2, step, 0)
        return carry

    lax.fori_loop(0, len(tiles), one_tile, 0)

    if stage != "far":
        for place in range(2):
            for head in range(GROUP):
                cols = slice(head * HD, (head + 1) * HD)
                turned = (dq_acc[place, :, cols] * SCALE).T.astype(jnp.bfloat16)
                if stage == "side":
                    dq_side[place * TILE : (place + 1) * TILE, cols] = turned
                else:
                    (dq_own, dq_peer)[place][:, cols] = turned
    if stage != "side":
        for shift, out_ref in enumerate(partial_refs):
            rows = slice(shift * LEVEL, (shift + 1) * LEVEL)
            out_ref[:, :HD] = dk_acc[rows, :].astype(out_ref.dtype)
            out_ref[:, HD:] = dv_acc[rows, :].astype(out_ref.dtype)


def work(ancestors, products):
    pairs = QUAD * (ancestors.shape[1] + 1)
    return pl.CostEstimate(
        flops=2 * products * pairs * GROUP * TILE * TILE * 2 * HD,
        transcendentals=pairs * GROUP * TILE * TILE,
        bytes_accessed=16 * 1024 * 1024,
    )


def fixed(shape):
    return pl.BlockSpec(shape, lambda i, *_: (0,) * len(shape))


def own_head(me_ref):
    return ((me_ref[0] & 1) << 1) | ((me_ref[0] >> 1) & 1)


WIDE = pl.BlockSpec((TILE, ROWS), lambda i, me_ref, anc_ref: (0, own_head(me_ref)))
SMALL = pl.BlockSpec((GROUP, TILE), lambda i, me_ref, anc_ref: (own_head(me_ref), 0))
SIDE = fixed((PAIR, ROWS))
LSE = fixed((QUAD, 1, ROWS))
KEYS = fixed((LEVEL, HD))
SUMS = fixed((LEVEL, 2 * HD))
DQ = fixed((QUAD, HD, ROWS))
WIDE_OUT = fixed((TILE, ROWS))


def statistics(me, ancestors, q_set, k_list):
    steps = len(k_list)
    return pl.pallas_call(
        functools.partial(stats_kernel, ancestors.shape[1], steps),
        grid_spec=pltpu.PrefetchScalarGridSpec(
            num_scalar_prefetch=2,
            grid=(1,),
            in_specs=[WIDE, WIDE, SIDE] + [KEYS] * steps,
            out_specs=LSE,
            scratch_shapes=[
                pltpu.VMEM((QUAD, TILE, ROWS), jnp.bfloat16),
                pltpu.VMEM((steps * LEVEL, HD), jnp.bfloat16),
                pltpu.VMEM((1, ROWS), jnp.float32),
                pltpu.VMEM((1, ROWS), jnp.float32),
            ],
        ),
        out_shape=jax.ShapeDtypeStruct((QUAD, 1, ROWS), jnp.float32),
        compiler_params=PARAMS,
        cost_estimate=work(ancestors, 1),
        name="statistics",
    )(me, ancestors, *q_set, *k_list)


def gradients(stage, me, ancestors, q_set, g_set, d_set, lse, k_list, v_list, *carried):
    steps = len(k_list)
    tiles = QUAD if stage == "far" else 2
    acc = (steps * LEVEL, HD)
    wide = jax.ShapeDtypeStruct((TILE, ROWS), jnp.bfloat16)
    sums = [jax.ShapeDtypeStruct((LEVEL, 2 * HD), jnp.bfloat16)] * steps
    accs = [jax.ShapeDtypeStruct(acc, jnp.float32)] * 2
    dq_half = pl.BlockSpec((2, HD, ROWS), lambda i, *_: (1 if stage == "side" else 0, 0, 0))
    extra_specs = [dq_half, fixed(acc), fixed(acc)][: len(carried)]
    if stage == "far":
        out_specs = [DQ] + [SUMS] * steps
        out_shape = [jax.ShapeDtypeStruct((QUAD, HD, ROWS), jnp.float32)] + sums
    elif stage == "side":
        out_specs = [SIDE, fixed(acc), fixed(acc)]
        out_shape = [jax.ShapeDtypeStruct((PAIR, ROWS), jnp.bfloat16)] + accs
    else:
        sums[0] = jax.ShapeDtypeStruct((LEVEL, 2 * HD), jnp.float32)
        out_specs = [WIDE_OUT, WIDE_OUT] + [SUMS] * steps
        out_shape = [wide, wide] + sums
    scratch = [
        pltpu.VMEM((tiles, TILE, ROWS), jnp.bfloat16),
        pltpu.VMEM((tiles, TILE, ROWS), jnp.bfloat16),
        pltpu.VMEM((tiles, 1, ROWS), jnp.float32),
        pltpu.VMEM(acc, jnp.bfloat16),
        pltpu.VMEM(acc, jnp.bfloat16),
    ]
    if stage != "side":
        scratch += [pltpu.VMEM(acc, jnp.float32)] * 2
    if stage != "far":
        scratch.append(pltpu.VMEM((tiles, HD, ROWS), jnp.float32))
    return pl.pallas_call(
        functools.partial(grads_kernel, ancestors.shape[1], stage, steps),
        grid_spec=pltpu.PrefetchScalarGridSpec(
            num_scalar_prefetch=2,
            grid=(1,),
            in_specs=[WIDE, WIDE, SIDE, WIDE, WIDE, SIDE, SMALL, SMALL, fixed((2 * GROUP, TILE)), LSE]
            + [KEYS] * (2 * steps)
            + extra_specs,
            out_specs=out_specs,
            scratch_shapes=scratch,
        ),
        out_shape=out_shape,
        compiler_params=PARAMS,
        cost_estimate=work(ancestors, 5),
        name=stage + "_grads",
    )(me, ancestors, *q_set, *g_set, *d_set, lse, *k_list, *v_list, *carried)


def side_head(me_ref):
    return own_head(me_ref) ^ 1


def head_columns(head, width):
    return pl.ds(pl.multiple_of(head * width, width), width)


def pack_keys_kernel(me_ref, k_own, v_own, k_peer, v_peer, mine_ref, send_ref):
    for head, out_ref in ((own_head(me_ref), mine_ref), (side_head(me_ref), send_ref)):
        at = head_columns(head, HD)
        out_ref[:TILE, :HD] = k_own[:, at]
        out_ref[:TILE, HD:] = v_own[:, at]
        out_ref[TILE:, :HD] = k_peer[:, at]
        out_ref[TILE:, HD:] = v_peer[:, at]


SCALARS = pl.BlockSpec(memory_space=pltpu.SMEM)
HERE = pl.BlockSpec(memory_space=pltpu.VMEM)


def pack_keys(me, *arrays):
    return pl.pallas_call(
        pack_keys_kernel,
        in_specs=[SCALARS] + [HERE] * 4,
        out_specs=[HERE] * 2,
        out_shape=[jax.ShapeDtypeStruct((PAIR, 2 * HD), jnp.bfloat16)] * 2,
        compiler_params=SMALL_PARAMS,
        name="pack_keys",
    )(me, *arrays)


def pack_queries_kernel(me_ref, q_own, q_peer, g_own, g_peer, q_ref, g_ref):
    at = head_columns(side_head(me_ref), ROWS)
    q_ref[:TILE, :] = q_own[:, at]
    q_ref[TILE:, :] = q_peer[:, at]
    g_ref[:TILE, :] = g_own[:, at]
    g_ref[TILE:, :] = g_peer[:, at]


def pack_queries(me, *arrays):
    return pl.pallas_call(
        pack_queries_kernel,
        in_specs=[SCALARS] + [HERE] * 4,
        out_specs=[HERE] * 2,
        out_shape=[jax.ShapeDtypeStruct((PAIR, ROWS), jnp.bfloat16)] * 2,
        compiler_params=SMALL_PARAMS,
        name="pack_queries",
    )(me, *arrays)


def pack_deltas_kernel(me_ref, d_own, d_peer, send_ref):
    send_ref[:GROUP, :] = d_own[...]
    send_ref[GROUP:, :] = d_peer[...]


def pack_deltas(me, deltas, d_peer):
    away = pl.BlockSpec((GROUP, TILE), lambda i, me_ref: (side_head(me_ref), 0))
    return pl.pallas_call(
        pack_deltas_kernel,
        grid_spec=pltpu.PrefetchScalarGridSpec(
            num_scalar_prefetch=1,
            grid=(1,),
            in_specs=[away] * 2,
            out_specs=fixed((2 * GROUP, TILE)),
        ),
        out_shape=jax.ShapeDtypeStruct((2 * GROUP, TILE), jnp.float32),
        compiler_params=SMALL_PARAMS,
        name="pack_deltas",
    )(me, deltas, d_peer)


def add_far_kernel(total_ref, *refs):
    parts, out_ref = refs[:-3], refs[-2]
    total = total_ref[...]
    for part in parts:
        total += part[...].astype(jnp.float32)
    out_ref[...] = total


def add_far(acc, parts, passing):
    here = pl.BlockSpec(memory_space=pltpu.VMEM)
    anywhere = pl.BlockSpec(memory_space=pl.ANY)
    return pl.pallas_call(
        add_far_kernel,
        in_specs=[here] * (1 + len(parts)) + [anywhere],
        out_specs=[here, anywhere],
        out_shape=[
            jax.ShapeDtypeStruct(acc.shape, jnp.float32),
            jax.ShapeDtypeStruct(passing.shape, passing.dtype),
        ],
        input_output_aliases={1 + len(parts): 1},
        compiler_params=SMALL_PARAMS,
        name="add_far",
    )(acc, *parts, passing)


def add_sums_kernel(total_ref, near_ref, own_ref, peer_ref, send_ref):
    total = total_ref[...] + near_ref[...].astype(jnp.float32)
    scaled = jnp.concatenate([total[:, :HD] * SCALE, total[:, HD:]], axis=1).astype(jnp.bfloat16)
    own_ref[...] = scaled[:TILE]
    peer_ref[...] = scaled[TILE:PAIR]
    send_ref[...] = scaled[PAIR:]


def add_sums(total, near):
    here = pl.BlockSpec(memory_space=pltpu.VMEM)
    return pl.pallas_call(
        add_sums_kernel,
        in_specs=[here] * 2,
        out_specs=[here] * 3,
        out_shape=[
            jax.ShapeDtypeStruct((TILE, 2 * HD), jnp.bfloat16),
            jax.ShapeDtypeStruct((TILE, 2 * HD), jnp.bfloat16),
            jax.ShapeDtypeStruct((PAIR, 2 * HD), jnp.bfloat16),
        ],
        compiler_params=SMALL_PARAMS,
        name="add_sums",
    )(total, near)


def placed(me_ref, width):
    head = own_head(me_ref)
    return [head_columns(head ^ flip, width) for flip in range(4)]


def place_queries_kernel(me_ref, own, side, peer, far, dq_ref):
    at = placed(me_ref, ROWS)
    dq_ref[:, at[0]] = own[...]
    dq_ref[:, at[1]] = side[:TILE, :]
    dq_ref[:, at[2]] = peer[...]
    dq_ref[:, at[3]] = far[...]


def place_queries(me, *pieces):
    return pl.pallas_call(
        place_queries_kernel,
        in_specs=[SCALARS] + [HERE] * 4,
        out_specs=HERE,
        out_shape=jax.ShapeDtypeStruct((TILE, QH * HD), jnp.bfloat16),
        compiler_params=SMALL_PARAMS,
        name="place_queries",
    )(me, *pieces)


def place_keys_kernel(me_ref, own, side, peer, far, dk_ref, dv_ref):
    at = placed(me_ref, HD)
    for spot, part in zip(at, (own[...], side[:TILE, :], peer[...], far[...])):
        dk_ref[:, spot] = part[:, :HD]
        dv_ref[:, spot] = part[:, HD:]


def place_keys(me, *pieces):
    return pl.pallas_call(
        place_keys_kernel,
        in_specs=[SCALARS] + [HERE] * 4,
        out_specs=[HERE] * 2,
        out_shape=[jax.ShapeDtypeStruct((TILE, KVH * HD), jnp.bfloat16)] * 2,
        compiler_params=SMALL_PARAMS,
        name="place_keys",
    )(me, *pieces)


def per_device(steps, queries, keys, values, outputs, out_grad, ancestors):
    level, side, core = (lax.axis_index(name) for name in ("level", "side", "core"))
    me = (QUAD * level + 2 * side + core).reshape(1).astype(jnp.int32)

    def to_peer(x):
        return lax.ppermute(x, "core", [(0, 1), (1, 0)])

    def to_side(x):
        return lax.ppermute(x, "side", [(0, 1), (1, 0)])

    def up(x, shift):
        return lax.ppermute(x, "level", [(z, z + shift) for z in range(steps - shift)])

    def down(x, shift):
        return lax.ppermute(x, "level", [(z + shift, z) for z in range(steps - shift)])

    kv_chip, kv_send = pack_keys(me, keys, values, to_peer(keys), to_peer(values))
    kv_side = to_side(kv_send)
    k_level = jnp.concatenate([kv_chip[:, :HD], kv_side[:, :HD]], axis=0)
    v_level = jnp.concatenate([kv_chip[:, HD:], kv_side[:, HD:]], axis=0)
    k_list = [k_level] + [up(k_level, shift) for shift in range(1, steps)]
    q_peer, g_peer = to_peer(queries), to_peer(out_grad)
    q_send, g_send = pack_queries(me, queries, q_peer, out_grad, g_peer)
    q_set = (queries, q_peer, to_side(q_send))
    v_list = [v_level] + [up(v_level, shift) for shift in range(1, steps)]
    g_set = (out_grad, g_peer, to_side(g_send))
    deltas = row_deltas(outputs, out_grad, kv_send)
    d_peer = to_peer(deltas)
    d_set = (deltas, d_peer, to_side(pack_deltas(me, deltas, d_peer)))

    lse = statistics(me, ancestors, q_set, k_list)
    common = (me, ancestors, q_set, g_set, d_set, lse)
    dq_far, *far = gradients("far", *common, k_list[2:], v_list[2:])
    back = [down(far[shift - 2], shift) for shift in range(2, steps)]
    dq_side, *accs = gradients("side", *common, k_list[:2], v_list[:2], dq_far)
    dq_side = to_side(dq_side)
    dq_own, dq_peer, total, near = gradients(
        "own", *common, k_list[:2], v_list[:2], dq_far, *accs
    )
    total, near = add_far(total, back, near)
    near = down(near, 1)
    dq_peer = to_peer(dq_peer)

    sum_own, sum_peer, sum_side = add_sums(total, near)
    dq_far = to_peer(dq_side[TILE:])
    sum_peer = to_peer(sum_peer)
    sum_side = to_side(sum_side)
    sum_far = to_peer(sum_side[TILE:])
    return (
        place_queries(me, dq_own, dq_side, dq_peer, dq_far),
        *place_keys(me, sum_own, sum_side, sum_peer, sum_far),
    )


def solution(mesh):
    parts, tok = mesh.shape["parts"], mesh.shape["tok"]
    quads = Mesh(
        mesh.devices.reshape(parts, tok // QUAD, 2, 2), ("parts", "level", "side", "core")
    )
    rows = P(("parts", "level", "side", "core"), None)
    return jax.shard_map(
        functools.partial(per_device, tok // QUAD),
        mesh=quads,
        in_specs=(rows, rows, rows, rows, rows, P("parts", None)),
        out_specs=(rows, rows, rows),
        check_vma=False,
    )
```

```python
import functools
import math

import jax
import jax.numpy as jnp
from jax import lax
from jax.experimental import pallas as pl
from jax.experimental.pallas import tpu as pltpu
from jax.sharding import Mesh
from jax.sharding import PartitionSpec as P

QH = 32
KVH = 4
HD = 128
TILE = 128
GROUP = QH // KVH
ROWS = GROUP * TILE
PAIR = 2 * TILE
QUAD = 4
LEVEL = QUAD * TILE
SCALE = HD ** (-0.5)
SCALE2 = SCALE / math.log(2.0)
MASKED = -1e30
NT_DIMS = (((1,), (1,)), ((), ()))
PARAMS = pltpu.CompilerParams(vmem_limit_bytes=28 * 1024 * 1024)
SMALL_PARAMS = pltpu.CompilerParams(vmem_limit_bytes=16 * 1024 * 1024)


def delta_kernel(out_ref, grad_ref, after_ref, delta_ref):
    for head in range(QH):
        cols = slice(head * HD, (head + 1) * HD)
        product = out_ref[:, cols].astype(jnp.float32) * grad_ref[:, cols].astype(jnp.float32)
        delta_ref[head : head + 1, :] = jnp.sum(product.T, axis=0, keepdims=True)


def row_deltas(outputs, out_grad, after):
    return pl.pallas_call(
        delta_kernel,
        in_specs=[pl.BlockSpec(memory_space=pltpu.VMEM)] * 2 + [pl.BlockSpec(memory_space=pl.ANY)],
        out_shape=jax.ShapeDtypeStruct((QH, TILE), jnp.float32),
        compiler_params=SMALL_PARAMS,
        name="row_deltas",
    )(outputs, out_grad, after)


def list_items(items, anc_ref, me, tiles, depth, part):
    tile_of, first_of, second_of, flags_of = items
    cut = ((me >> 2) - 1) * QUAD
    lowest = 2 if part == "far" else 0
    count = jnp.int32(0)
    for place, u in enumerate(tiles):
        tile = me ^ u
        near, live = jnp.int32(1), jnp.int32(1)
        for slot in range(depth):
            entry = anc_ref[tile, slot]
            live += (entry >= 0).astype(jnp.int32)
            near += ((entry >= 0) & (entry >= cut)).astype(jnp.int32)
        start = near if part == "far" else jnp.int32(0)
        stop = near if part == "near" else live
        chunks = (stop - start + 1) // 2

        def slot_of(entry, tile=tile):
            seen = jnp.where(entry == 0, tile, anc_ref[tile, jnp.clip(entry - 1, 0, depth - 1)])
            return ((me >> 2) - (seen >> 2) - lowest) * QUAD + ((seen ^ me) & (QUAD - 1))

        def note(chunk, carry, place=place, start=start, stop=stop, count=count, slot_of=slot_of):
            entry = start + 2 * chunk
            good = entry + 1 < stop
            first = slot_of(entry)
            tile_of[count + chunk] = place
            first_of[count + chunk] = first
            second_of[count + chunk] = jnp.where(good, slot_of(entry + 1), first)
            flags_of[count + chunk] = 1 + 2 * good.astype(jnp.int32) + 4 * (entry == 0).astype(jnp.int32)
            return carry

        lax.fori_loop(0, chunks, note, 0)
        count += chunks
    for extra in range(2):
        tile_of[count + extra] = 0
        first_of[count + extra] = 0
        second_of[count + extra] = 0
        flags_of[count + extra] = 0
    return count


def item_scratch(tiles, depth):
    return [pltpu.SMEM((tiles * ((depth + 2) // 2) + 2,), jnp.int32)] * 4


def slot_rows(slot):
    return pl.ds(pl.multiple_of(slot * TILE, TILE), TILE)


def two_tiles(ref, first, second):
    return jnp.concatenate([ref[slot_rows(first), :], ref[slot_rows(second), :]], axis=0)


def heads_below(ref, u, first, count):
    return jnp.concatenate(
        [ref[u, :, head * HD : (head + 1) * HD] for head in range(first, first + count)], axis=0
    )


def visible_mask(flags):
    key_pos = lax.broadcasted_iota(jnp.int32, (TILE, PAIR), 0)
    query_pos = lax.broadcasted_iota(jnp.int32, (TILE, PAIR), 1) & (TILE - 1)
    return key_pos - query_pos <= jnp.where((flags & 4) != 0, 0, TILE)


def gather_queries(scratch, own, peer, side):
    scratch[0] = own[...]
    scratch[1] = peer[...]
    scratch[2] = side[:TILE, :]
    scratch[3] = side[TILE:, :]


def stats_kernel(depth, steps, me_ref, anc_ref, q_own, q_peer, q_side, *rest):
    k_refs = rest[:steps]
    lse_ref, q_all, k_all, item_max, item_sum, *items = rest[steps:]
    me = me_ref[0]
    gather_queries(q_all, q_own, q_peer, q_side)
    for shift, k_ref in enumerate(k_refs):
        k_all[shift * LEVEL : (shift + 1) * LEVEL, :] = k_ref[...]
    count = list_items(items, anc_ref, me, range(QUAD), depth, "all")
    tile_of, first_of, second_of, flags_of = items

    def one_item(index):
        u, flags = tile_of[index], flags_of[index]
        good = (flags & 2) != 0
        key_block = two_tiles(k_all, first_of[index], second_of[index])
        mask = visible_mask(flags)
        for pair in range(GROUP // 2):
            rows = slice(pair * PAIR, (pair + 1) * PAIR)
            raw = lax.dot_general(
                key_block,
                heads_below(q_all, u, 2 * pair, 2),
                NT_DIMS,
                preferred_element_type=jnp.float32,
            )
            top, low = jnp.where(mask, raw[:TILE], MASKED), raw[TILE:]
            low_max = jnp.max(low, axis=0, keepdims=True)
            new_max = jnp.maximum(
                jnp.max(top, axis=0, keepdims=True), jnp.where(good, low_max, MASKED)
            )
            low_base = jnp.where(good, new_max, -MASKED)
            item_max[index, :, rows] = new_max
            item_sum[index, :, rows] = jnp.sum(
                jnp.exp2((top - new_max) * SCALE2), axis=0, keepdims=True
            ) + jnp.sum(jnp.exp2((low - low_base) * SCALE2), axis=0, keepdims=True)

    def step(index, carry):
        one_item(2 * index)
        one_item(2 * index + 1)
        return carry

    lax.fori_loop(0, (count + 1) // 2, step, 0)

    lse_ref[...] = jnp.full_like(lse_ref, MASKED)

    def combine(index, carry):
        u = tile_of[index]
        old = lse_ref[u]
        new = item_max[index] * SCALE2 + jnp.log2(item_sum[index])
        top = jnp.maximum(old, new)
        lse_ref[u] = top + jnp.log2(jnp.exp2(old - top) + jnp.exp2(new - top))
        return carry

    lax.fori_loop(0, count, combine, 0)


def grads_kernel(depth, stage, steps, me_ref, anc_ref, q_own, q_peer, q_side, g_own, g_peer, g_side, d_own, d_peer, d_side, lse_ref, *rest):
    kv_refs, rest = rest[: 2 * steps], rest[2 * steps :]
    if stage != "far":
        dq_in, rest = rest[0], rest[1:]
    if stage == "own":
        dk_in, dv_in, rest = rest[0], rest[1], rest[2:]
    tiles = {"far": (0, 1, 2, 3), "side": (2, 3), "own": (0, 1)}[stage]
    if stage == "far":
        dq_acc, partial_refs, rest = rest[0], rest[1 : 1 + steps], rest[1 + steps :]
    elif stage == "side":
        dq_side, dk_acc, dv_acc, rest = rest[0], rest[1], rest[2], rest[3:]
    else:
        dq_own, dq_peer, partial_refs, rest = rest[0], rest[1], rest[2 : 2 + steps], rest[2 + steps :]
    items, rest = rest[:4], rest[4:]
    q_all, g_all, delta, k_all, v_all = rest[:5]
    buffers, rest = ((rest[5], rest[6]), (rest[7], rest[8])), rest[9:]
    if stage != "side":
        dk_acc, dv_acc, rest = rest[0], rest[1], rest[2:]
    if stage != "far":
        dq_acc = rest[0]
    me = me_ref[0]
    for place, u in enumerate(tiles):
        if u < 2:
            q_all[place] = (q_own, q_peer)[u][...]
            g_all[place] = (g_own, g_peer)[u][...]
        else:
            rows = slice((u - 2) * TILE, (u - 1) * TILE)
            q_all[place] = q_side[rows, :]
            g_all[place] = g_side[rows, :]
        for head in range(GROUP):
            cols = slice(head * TILE, (head + 1) * TILE)
            d_ref, row = ((d_own, 0), (d_peer, 0), (d_side, 0), (d_side, GROUP))[u]
            delta[place, :, cols] = d_ref[row + head : row + head + 1, :]
    for shift in range(steps):
        k_all[shift * LEVEL : (shift + 1) * LEVEL, :] = kv_refs[shift][...]
        v_all[shift * LEVEL : (shift + 1) * LEVEL, :] = kv_refs[steps + shift][...]
    if stage == "own":
        dk_acc[...] = dk_in[...]
        dv_acc[...] = dv_in[...]
    else:
        dk_acc[...] = jnp.zeros_like(dk_acc)
        dv_acc[...] = jnp.zeros_like(dv_acc)
    if stage == "far":
        dq_acc[...] = jnp.zeros_like(dq_acc)
    else:
        dq_acc[...] = dq_in[...]
    for buffer in buffers[1]:
        buffer[...] = jnp.zeros_like(buffer)
    count = list_items(items, anc_ref, me, tiles, depth, "far" if stage == "far" else "near")
    tile_of, first_of, second_of, flags_of = items

    def scores_part(index, low_ref, score_ref):
        place, flags = tile_of[index], flags_of[index]
        first, second = first_of[index], second_of[index]
        key_block = two_tiles(k_all, first, second)
        value_block = two_tiles(v_all, first, second)
        for pair in range(GROUP // 2):
            rows = slice(pair * PAIR, (pair + 1) * PAIR)
            raw = lax.dot_general(
                key_block,
                heads_below(q_all, place, 2 * pair, 2),
                NT_DIMS,
                preferred_element_type=jnp.float32,
            )
            grad_probs = lax.dot_general(
                value_block,
                heads_below(g_all, place, 2 * pair, 2),
                NT_DIMS,
                preferred_element_type=jnp.float32,
            )
            lse = lse_ref[tiles[0] + place, :, rows]
            away = delta[place, :, rows]
            for part in range(2):
                half = slice(part * TILE, (part + 1) * TILE)
                base = jnp.where((flags & (1 + part)) != 0, lse, -MASKED)
                attn = jnp.exp2(raw[half] * SCALE2 - base)
                if stage != "far" and part == 0:
                    attn = jnp.where(visible_mask(flags), attn, 0.0)
                low_ref[half, rows] = attn.astype(jnp.bfloat16)
                score_ref[half, rows] = (attn * (grad_probs[half] - away)).astype(jnp.bfloat16)

    def grads_part(index, low_ref, score_ref):
        index = jnp.maximum(index, 0)
        place, first, second = tile_of[index], first_of[index], second_of[index]
        dv = jnp.dot(
            low_ref[...], heads_below(g_all, place, 0, GROUP), preferred_element_type=jnp.float32
        )
        dk = jnp.dot(
            score_ref[...], heads_below(q_all, place, 0, GROUP), preferred_element_type=jnp.float32
        )
        dq_acc[place] += jnp.dot(
            two_tiles(k_all, first, second).T, score_ref[...], preferred_element_type=jnp.float32
        )
        dk_acc[slot_rows(first), :] += dk[:TILE]
        dk_acc[slot_rows(second), :] += dk[TILE:]
        dv_acc[slot_rows(first), :] += dv[:TILE]
        dv_acc[slot_rows(second), :] += dv[TILE:]

    def step(index, carry):
        scores_part(2 * index, *buffers[0])
        grads_part(2 * index - 1, *buffers[1])
        scores_part(2 * index + 1, *buffers[1])
        grads_part(2 * index, *buffers[0])
        return carry

    lax.fori_loop(0, jnp.where(count > 0, (count + 2) // 2, 0), step, 0)

    if stage != "far":
        for place in range(2):
            for head in range(GROUP):
                cols = slice(head * HD, (head + 1) * HD)
                turned = (dq_acc[place, :, cols] * SCALE).T.astype(jnp.bfloat16)
                if stage == "side":
                    dq_side[place * TILE : (place + 1) * TILE, cols] = turned
                else:
                    (dq_own, dq_peer)[place][:, cols] = turned
    if stage != "side":
        for shift, out_ref in enumerate(partial_refs):
            rows = slice(shift * LEVEL, (shift + 1) * LEVEL)
            out_ref[:, :HD] = dk_acc[rows, :].astype(out_ref.dtype)
            out_ref[:, HD:] = dv_acc[rows, :].astype(out_ref.dtype)


def work(ancestors, products):
    pairs = QUAD * (ancestors.shape[1] + 1)
    return pl.CostEstimate(
        flops=2 * products * pairs * GROUP * TILE * TILE * 2 * HD,
        transcendentals=pairs * GROUP * TILE * TILE,
        bytes_accessed=16 * 1024 * 1024,
    )


def fixed(shape):
    return pl.BlockSpec(shape, lambda i, *_: (0,) * len(shape))


def own_head(me_ref):
    return ((me_ref[0] & 1) << 1) | ((me_ref[0] >> 1) & 1)


WIDE = pl.BlockSpec((TILE, ROWS), lambda i, me_ref, anc_ref: (0, own_head(me_ref)))
SMALL = pl.BlockSpec((GROUP, TILE), lambda i, me_ref, anc_ref: (own_head(me_ref), 0))
SIDE = fixed((PAIR, ROWS))
LSE = fixed((QUAD, 1, ROWS))
KEYS = fixed((LEVEL, HD))
SUMS = fixed((LEVEL, 2 * HD))
DQ = fixed((QUAD, HD, ROWS))
WIDE_OUT = fixed((TILE, ROWS))


def statistics(me, ancestors, q_set, k_list):
    steps = len(k_list)
    items = item_scratch(QUAD, ancestors.shape[1])
    count = items[0].shape[0]
    return pl.pallas_call(
        functools.partial(stats_kernel, ancestors.shape[1], steps),
        grid_spec=pltpu.PrefetchScalarGridSpec(
            num_scalar_prefetch=2,
            grid=(1,),
            in_specs=[WIDE, WIDE, SIDE] + [KEYS] * steps,
            out_specs=LSE,
            scratch_shapes=[
                pltpu.VMEM((QUAD, TILE, ROWS), jnp.bfloat16),
                pltpu.VMEM((steps * LEVEL, HD), jnp.bfloat16),
                pltpu.VMEM((count, 1, ROWS), jnp.float32),
                pltpu.VMEM((count, 1, ROWS), jnp.float32),
                *items,
            ],
        ),
        out_shape=jax.ShapeDtypeStruct((QUAD, 1, ROWS), jnp.float32),
        compiler_params=PARAMS,
        cost_estimate=work(ancestors, 1),
        name="statistics",
    )(me, ancestors, *q_set, *k_list)


def gradients(stage, me, ancestors, q_set, g_set, d_set, lse, k_list, v_list, *carried):
    steps = len(k_list)
    tiles = QUAD if stage == "far" else 2
    acc = (steps * LEVEL, HD)
    wide = jax.ShapeDtypeStruct((TILE, ROWS), jnp.bfloat16)
    sums = [jax.ShapeDtypeStruct((LEVEL, 2 * HD), jnp.bfloat16)] * steps
    accs = [jax.ShapeDtypeStruct(acc, jnp.float32)] * 2
    dq_half = pl.BlockSpec((2, HD, ROWS), lambda i, *_: (1 if stage == "side" else 0, 0, 0))
    extra_specs = [dq_half, fixed(acc), fixed(acc)][: len(carried)]
    if stage == "far":
        out_specs = [DQ] + [SUMS] * steps
        out_shape = [jax.ShapeDtypeStruct((QUAD, HD, ROWS), jnp.float32)] + sums
    elif stage == "side":
        out_specs = [SIDE, fixed(acc), fixed(acc)]
        out_shape = [jax.ShapeDtypeStruct((PAIR, ROWS), jnp.bfloat16)] + accs
    else:
        sums[0] = jax.ShapeDtypeStruct((LEVEL, 2 * HD), jnp.float32)
        out_specs = [WIDE_OUT, WIDE_OUT] + [SUMS] * steps
        out_shape = [wide, wide] + sums
    scratch = item_scratch(tiles, ancestors.shape[1]) + [
        pltpu.VMEM((tiles, TILE, ROWS), jnp.bfloat16),
        pltpu.VMEM((tiles, TILE, ROWS), jnp.bfloat16),
        pltpu.VMEM((tiles, 1, ROWS), jnp.float32),
        pltpu.VMEM(acc, jnp.bfloat16),
        pltpu.VMEM(acc, jnp.bfloat16),
    ]
    scratch += [pltpu.VMEM((PAIR, ROWS), jnp.bfloat16)] * 4
    if stage != "side":
        scratch += [pltpu.VMEM(acc, jnp.float32)] * 2
    if stage != "far":
        scratch.append(pltpu.VMEM((tiles, HD, ROWS), jnp.float32))
    return pl.pallas_call(
        functools.partial(grads_kernel, ancestors.shape[1], stage, steps),
        grid_spec=pltpu.PrefetchScalarGridSpec(
            num_scalar_prefetch=2,
            grid=(1,),
            in_specs=[WIDE, WIDE, SIDE, WIDE, WIDE, SIDE, SMALL, SMALL, fixed((2 * GROUP, TILE)), LSE]
            + [KEYS] * (2 * steps)
            + extra_specs,
            out_specs=out_specs,
            scratch_shapes=scratch,
        ),
        out_shape=out_shape,
        compiler_params=PARAMS,
        cost_estimate=work(ancestors, 5),
        name=stage + "_grads",
    )(me, ancestors, *q_set, *g_set, *d_set, lse, *k_list, *v_list, *carried)


def side_head(me_ref):
    return own_head(me_ref) ^ 1


def head_columns(head, width):
    return pl.ds(pl.multiple_of(head * width, width), width)


def pack_keys_kernel(me_ref, k_own, v_own, k_peer, v_peer, mine_ref, send_ref):
    for head, out_ref in ((own_head(me_ref), mine_ref), (side_head(me_ref), send_ref)):
        at = head_columns(head, HD)
        out_ref[:TILE, :HD] = k_own[:, at]
        out_ref[:TILE, HD:] = v_own[:, at]
        out_ref[TILE:, :HD] = k_peer[:, at]
        out_ref[TILE:, HD:] = v_peer[:, at]


SCALARS = pl.BlockSpec(memory_space=pltpu.SMEM)
HERE = pl.BlockSpec(memory_space=pltpu.VMEM)


def pack_keys(me, *arrays):
    return pl.pallas_call(
        pack_keys_kernel,
        in_specs=[SCALARS] + [HERE] * 4,
        out_specs=[HERE] * 2,
        out_shape=[jax.ShapeDtypeStruct((PAIR, 2 * HD), jnp.bfloat16)] * 2,
        compiler_params=SMALL_PARAMS,
        name="pack_keys",
    )(me, *arrays)


def pack_queries_kernel(me_ref, q_own, q_peer, g_own, g_peer, q_ref, g_ref):
    at = head_columns(side_head(me_ref), ROWS)
    q_ref[:TILE, :] = q_own[:, at]
    q_ref[TILE:, :] = q_peer[:, at]
    g_ref[:TILE, :] = g_own[:, at]
    g_ref[TILE:, :] = g_peer[:, at]


def pack_queries(me, *arrays):
    return pl.pallas_call(
        pack_queries_kernel,
        in_specs=[SCALARS] + [HERE] * 4,
        out_specs=[HERE] * 2,
        out_shape=[jax.ShapeDtypeStruct((PAIR, ROWS), jnp.bfloat16)] * 2,
        compiler_params=SMALL_PARAMS,
        name="pack_queries",
    )(me, *arrays)


def pack_deltas_kernel(me_ref, d_own, d_peer, send_ref):
    send_ref[:GROUP, :] = d_own[...]
    send_ref[GROUP:, :] = d_peer[...]


def pack_deltas(me, deltas, d_peer):
    away = pl.BlockSpec((GROUP, TILE), lambda i, me_ref: (side_head(me_ref), 0))
    return pl.pallas_call(
        pack_deltas_kernel,
        grid_spec=pltpu.PrefetchScalarGridSpec(
            num_scalar_prefetch=1,
            grid=(1,),
            in_specs=[away] * 2,
            out_specs=fixed((2 * GROUP, TILE)),
        ),
        out_shape=jax.ShapeDtypeStruct((2 * GROUP, TILE), jnp.float32),
        compiler_params=SMALL_PARAMS,
        name="pack_deltas",
    )(me, deltas, d_peer)


def add_far_kernel(total_ref, *refs):
    parts, out_ref = refs[:-3], refs[-2]
    total = total_ref[...]
    for part in parts:
        total += part[...].astype(jnp.float32)
    out_ref[...] = total


def add_far(acc, parts, passing):
    here = pl.BlockSpec(memory_space=pltpu.VMEM)
    anywhere = pl.BlockSpec(memory_space=pl.ANY)
    return pl.pallas_call(
        add_far_kernel,
        in_specs=[here] * (1 + len(parts)) + [anywhere],
        out_specs=[here, anywhere],
        out_shape=[
            jax.ShapeDtypeStruct(acc.shape, jnp.float32),
            jax.ShapeDtypeStruct(passing.shape, passing.dtype),
        ],
        input_output_aliases={1 + len(parts): 1},
        compiler_params=SMALL_PARAMS,
        name="add_far",
    )(acc, *parts, passing)


def add_sums_kernel(total_ref, near_ref, own_ref, peer_ref, send_ref):
    total = total_ref[...] + near_ref[...].astype(jnp.float32)
    scaled = jnp.concatenate([total[:, :HD] * SCALE, total[:, HD:]], axis=1).astype(jnp.bfloat16)
    own_ref[...] = scaled[:TILE]
    peer_ref[...] = scaled[TILE:PAIR]
    send_ref[...] = scaled[PAIR:]


def add_sums(total, near):
    here = pl.BlockSpec(memory_space=pltpu.VMEM)
    return pl.pallas_call(
        add_sums_kernel,
        in_specs=[here] * 2,
        out_specs=[here] * 3,
        out_shape=[
            jax.ShapeDtypeStruct((TILE, 2 * HD), jnp.bfloat16),
            jax.ShapeDtypeStruct((TILE, 2 * HD), jnp.bfloat16),
            jax.ShapeDtypeStruct((PAIR, 2 * HD), jnp.bfloat16),
        ],
        compiler_params=SMALL_PARAMS,
        name="add_sums",
    )(total, near)


def placed(me_ref, width):
    head = own_head(me_ref)
    return [head_columns(head ^ flip, width) for flip in range(4)]


def place_queries_kernel(me_ref, own, side, peer, far, dq_ref):
    at = placed(me_ref, ROWS)
    dq_ref[:, at[0]] = own[...]
    dq_ref[:, at[1]] = side[:TILE, :]
    dq_ref[:, at[2]] = peer[...]
    dq_ref[:, at[3]] = far[...]


def place_queries(me, *pieces):
    return pl.pallas_call(
        place_queries_kernel,
        in_specs=[SCALARS] + [HERE] * 4,
        out_specs=HERE,
        out_shape=jax.ShapeDtypeStruct((TILE, QH * HD), jnp.bfloat16),
        compiler_params=SMALL_PARAMS,
        name="place_queries",
    )(me, *pieces)


def place_keys_kernel(me_ref, own, side, peer, far, dk_ref, dv_ref):
    at = placed(me_ref, HD)
    for spot, part in zip(at, (own[...], side[:TILE, :], peer[...], far[...])):
        dk_ref[:, spot] = part[:, :HD]
        dv_ref[:, spot] = part[:, HD:]


def place_keys(me, *pieces):
    return pl.pallas_call(
        place_keys_kernel,
        in_specs=[SCALARS] + [HERE] * 4,
        out_specs=[HERE] * 2,
        out_shape=[jax.ShapeDtypeStruct((TILE, KVH * HD), jnp.bfloat16)] * 2,
        compiler_params=SMALL_PARAMS,
        name="place_keys",
    )(me, *pieces)


def per_device(steps, queries, keys, values, outputs, out_grad, ancestors):
    level, side, core = (lax.axis_index(name) for name in ("level", "side", "core"))
    me = (QUAD * level + 2 * side + core).reshape(1).astype(jnp.int32)

    def to_peer(x):
        return lax.ppermute(x, "core", [(0, 1), (1, 0)])

    def to_side(x):
        return lax.ppermute(x, "side", [(0, 1), (1, 0)])

    def up(x, shift):
        return lax.ppermute(x, "level", [(z, z + shift) for z in range(steps - shift)])

    def up_all(x):
        arrivals = [x] + [up(x, shift) for shift in range(1, min(steps, 3))]
        for shift in range(3, steps):
            pairs = [(z, z + 1) for z in range(shift - 1, steps - 1)]
            arrivals.append(lax.ppermute(arrivals[-1], "level", pairs))
        return arrivals

    def down(x, shift):
        return lax.ppermute(x, "level", [(z + shift, z) for z in range(steps - shift)])

    kv_chip, kv_send = pack_keys(me, keys, values, to_peer(keys), to_peer(values))
    kv_side = to_side(kv_send)
    k_level = jnp.concatenate([kv_chip[:, :HD], kv_side[:, :HD]], axis=0)
    v_level = jnp.concatenate([kv_chip[:, HD:], kv_side[:, HD:]], axis=0)
    k_list = up_all(k_level)
    q_peer, g_peer = to_peer(queries), to_peer(out_grad)
    q_send, g_send = pack_queries(me, queries, q_peer, out_grad, g_peer)
    q_set = (queries, q_peer, to_side(q_send))
    v_list = up_all(v_level)
    g_set = (out_grad, g_peer, to_side(g_send))
    deltas = row_deltas(outputs, out_grad, kv_send)
    d_peer = to_peer(deltas)
    d_set = (deltas, d_peer, to_side(pack_deltas(me, deltas, d_peer)))

    lse = statistics(me, ancestors, q_set, k_list)
    common = (me, ancestors, q_set, g_set, d_set, lse)
    dq_far, *far = gradients("far", *common, k_list[2:], v_list[2:])
    back = [down(far[shift - 2], shift) for shift in range(2, steps)]
    dq_side, *accs = gradients("side", *common, k_list[:2], v_list[:2], dq_far)
    dq_side = to_side(dq_side)
    dq_own, dq_peer, total, near = gradients(
        "own", *common, k_list[:2], v_list[:2], dq_far, *accs
    )
    total, near = add_far(total, back, near)
    near = down(near, 1)
    dq_peer = to_peer(dq_peer)

    sum_own, sum_peer, sum_side = add_sums(total, near)
    dq_far = to_peer(dq_side[TILE:])
    sum_peer = to_peer(sum_peer)
    sum_side = to_side(sum_side)
    sum_far = to_peer(sum_side[TILE:])
    return (
        place_queries(me, dq_own, dq_side, dq_peer, dq_far),
        *place_keys(me, sum_own, sum_side, sum_peer, sum_far),
    )


def solution(mesh):
    parts, tok = mesh.shape["parts"], mesh.shape["tok"]
    quads = Mesh(
        mesh.devices.reshape(parts, tok // QUAD, 2, 2), ("parts", "level", "side", "core")
    )
    rows = P(("parts", "level", "side", "core"), None)
    return jax.shard_map(
        functools.partial(per_device, tok // QUAD),
        mesh=quads,
        in_specs=(rows, rows, rows, rows, rows, P("parts", None)),
        out_specs=(rows, rows, rows),
        check_vma=False,
    )
```

```python
import functools
import math

import jax
import jax.numpy as jnp
from jax import lax
from jax.experimental import pallas as pl
from jax.experimental.pallas import tpu as pltpu
from jax.sharding import Mesh
from jax.sharding import PartitionSpec as P

QH = 32
KVH = 4
HD = 128
TILE = 128
GROUP = QH // KVH
ROWS = GROUP * TILE
PAIR = 2 * TILE
QUAD = 4
LEVEL = QUAD * TILE
SCALE = HD ** (-0.5)
SCALE2 = SCALE / math.log(2.0)
MASKED = -1e30
NT_DIMS = (((1,), (1,)), ((), ()))
PARAMS = pltpu.CompilerParams(vmem_limit_bytes=28 * 1024 * 1024)
SMALL_PARAMS = pltpu.CompilerParams(vmem_limit_bytes=16 * 1024 * 1024)


def delta_kernel(out_ref, grad_ref, after_ref, delta_ref):
    for head in range(QH):
        cols = slice(head * HD, (head + 1) * HD)
        product = out_ref[:, cols].astype(jnp.float32) * grad_ref[:, cols].astype(jnp.float32)
        delta_ref[head : head + 1, :] = jnp.sum(product.T, axis=0, keepdims=True)


def row_deltas(outputs, out_grad, after):
    return pl.pallas_call(
        delta_kernel,
        in_specs=[pl.BlockSpec(memory_space=pltpu.VMEM)] * 2 + [pl.BlockSpec(memory_space=pl.ANY)],
        out_shape=jax.ShapeDtypeStruct((QH, TILE), jnp.float32),
        compiler_params=SMALL_PARAMS,
        name="row_deltas",
    )(outputs, out_grad, after)


def list_items(items, anc_ref, me, tiles, depth, part):
    tile_of, first_of, second_of, flags_of = items
    cut = ((me >> 2) - 1) * QUAD
    lowest = 2 if part == "far" else 0
    count = jnp.int32(0)
    for place, u in enumerate(tiles):
        tile = me ^ u
        near, live = jnp.int32(1), jnp.int32(1)
        for slot in range(depth):
            entry = anc_ref[tile, slot]
            live += (entry >= 0).astype(jnp.int32)
            near += ((entry >= 0) & (entry >= cut)).astype(jnp.int32)
        start = near if part == "far" else jnp.int32(0)
        stop = near if part == "near" else live
        chunks = (stop - start + 1) // 2

        def slot_of(entry, tile=tile):
            seen = jnp.where(entry == 0, tile, anc_ref[tile, jnp.clip(entry - 1, 0, depth - 1)])
            return ((me >> 2) - (seen >> 2) - lowest) * QUAD + ((seen ^ me) & (QUAD - 1))

        def note(chunk, carry, place=place, start=start, stop=stop, count=count, slot_of=slot_of):
            entry = start + 2 * chunk
            good = entry + 1 < stop
            first = slot_of(entry)
            tile_of[count + chunk] = place
            first_of[count + chunk] = first
            second_of[count + chunk] = jnp.where(good, slot_of(entry + 1), first)
            flags_of[count + chunk] = 1 + 2 * good.astype(jnp.int32) + 4 * (entry == 0).astype(jnp.int32)
            return carry

        lax.fori_loop(0, chunks, note, 0)
        count += chunks
    for extra in range(2):
        tile_of[count + extra] = 0
        first_of[count + extra] = 0
        second_of[count + extra] = 0
        flags_of[count + extra] = 0
    return count


def item_scratch(tiles, depth):
    return [pltpu.SMEM((tiles * ((depth + 2) // 2) + 2,), jnp.int32)] * 4


def slot_rows(slot):
    return pl.ds(pl.multiple_of(slot * TILE, TILE), TILE)


def two_tiles(ref, first, second):
    return jnp.concatenate([ref[slot_rows(first), :], ref[slot_rows(second), :]], axis=0)


def heads_below(ref, u, first, count):
    return jnp.concatenate(
        [ref[u, :, head * HD : (head + 1) * HD] for head in range(first, first + count)], axis=0
    )


def visible_mask(flags):
    key_pos = lax.broadcasted_iota(jnp.int32, (TILE, PAIR), 0)
    query_pos = lax.broadcasted_iota(jnp.int32, (TILE, PAIR), 1) & (TILE - 1)
    return key_pos - query_pos <= jnp.where((flags & 4) != 0, 0, TILE)


def stats_kernel(depth, tiles, steps, me_ref, anc_ref, *rest):
    if tiles[0] == 0:
        (q_own, q_peer), rest = rest[:2], rest[2:]
    else:
        q_side, rest = rest[0], rest[1:]
    k_refs = rest[:steps]
    lse_ref, q_all, k_all, item_max, item_sum, *items = rest[steps:]
    me = me_ref[0]
    if tiles[0] == 0:
        q_all[0] = q_own[...]
        q_all[1] = q_peer[...]
    else:
        q_all[0] = q_side[:TILE, :]
        q_all[1] = q_side[TILE:, :]
    for shift, k_ref in enumerate(k_refs):
        k_all[shift * LEVEL : (shift + 1) * LEVEL, :] = k_ref[...]
    count = list_items(items, anc_ref, me, tiles, depth, "all")
    tile_of, first_of, second_of, flags_of = items

    def one_item(index):
        u, flags = tile_of[index], flags_of[index]
        good = (flags & 2) != 0
        key_block = two_tiles(k_all, first_of[index], second_of[index])
        mask = visible_mask(flags)
        for pair in range(GROUP // 2):
            rows = slice(pair * PAIR, (pair + 1) * PAIR)
            raw = lax.dot_general(
                key_block,
                heads_below(q_all, u, 2 * pair, 2),
                NT_DIMS,
                preferred_element_type=jnp.float32,
            )
            top, low = jnp.where(mask, raw[:TILE], MASKED), raw[TILE:]
            low_max = jnp.max(low, axis=0, keepdims=True)
            new_max = jnp.maximum(
                jnp.max(top, axis=0, keepdims=True), jnp.where(good, low_max, MASKED)
            )
            low_base = jnp.where(good, new_max, -MASKED)
            item_max[index, :, rows] = new_max
            item_sum[index, :, rows] = jnp.sum(
                jnp.exp2((top - new_max) * SCALE2), axis=0, keepdims=True
            ) + jnp.sum(jnp.exp2((low - low_base) * SCALE2), axis=0, keepdims=True)

    def step(index, carry):
        one_item(2 * index)
        one_item(2 * index + 1)
        return carry

    lax.fori_loop(0, (count + 1) // 2, step, 0)

    lse_ref[...] = jnp.full_like(lse_ref, MASKED)

    def combine(index, carry):
        u = tile_of[index]
        old = lse_ref[u]
        new = item_max[index] * SCALE2 + jnp.log2(item_sum[index])
        top = jnp.maximum(old, new)
        lse_ref[u] = top + jnp.log2(jnp.exp2(old - top) + jnp.exp2(new - top))
        return carry

    lax.fori_loop(0, count, combine, 0)


def grads_kernel(depth, stage, steps, me_ref, anc_ref, q_own, q_peer, q_side, g_own, g_peer, g_side, d_own, d_peer, d_side, lse_own, lse_side, *rest):
    kv_refs, rest = rest[: 2 * steps], rest[2 * steps :]
    if stage != "far":
        dq_in, rest = rest[0], rest[1:]
    if stage == "own":
        dk_in, dv_in, rest = rest[0], rest[1], rest[2:]
    tiles = {"far": (0, 1, 2, 3), "side": (2, 3), "own": (0, 1)}[stage]
    if stage == "far":
        dq_acc, partial_refs, rest = rest[0], rest[1 : 1 + steps], rest[1 + steps :]
    elif stage == "side":
        dq_side, dk_acc, dv_acc, rest = rest[0], rest[1], rest[2], rest[3:]
    else:
        dq_own, dq_peer, partial_refs, rest = rest[0], rest[1], rest[2 : 2 + steps], rest[2 + steps :]
    items, rest = rest[:4], rest[4:]
    q_all, g_all, delta, lse_all, k_all, v_all = rest[:6]
    buffers, rest = ((rest[6], rest[7]), (rest[8], rest[9])), rest[10:]
    if stage != "side":
        dk_acc, dv_acc, rest = rest[0], rest[1], rest[2:]
    if stage != "far":
        dq_acc = rest[0]
    me = me_ref[0]
    for place, u in enumerate(tiles):
        if u < 2:
            q_all[place] = (q_own, q_peer)[u][...]
            g_all[place] = (g_own, g_peer)[u][...]
        else:
            rows = slice((u - 2) * TILE, (u - 1) * TILE)
            q_all[place] = q_side[rows, :]
            g_all[place] = g_side[rows, :]
        for head in range(GROUP):
            cols = slice(head * TILE, (head + 1) * TILE)
            d_ref, row = ((d_own, 0), (d_peer, 0), (d_side, 0), (d_side, GROUP))[u]
            delta[place, :, cols] = d_ref[row + head : row + head + 1, :]
        lse_all[place] = (lse_own, lse_side)[u // 2][u % 2]
    for shift in range(steps):
        k_all[shift * LEVEL : (shift + 1) * LEVEL, :] = kv_refs[shift][...]
        v_all[shift * LEVEL : (shift + 1) * LEVEL, :] = kv_refs[steps + shift][...]
    if stage == "own":
        dk_acc[...] = dk_in[...]
        dv_acc[...] = dv_in[...]
    else:
        dk_acc[...] = jnp.zeros_like(dk_acc)
        dv_acc[...] = jnp.zeros_like(dv_acc)
    if stage == "far":
        dq_acc[...] = jnp.zeros_like(dq_acc)
    else:
        dq_acc[...] = dq_in[...]
    for buffer in buffers[1]:
        buffer[...] = jnp.zeros_like(buffer)
    count = list_items(items, anc_ref, me, tiles, depth, "far" if stage == "far" else "near")
    tile_of, first_of, second_of, flags_of = items

    def scores_part(index, low_ref, score_ref):
        place, flags = tile_of[index], flags_of[index]
        first, second = first_of[index], second_of[index]
        key_block = two_tiles(k_all, first, second)
        value_block = two_tiles(v_all, first, second)
        for pair in range(GROUP // 2):
            rows = slice(pair * PAIR, (pair + 1) * PAIR)
            raw = lax.dot_general(
                key_block,
                heads_below(q_all, place, 2 * pair, 2),
                NT_DIMS,
                preferred_element_type=jnp.float32,
            )
            grad_probs = lax.dot_general(
                value_block,
                heads_below(g_all, place, 2 * pair, 2),
                NT_DIMS,
                preferred_element_type=jnp.float32,
            )
            lse = lse_all[place, :, rows]
            away = delta[place, :, rows]
            for part in range(2):
                half = slice(part * TILE, (part + 1) * TILE)
                base = jnp.where((flags & (1 + part)) != 0, lse, -MASKED)
                attn = jnp.exp2(raw[half] * SCALE2 - base)
                if stage != "far" and part == 0:
                    attn = jnp.where(visible_mask(flags), attn, 0.0)
                low_ref[half, rows] = attn.astype(jnp.bfloat16)
                score_ref[half, rows] = (attn * (grad_probs[half] - away)).astype(jnp.bfloat16)

    def grads_part(index, low_ref, score_ref):
        index = jnp.maximum(index, 0)
        place, first, second = tile_of[index], first_of[index], second_of[index]
        dv = jnp.dot(
            low_ref[...], heads_below(g_all, place, 0, GROUP), preferred_element_type=jnp.float32
        )
        dk = jnp.dot(
            score_ref[...], heads_below(q_all, place, 0, GROUP), preferred_element_type=jnp.float32
        )
        dq_acc[place] += jnp.dot(
            two_tiles(k_all, first, second).T, score_ref[...], preferred_element_type=jnp.float32
        )
        dk_acc[slot_rows(first), :] += dk[:TILE]
        dk_acc[slot_rows(second), :] += dk[TILE:]
        dv_acc[slot_rows(first), :] += dv[:TILE]
        dv_acc[slot_rows(second), :] += dv[TILE:]

    def step(index, carry):
        scores_part(2 * index, *buffers[0])
        grads_part(2 * index - 1, *buffers[1])
        scores_part(2 * index + 1, *buffers[1])
        grads_part(2 * index, *buffers[0])
        return carry

    lax.fori_loop(0, jnp.where(count > 0, (count + 2) // 2, 0), step, 0)

    if stage != "far":
        for place in range(2):
            for head in range(GROUP):
                cols = slice(head * HD, (head + 1) * HD)
                turned = (dq_acc[place, :, cols] * SCALE).T.astype(jnp.bfloat16)
                if stage == "side":
                    dq_side[place * TILE : (place + 1) * TILE, cols] = turned
                else:
                    (dq_own, dq_peer)[place][:, cols] = turned
    if stage != "side":
        for shift, out_ref in enumerate(partial_refs):
            rows = slice(shift * LEVEL, (shift + 1) * LEVEL)
            out_ref[:, :HD] = dk_acc[rows, :].astype(out_ref.dtype)
            out_ref[:, HD:] = dv_acc[rows, :].astype(out_ref.dtype)


def work(ancestors, products):
    pairs = QUAD * (ancestors.shape[1] + 1)
    return pl.CostEstimate(
        flops=2 * products * pairs * GROUP * TILE * TILE * 2 * HD,
        transcendentals=pairs * GROUP * TILE * TILE,
        bytes_accessed=16 * 1024 * 1024,
    )


def fixed(shape):
    return pl.BlockSpec(shape, lambda i, *_: (0,) * len(shape))


def own_head(me_ref):
    return ((me_ref[0] & 1) << 1) | ((me_ref[0] >> 1) & 1)


WIDE = pl.BlockSpec((TILE, ROWS), lambda i, me_ref, anc_ref: (0, own_head(me_ref)))
SMALL = pl.BlockSpec((GROUP, TILE), lambda i, me_ref, anc_ref: (own_head(me_ref), 0))
SIDE = fixed((PAIR, ROWS))
LSE = fixed((2, 1, ROWS))
KEYS = fixed((LEVEL, HD))
SUMS = fixed((LEVEL, 2 * HD))
DQ = fixed((QUAD, HD, ROWS))
WIDE_OUT = fixed((TILE, ROWS))


def statistics(tiles, me, ancestors, queries, k_list):
    steps = len(k_list)
    items = item_scratch(2, ancestors.shape[1])
    count = items[0].shape[0]
    return pl.pallas_call(
        functools.partial(stats_kernel, ancestors.shape[1], tiles, steps),
        grid_spec=pltpu.PrefetchScalarGridSpec(
            num_scalar_prefetch=2,
            grid=(1,),
            in_specs=([WIDE, WIDE] if tiles[0] == 0 else [SIDE]) + [KEYS] * steps,
            out_specs=LSE,
            scratch_shapes=[
                pltpu.VMEM((2, TILE, ROWS), jnp.bfloat16),
                pltpu.VMEM((steps * LEVEL, HD), jnp.bfloat16),
                pltpu.VMEM((count, 1, ROWS), jnp.float32),
                pltpu.VMEM((count, 1, ROWS), jnp.float32),
                *items,
            ],
        ),
        out_shape=jax.ShapeDtypeStruct((2, 1, ROWS), jnp.float32),
        compiler_params=PARAMS,
        cost_estimate=work(ancestors, 1),
        name="own_stats" if tiles[0] == 0 else "side_stats",
    )(me, ancestors, *queries, *k_list)


def gradients(stage, me, ancestors, q_set, g_set, d_set, lse, k_list, v_list, *carried):
    steps = len(k_list)
    tiles = QUAD if stage == "far" else 2
    acc = (steps * LEVEL, HD)
    wide = jax.ShapeDtypeStruct((TILE, ROWS), jnp.bfloat16)
    sums = [jax.ShapeDtypeStruct((LEVEL, 2 * HD), jnp.bfloat16)] * steps
    accs = [jax.ShapeDtypeStruct(acc, jnp.float32)] * 2
    dq_half = pl.BlockSpec((2, HD, ROWS), lambda i, *_: (1 if stage == "side" else 0, 0, 0))
    extra_specs = [dq_half, fixed(acc), fixed(acc)][: len(carried)]
    if stage == "far":
        out_specs = [DQ] + [SUMS] * steps
        out_shape = [jax.ShapeDtypeStruct((QUAD, HD, ROWS), jnp.float32)] + sums
    elif stage == "side":
        out_specs = [SIDE, fixed(acc), fixed(acc)]
        out_shape = [jax.ShapeDtypeStruct((PAIR, ROWS), jnp.bfloat16)] + accs
    else:
        sums[0] = jax.ShapeDtypeStruct((LEVEL, 2 * HD), jnp.float32)
        out_specs = [WIDE_OUT, WIDE_OUT] + [SUMS] * steps
        out_shape = [wide, wide] + sums
    scratch = item_scratch(tiles, ancestors.shape[1]) + [
        pltpu.VMEM((tiles, TILE, ROWS), jnp.bfloat16),
        pltpu.VMEM((tiles, TILE, ROWS), jnp.bfloat16),
        pltpu.VMEM((tiles, 1, ROWS), jnp.float32),
        pltpu.VMEM((tiles, 1, ROWS), jnp.float32),
        pltpu.VMEM(acc, jnp.bfloat16),
        pltpu.VMEM(acc, jnp.bfloat16),
    ]
    scratch += [pltpu.VMEM((PAIR, ROWS), jnp.bfloat16)] * 4
    if stage != "side":
        scratch += [pltpu.VMEM(acc, jnp.float32)] * 2
    if stage != "far":
        scratch.append(pltpu.VMEM((tiles, HD, ROWS), jnp.float32))
    return pl.pallas_call(
        functools.partial(grads_kernel, ancestors.shape[1], stage, steps),
        grid_spec=pltpu.PrefetchScalarGridSpec(
            num_scalar_prefetch=2,
            grid=(1,),
            in_specs=[WIDE, WIDE, SIDE, WIDE, WIDE, SIDE, SMALL, SMALL, fixed((2 * GROUP, TILE)), LSE, LSE]
            + [KEYS] * (2 * steps)
            + extra_specs,
            out_specs=out_specs,
            scratch_shapes=scratch,
        ),
        out_shape=out_shape,
        compiler_params=PARAMS,
        cost_estimate=work(ancestors, 5),
        name=stage + "_grads",
    )(me, ancestors, *q_set, *g_set, *d_set, *lse, *k_list, *v_list, *carried)


def side_head(me_ref):
    return own_head(me_ref) ^ 1


def head_columns(head, width):
    return pl.ds(pl.multiple_of(head * width, width), width)


SCALARS = pl.BlockSpec(memory_space=pltpu.SMEM)
HERE = pl.BlockSpec(memory_space=pltpu.VMEM)


def pack_own_kernel(me_ref, k_own, v_own, mine_ref, send_ref):
    for head, out_ref in ((own_head(me_ref), mine_ref), (side_head(me_ref), send_ref)):
        at = head_columns(head, HD)
        out_ref[:TILE, :HD] = k_own[:, at]
        out_ref[:TILE, HD:] = v_own[:, at]


def pack_peer_kernel(me_ref, k_peer, v_peer, mine_in, send_in, mine_ref, send_ref):
    for head, in_ref, out_ref in (
        (own_head(me_ref), mine_in, mine_ref),
        (side_head(me_ref), send_in, send_ref),
    ):
        at = head_columns(head, HD)
        out_ref[:TILE, :] = in_ref[:TILE, :]
        out_ref[TILE:, :HD] = k_peer[:, at]
        out_ref[TILE:, HD:] = v_peer[:, at]


def pack_keys(name, kernel, *arrays):
    return pl.pallas_call(
        kernel,
        in_specs=[SCALARS] + [HERE] * (len(arrays) - 1),
        out_specs=[HERE] * 2,
        out_shape=[jax.ShapeDtypeStruct((PAIR, 2 * HD), jnp.bfloat16)] * 2,
        compiler_params=SMALL_PARAMS,
        name=name,
    )(*arrays)


def pack_queries_kernel(me_ref, own, peer, send_ref):
    at = head_columns(side_head(me_ref), ROWS)
    send_ref[:TILE, :] = own[:, at]
    send_ref[TILE:, :] = peer[:, at]


def pack_queries(me, own, peer):
    return pl.pallas_call(
        pack_queries_kernel,
        in_specs=[SCALARS, HERE, HERE],
        out_specs=HERE,
        out_shape=jax.ShapeDtypeStruct((PAIR, ROWS), jnp.bfloat16),
        compiler_params=SMALL_PARAMS,
        name="pack_queries",
    )(me, own, peer)


def join_keys_kernel(chip_ref, side_ref, k_ref, v_ref):
    for place, ref in enumerate((chip_ref, side_ref)):
        rows = slice(place * PAIR, (place + 1) * PAIR)
        k_ref[rows, :] = ref[:, :HD]
        v_ref[rows, :] = ref[:, HD:]


def join_keys(chip, side):
    return pl.pallas_call(
        join_keys_kernel,
        in_specs=[HERE] * 2,
        out_specs=[HERE] * 2,
        out_shape=[jax.ShapeDtypeStruct((LEVEL, HD), jnp.bfloat16)] * 2,
        compiler_params=SMALL_PARAMS,
        name="join_keys",
    )(chip, side)


def pack_deltas_kernel(me_ref, d_own, d_peer, send_ref):
    send_ref[:GROUP, :] = d_own[...]
    send_ref[GROUP:, :] = d_peer[...]


def pack_deltas(me, deltas, d_peer):
    away = pl.BlockSpec((GROUP, TILE), lambda i, me_ref: (side_head(me_ref), 0))
    return pl.pallas_call(
        pack_deltas_kernel,
        grid_spec=pltpu.PrefetchScalarGridSpec(
            num_scalar_prefetch=1,
            grid=(1,),
            in_specs=[away] * 2,
            out_specs=fixed((2 * GROUP, TILE)),
        ),
        out_shape=jax.ShapeDtypeStruct((2 * GROUP, TILE), jnp.float32),
        compiler_params=SMALL_PARAMS,
        name="pack_deltas",
    )(me, deltas, d_peer)


def add_far_kernel(total_ref, *refs):
    parts, out_ref = refs[:-3], refs[-2]
    total = total_ref[...]
    for part in parts:
        total += part[...].astype(jnp.float32)
    out_ref[...] = total


def add_far(acc, parts, passing):
    here = pl.BlockSpec(memory_space=pltpu.VMEM)
    anywhere = pl.BlockSpec(memory_space=pl.ANY)
    return pl.pallas_call(
        add_far_kernel,
        in_specs=[here] * (1 + len(parts)) + [anywhere],
        out_specs=[here, anywhere],
        out_shape=[
            jax.ShapeDtypeStruct(acc.shape, jnp.float32),
            jax.ShapeDtypeStruct(passing.shape, passing.dtype),
        ],
        input_output_aliases={1 + len(parts): 1},
        compiler_params=SMALL_PARAMS,
        name="add_far",
    )(acc, *parts, passing)


def add_sums_kernel(total_ref, near_ref, own_ref, peer_ref, send_ref):
    total = total_ref[...] + near_ref[...].astype(jnp.float32)
    scaled = jnp.concatenate([total[:, :HD] * SCALE, total[:, HD:]], axis=1).astype(jnp.bfloat16)
    own_ref[...] = scaled[:TILE]
    peer_ref[...] = scaled[TILE:PAIR]
    send_ref[...] = scaled[PAIR:]


def add_sums(total, near):
    here = pl.BlockSpec(memory_space=pltpu.VMEM)
    return pl.pallas_call(
        add_sums_kernel,
        in_specs=[here] * 2,
        out_specs=[here] * 3,
        out_shape=[
            jax.ShapeDtypeStruct((TILE, 2 * HD), jnp.bfloat16),
            jax.ShapeDtypeStruct((TILE, 2 * HD), jnp.bfloat16),
            jax.ShapeDtypeStruct((PAIR, 2 * HD), jnp.bfloat16),
        ],
        compiler_params=SMALL_PARAMS,
        name="add_sums",
    )(total, near)


def placed(me_ref, width):
    head = own_head(me_ref)
    return [head_columns(head ^ flip, width) for flip in range(4)]


def place_queries_kernel(me_ref, own, side, peer, far, dq_ref):
    at = placed(me_ref, ROWS)
    dq_ref[:, at[0]] = own[...]
    dq_ref[:, at[1]] = side[:TILE, :]
    dq_ref[:, at[2]] = peer[...]
    dq_ref[:, at[3]] = far[...]


def place_queries(me, *pieces):
    return pl.pallas_call(
        place_queries_kernel,
        in_specs=[SCALARS] + [HERE] * 4,
        out_specs=HERE,
        out_shape=jax.ShapeDtypeStruct((TILE, QH * HD), jnp.bfloat16),
        compiler_params=SMALL_PARAMS,
        name="place_queries",
    )(me, *pieces)


def place_keys_kernel(me_ref, own, side, peer, far, dk_ref, dv_ref):
    at = placed(me_ref, HD)
    for spot, part in zip(at, (own[...], side[:TILE, :], peer[...], far[...])):
        dk_ref[:, spot] = part[:, :HD]
        dv_ref[:, spot] = part[:, HD:]


def place_keys(me, *pieces):
    return pl.pallas_call(
        place_keys_kernel,
        in_specs=[SCALARS] + [HERE] * 4,
        out_specs=[HERE] * 2,
        out_shape=[jax.ShapeDtypeStruct((TILE, KVH * HD), jnp.bfloat16)] * 2,
        compiler_params=SMALL_PARAMS,
        name="place_keys",
    )(me, *pieces)


def per_device(steps, queries, keys, values, outputs, out_grad, ancestors):
    level, side, core = (lax.axis_index(name) for name in ("level", "side", "core"))
    me = (QUAD * level + 2 * side + core).reshape(1).astype(jnp.int32)

    def to_peer(x):
        return lax.ppermute(x, "core", [(0, 1), (1, 0)])

    def to_side(x):
        return lax.ppermute(x, "side", [(0, 1), (1, 0)])

    def after(x, done):
        return lax.optimization_barrier((x, done))[0]

    def up(x, shift):
        return lax.ppermute(x, "level", [(z, z + shift) for z in range(steps - shift)])

    def up_chain(x):
        arrivals = [x]
        for shift in range(1, steps):
            pairs = [(z, z + 1) for z in range(shift - 1, steps - 1)]
            arrivals.append(lax.ppermute(arrivals[-1], "level", pairs))
        return arrivals

    def down(x, shift):
        return lax.ppermute(x, "level", [(z + shift, z) for z in range(steps - shift)])

    k_peer, v_peer = to_peer(keys), to_peer(values)
    own_parts = pack_keys("pack_own", pack_own_kernel, me, keys, values)
    kv_chip, kv_send = pack_keys("pack_peer", pack_peer_kernel, me, k_peer, v_peer, *own_parts)
    kv_side = to_side(kv_send)
    q_peer = to_peer(after(queries, own_parts))
    q_send = pack_queries(me, queries, q_peer)
    q_set = (queries, q_peer, to_side(q_send))
    k_level, v_level = join_keys(kv_chip, after(kv_side, q_send))
    k_list = up_chain(k_level)
    g_peer = to_peer(after(out_grad, k_list[1]))
    v_level = after(v_level, k_list[2])
    v_list = [v_level] + [up(v_level, shift) for shift in range(1, steps)]
    g_set = (out_grad, g_peer, to_side(after(pack_queries(me, out_grad, g_peer), k_list[1])))
    deltas = row_deltas(outputs, out_grad, k_list[2])
    d_peer = to_peer(deltas)
    d_set = (deltas, d_peer, to_side(pack_deltas(me, deltas, d_peer)))

    lse = [statistics((0, 1), me, ancestors, q_set[:2], k_list)]
    lse.append(statistics((2, 3), me, ancestors, q_set[2:], after(k_list, lse[0])))
    common = (me, ancestors, q_set, g_set, d_set, lse)
    dq_far, *far = gradients("far", *common, k_list[2:], v_list[2:])
    back = [down(far[shift - 2], shift) for shift in range(2, steps)]
    dq_side, *accs = gradients("side", *common, k_list[:2], v_list[:2], dq_far)
    dq_side = to_side(dq_side)
    dq_own, dq_peer, total, near = gradients(
        "own", *common, k_list[:2], v_list[:2], dq_far, *accs
    )
    total, near = add_far(total, back, near)
    near = down(near, 1)

    sum_own, sum_peer, sum_side = add_sums(total, near)
    dq_peer = to_peer(after(dq_peer, total))
    sum_peer = to_peer(sum_peer)
    sum_side = to_side(sum_side)
    sum_far = to_peer(sum_side[TILE:])
    dq_side = after(dq_side, sum_side)
    dq_far = to_peer(dq_side[TILE:])
    return (
        place_queries(me, dq_own, dq_side, dq_peer, dq_far),
        *place_keys(me, sum_own, sum_side, sum_peer, sum_far),
    )


def solution(mesh):
    parts, tok = mesh.shape["parts"], mesh.shape["tok"]
    quads = Mesh(
        mesh.devices.reshape(parts, tok // QUAD, 2, 2), ("parts", "level", "side", "core")
    )
    rows = P(("parts", "level", "side", "core"), None)
    return jax.shard_map(
        functools.partial(per_device, tok // QUAD),
        mesh=quads,
        in_specs=(rows, rows, rows, rows, rows, P("parts", None)),
        out_specs=(rows, rows, rows),
        check_vma=False,
    )
```

```python
import functools
import math

import jax
import jax.numpy as jnp
from jax import lax
from jax.experimental import pallas as pl
from jax.experimental.pallas import tpu as pltpu
from jax.sharding import Mesh
from jax.sharding import PartitionSpec as P

QH = 32
KVH = 4
HD = 128
TILE = 128
GROUP = QH // KVH
ROWS = GROUP * TILE
PAIR = 2 * TILE
QUAD = 4
LEVEL = QUAD * TILE
SCALE = HD ** (-0.5)
SCALE2 = SCALE / math.log(2.0)
MASKED = -1e30
SCALARS = pl.BlockSpec(memory_space=pltpu.SMEM)
HERE = pl.BlockSpec(memory_space=pltpu.VMEM)
NT_DIMS = (((1,), (1,)), ((), ()))
PARAMS = pltpu.CompilerParams(vmem_limit_bytes=28 * 1024 * 1024)
SMALL_PARAMS = pltpu.CompilerParams(vmem_limit_bytes=16 * 1024 * 1024)


def delta_kernel(me_ref, out_ref, grad_ref, after_ref, *delta_refs):
    for flip, delta_ref in enumerate(delta_refs):
        base = (own_head(me_ref) ^ flip) * ROWS
        for head in range(GROUP):
            cols = pl.ds(pl.multiple_of(base + head * HD, HD), HD)
            product = out_ref[:, cols].astype(jnp.float32) * grad_ref[:, cols].astype(jnp.float32)
            delta_ref[head : head + 1, :] = jnp.sum(product.T, axis=0, keepdims=True)


def row_deltas(me, outputs, out_grad, after):
    return pl.pallas_call(
        delta_kernel,
        in_specs=[SCALARS, HERE, HERE, pl.BlockSpec(memory_space=pl.ANY)],
        out_specs=[HERE] * QUAD,
        out_shape=[jax.ShapeDtypeStruct((GROUP, TILE), jnp.float32)] * QUAD,
        compiler_params=SMALL_PARAMS,
        name="row_deltas",
    )(me, outputs, out_grad, after)


def list_items(items, anc_ref, me, tiles, depth, part):
    tile_of, first_of, second_of, flags_of = items
    cut = ((me >> 2) - 1) * QUAD
    lowest = 2 if part == "far" else 0
    count = jnp.int32(0)
    for place, u in enumerate(tiles):
        tile = me ^ u
        near, live = jnp.int32(1), jnp.int32(1)
        for slot in range(depth):
            entry = anc_ref[tile, slot]
            live += (entry >= 0).astype(jnp.int32)
            near += ((entry >= 0) & (entry >= cut)).astype(jnp.int32)
        start = near if part == "far" else jnp.int32(0)
        stop = near if part == "near" else live
        chunks = (stop - start + 1) // 2

        def slot_of(entry, tile=tile):
            seen = jnp.where(entry == 0, tile, anc_ref[tile, jnp.clip(entry - 1, 0, depth - 1)])
            return ((me >> 2) - (seen >> 2) - lowest) * QUAD + ((seen ^ me) & (QUAD - 1))

        def note(chunk, carry, place=place, start=start, stop=stop, count=count, slot_of=slot_of):
            entry = start + 2 * chunk
            good = entry + 1 < stop
            first = slot_of(entry)
            tile_of[count + chunk] = place
            first_of[count + chunk] = first
            second_of[count + chunk] = jnp.where(good, slot_of(entry + 1), first)
            flags_of[count + chunk] = 1 + 2 * good.astype(jnp.int32) + 4 * (entry == 0).astype(jnp.int32)
            return carry

        lax.fori_loop(0, chunks, note, 0)
        count += chunks
    for extra in range(2):
        tile_of[count + extra] = 0
        first_of[count + extra] = 0
        second_of[count + extra] = 0
        flags_of[count + extra] = 0
    return count


def item_scratch(tiles, depth):
    return [pltpu.SMEM((tiles * ((depth + 2) // 2) + 2,), jnp.int32)] * 4


def slot_rows(slot):
    return pl.ds(pl.multiple_of(slot * TILE, TILE), TILE)


def two_tiles(ref, first, second):
    return jnp.concatenate([ref[slot_rows(first), :], ref[slot_rows(second), :]], axis=0)


def heads_below(ref, u, first, count):
    return jnp.concatenate(
        [ref[u, :, head * HD : (head + 1) * HD] for head in range(first, first + count)], axis=0
    )


def visible_mask(flags):
    key_pos = lax.broadcasted_iota(jnp.int32, (TILE, PAIR), 0)
    query_pos = lax.broadcasted_iota(jnp.int32, (TILE, PAIR), 1) & (TILE - 1)
    return key_pos - query_pos <= jnp.where((flags & 4) != 0, 0, TILE)


def stats_kernel(depth, steps, me_ref, anc_ref, *rest):
    q_refs, rest = rest[:QUAD], rest[QUAD:]
    k_refs = rest[:steps]
    lse_ref, q_all, k_all, item_max, item_sum, *items = rest[steps:]
    me = me_ref[0]
    for u, q_ref in enumerate(q_refs):
        q_all[u] = q_ref[...]
    for shift, k_ref in enumerate(k_refs):
        k_all[shift * LEVEL : (shift + 1) * LEVEL, :] = k_ref[...]
    count = list_items(items, anc_ref, me, range(QUAD), depth, "all")
    tile_of, first_of, second_of, flags_of = items

    def one_item(index):
        u, flags = tile_of[index], flags_of[index]
        good = (flags & 2) != 0
        key_block = two_tiles(k_all, first_of[index], second_of[index])
        mask = visible_mask(flags)
        for pair in range(GROUP // 2):
            rows = slice(pair * PAIR, (pair + 1) * PAIR)
            raw = lax.dot_general(
                key_block,
                heads_below(q_all, u, 2 * pair, 2),
                NT_DIMS,
                preferred_element_type=jnp.float32,
            )
            top, low = jnp.where(mask, raw[:TILE], MASKED), raw[TILE:]
            low_max = jnp.max(low, axis=0, keepdims=True)
            new_max = jnp.maximum(
                jnp.max(top, axis=0, keepdims=True), jnp.where(good, low_max, MASKED)
            )
            low_base = jnp.where(good, new_max, -MASKED)
            item_max[index, :, rows] = new_max
            item_sum[index, :, rows] = jnp.sum(
                jnp.exp2((top - new_max) * SCALE2), axis=0, keepdims=True
            ) + jnp.sum(jnp.exp2((low - low_base) * SCALE2), axis=0, keepdims=True)

    def step(index, carry):
        one_item(2 * index)
        one_item(2 * index + 1)
        return carry

    lax.fori_loop(0, (count + 1) // 2, step, 0)

    lse_ref[...] = jnp.full_like(lse_ref, MASKED)

    def combine(index, carry):
        u = tile_of[index]
        old = lse_ref[u]
        new = item_max[index] * SCALE2 + jnp.log2(item_sum[index])
        top = jnp.maximum(old, new)
        lse_ref[u] = top + jnp.log2(jnp.exp2(old - top) + jnp.exp2(new - top))
        return carry

    lax.fori_loop(0, count, combine, 0)


def grads_kernel(depth, stage, steps, me_ref, anc_ref, *rest):
    q_refs, g_refs, d_refs, rest = rest[:4], rest[4:8], rest[8:12], rest[12:]
    lse_ref, rest = rest[0], rest[1:]
    kv_refs, rest = rest[: 2 * steps], rest[2 * steps :]
    if stage != "far":
        dq_in, rest = rest[0], rest[1:]
    if stage == "own":
        dk_in, dv_in, rest = rest[0], rest[1], rest[2:]
    tiles = {"far": (0, 1, 2, 3), "side": (2, 3), "own": (0, 1)}[stage]
    if stage == "far":
        dq_acc, partial_refs, rest = rest[0], rest[1 : 1 + steps], rest[1 + steps :]
    elif stage == "side":
        dq_refs = (rest[0].at[:TILE, :], rest[0].at[TILE:, :])
        dk_acc, dv_acc, rest = rest[1], rest[2], rest[3:]
    else:
        dq_refs, partial_refs, rest = rest[:2], rest[2 : 2 + steps], rest[2 + steps :]
    items, rest = rest[:4], rest[4:]
    q_all, g_all, delta, k_all, v_all = rest[:5]
    buffers, rest = ((rest[5], rest[6]), (rest[7], rest[8])), rest[9:]
    if stage != "side":
        dk_acc, dv_acc, rest = rest[0], rest[1], rest[2:]
    if stage != "far":
        dq_acc = rest[0]
    me = me_ref[0]
    for place, u in enumerate(tiles):
        q_all[place] = q_refs[u][...]
        g_all[place] = g_refs[u][...]
        for head in range(GROUP):
            cols = slice(head * TILE, (head + 1) * TILE)
            delta[place, :, cols] = d_refs[u][head : head + 1, :]
    for shift in range(steps):
        k_all[shift * LEVEL : (shift + 1) * LEVEL, :] = kv_refs[shift][...]
        v_all[shift * LEVEL : (shift + 1) * LEVEL, :] = kv_refs[steps + shift][...]
    if stage == "own":
        dk_acc[...] = dk_in[...]
        dv_acc[...] = dv_in[...]
    else:
        dk_acc[...] = jnp.zeros_like(dk_acc)
        dv_acc[...] = jnp.zeros_like(dv_acc)
    if stage == "far":
        dq_acc[...] = jnp.zeros_like(dq_acc)
    else:
        dq_acc[...] = dq_in[...]
    for buffer in buffers[1]:
        buffer[...] = jnp.zeros_like(buffer)
    count = list_items(items, anc_ref, me, tiles, depth, "far" if stage == "far" else "near")
    tile_of, first_of, second_of, flags_of = items

    def scores_part(index, low_ref, score_ref):
        place, flags = tile_of[index], flags_of[index]
        first, second = first_of[index], second_of[index]
        key_block = two_tiles(k_all, first, second)
        value_block = two_tiles(v_all, first, second)
        for pair in range(GROUP // 2):
            rows = slice(pair * PAIR, (pair + 1) * PAIR)
            raw = lax.dot_general(
                key_block,
                heads_below(q_all, place, 2 * pair, 2),
                NT_DIMS,
                preferred_element_type=jnp.float32,
            )
            grad_probs = lax.dot_general(
                value_block,
                heads_below(g_all, place, 2 * pair, 2),
                NT_DIMS,
                preferred_element_type=jnp.float32,
            )
            lse = lse_ref[tiles[0] + place, :, rows]
            away = delta[place, :, rows]
            for part in range(2):
                half = slice(part * TILE, (part + 1) * TILE)
                base = jnp.where((flags & (1 + part)) != 0, lse, -MASKED)
                attn = jnp.exp2(raw[half] * SCALE2 - base)
                if stage != "far" and part == 0:
                    attn = jnp.where(visible_mask(flags), attn, 0.0)
                low_ref[half, rows] = attn.astype(jnp.bfloat16)
                score_ref[half, rows] = (attn * (grad_probs[half] - away)).astype(jnp.bfloat16)

    def grads_part(index, low_ref, score_ref):
        index = jnp.maximum(index, 0)
        place, first, second = tile_of[index], first_of[index], second_of[index]
        dv = jnp.dot(
            low_ref[...], heads_below(g_all, place, 0, GROUP), preferred_element_type=jnp.float32
        )
        dk = jnp.dot(
            score_ref[...], heads_below(q_all, place, 0, GROUP), preferred_element_type=jnp.float32
        )
        dq_acc[place] += jnp.dot(
            two_tiles(k_all, first, second).T, score_ref[...], preferred_element_type=jnp.float32
        )
        dk_acc[slot_rows(first), :] += dk[:TILE]
        dk_acc[slot_rows(second), :] += dk[TILE:]
        dv_acc[slot_rows(first), :] += dv[:TILE]
        dv_acc[slot_rows(second), :] += dv[TILE:]

    def step(index, carry):
        scores_part(2 * index, *buffers[0])
        grads_part(2 * index - 1, *buffers[1])
        scores_part(2 * index + 1, *buffers[1])
        grads_part(2 * index, *buffers[0])
        return carry

    lax.fori_loop(0, jnp.where(count > 0, (count + 2) // 2, 0), step, 0)

    if stage != "far":
        for place in range(2):
            for head in range(GROUP):
                cols = slice(head * HD, (head + 1) * HD)
                dq_refs[place][:, cols] = (dq_acc[place, :, cols] * SCALE).T.astype(jnp.bfloat16)
    if stage != "side":
        for shift, out_ref in enumerate(partial_refs):
            rows = slice(shift * LEVEL, (shift + 1) * LEVEL)
            out_ref[:, :HD] = dk_acc[rows, :].astype(out_ref.dtype)
            out_ref[:, HD:] = dv_acc[rows, :].astype(out_ref.dtype)


def work(ancestors, products):
    pairs = QUAD * (ancestors.shape[1] + 1)
    return pl.CostEstimate(
        flops=2 * products * pairs * GROUP * TILE * TILE * 2 * HD,
        transcendentals=pairs * GROUP * TILE * TILE,
        bytes_accessed=16 * 1024 * 1024,
    )


def fixed(shape):
    return pl.BlockSpec(shape, lambda i, *_: (0,) * len(shape))


def own_head(me_ref):
    return ((me_ref[0] & 1) << 1) | ((me_ref[0] >> 1) & 1)


WIDE = pl.BlockSpec((TILE, ROWS), lambda i, me_ref, anc_ref: (0, own_head(me_ref)))
LSE = fixed((QUAD, 1, ROWS))
KEYS = fixed((LEVEL, HD))
SUMS = fixed((LEVEL, 2 * HD))
DQ = fixed((QUAD, HD, ROWS))
PIECE = fixed((TILE, ROWS))
SIDE = fixed((PAIR, ROWS))


def statistics(me, ancestors, q_set, k_list):
    steps = len(k_list)
    items = item_scratch(QUAD, ancestors.shape[1])
    count = items[0].shape[0]
    return pl.pallas_call(
        functools.partial(stats_kernel, ancestors.shape[1], steps),
        grid_spec=pltpu.PrefetchScalarGridSpec(
            num_scalar_prefetch=2,
            grid=(1,),
            in_specs=[WIDE] + [PIECE] * 3 + [KEYS] * steps,
            out_specs=LSE,
            scratch_shapes=[
                pltpu.VMEM((QUAD, TILE, ROWS), jnp.bfloat16),
                pltpu.VMEM((steps * LEVEL, HD), jnp.bfloat16),
                pltpu.VMEM((count, 1, ROWS), jnp.float32),
                pltpu.VMEM((count, 1, ROWS), jnp.float32),
                *items,
            ],
        ),
        out_shape=jax.ShapeDtypeStruct((QUAD, 1, ROWS), jnp.float32),
        compiler_params=PARAMS,
        cost_estimate=work(ancestors, 1),
        name="statistics",
    )(me, ancestors, *q_set, *k_list)


def gradients(stage, me, ancestors, q_set, g_set, d_set, lse, k_list, v_list, *carried):
    steps = len(k_list)
    tiles = QUAD if stage == "far" else 2
    acc = (steps * LEVEL, HD)
    wide = jax.ShapeDtypeStruct((TILE, ROWS), jnp.bfloat16)
    sums = [jax.ShapeDtypeStruct((LEVEL, 2 * HD), jnp.bfloat16)] * steps
    accs = [jax.ShapeDtypeStruct(acc, jnp.float32)] * 2
    dq_half = pl.BlockSpec((2, HD, ROWS), lambda i, *_: (1 if stage == "side" else 0, 0, 0))
    extra_specs = [dq_half, fixed(acc), fixed(acc)][: len(carried)]
    if stage == "far":
        out_specs = [DQ] + [SUMS] * steps
        out_shape = [jax.ShapeDtypeStruct((QUAD, HD, ROWS), jnp.float32)] + sums
    elif stage == "side":
        out_specs = [SIDE, fixed(acc), fixed(acc)]
        out_shape = [jax.ShapeDtypeStruct((PAIR, ROWS), jnp.bfloat16)] + accs
    else:
        sums[0] = jax.ShapeDtypeStruct((LEVEL, 2 * HD), jnp.float32)
        out_specs = [PIECE, PIECE] + [SUMS] * steps
        out_shape = [wide, wide] + sums
    scratch = item_scratch(tiles, ancestors.shape[1]) + [
        pltpu.VMEM((tiles, TILE, ROWS), jnp.bfloat16),
        pltpu.VMEM((tiles, TILE, ROWS), jnp.bfloat16),
        pltpu.VMEM((tiles, 1, ROWS), jnp.float32),
        pltpu.VMEM(acc, jnp.bfloat16),
        pltpu.VMEM(acc, jnp.bfloat16),
    ]
    scratch += [pltpu.VMEM((PAIR, ROWS), jnp.bfloat16)] * 4
    if stage != "side":
        scratch += [pltpu.VMEM(acc, jnp.float32)] * 2
    if stage != "far":
        scratch.append(pltpu.VMEM((tiles, HD, ROWS), jnp.float32))
    return pl.pallas_call(
        functools.partial(grads_kernel, ancestors.shape[1], stage, steps),
        grid_spec=pltpu.PrefetchScalarGridSpec(
            num_scalar_prefetch=2,
            grid=(1,),
            in_specs=([WIDE] + [PIECE] * 3) * 2 + [fixed((GROUP, TILE))] * 4 + [LSE]
            + [KEYS] * (2 * steps)
            + extra_specs,
            out_specs=out_specs,
            scratch_shapes=scratch,
        ),
        out_shape=out_shape,
        compiler_params=PARAMS,
        cost_estimate=work(ancestors, 5),
        name=stage + "_grads",
    )(me, ancestors, *q_set, *g_set, *d_set, lse, *k_list, *v_list, *carried)


def head_columns(head, width):
    return pl.ds(pl.multiple_of(head * width, width), width)


def pack_keys_kernel(me_ref, keys, values, *out_refs):
    for flip, out_ref in enumerate(out_refs):
        at = head_columns(own_head(me_ref) ^ flip, HD)
        out_ref[:, :HD] = keys[:, at]
        out_ref[:, HD:] = values[:, at]


def pack_keys(me, keys, values):
    return pl.pallas_call(
        pack_keys_kernel,
        in_specs=[SCALARS, HERE, HERE],
        out_specs=[HERE] * QUAD,
        out_shape=[jax.ShapeDtypeStruct((TILE, 2 * HD), jnp.bfloat16)] * QUAD,
        compiler_params=SMALL_PARAMS,
        name="pack_keys",
    )(me, keys, values)


def join_keys_kernel(*refs):
    k_ref, v_ref = refs[-2:]
    for place, ref in enumerate(refs[:-2]):
        rows = slice(place * TILE, (place + 1) * TILE)
        k_ref[rows, :] = ref[:, :HD]
        v_ref[rows, :] = ref[:, HD:]


def join_keys(*pieces):
    return pl.pallas_call(
        join_keys_kernel,
        in_specs=[HERE] * QUAD,
        out_specs=[HERE] * 2,
        out_shape=[jax.ShapeDtypeStruct((LEVEL, HD), jnp.bfloat16)] * 2,
        compiler_params=SMALL_PARAMS,
        name="join_keys",
    )(*pieces)


def pack_queries_kernel(me_ref, whole, *out_refs):
    for flip, out_ref in enumerate(out_refs):
        out_ref[...] = whole[:, head_columns(own_head(me_ref) ^ (flip + 1), ROWS)]


def pack_queries(me, whole):
    return pl.pallas_call(
        pack_queries_kernel,
        in_specs=[SCALARS, HERE],
        out_specs=[HERE] * 3,
        out_shape=[jax.ShapeDtypeStruct((TILE, ROWS), jnp.bfloat16)] * 3,
        compiler_params=SMALL_PARAMS,
        name="pack_queries",
    )(me, whole)


def add_far_kernel(total_ref, *refs):
    parts, out_ref = refs[:-3], refs[-2]
    total = total_ref[...]
    for part in parts:
        total += part[...].astype(jnp.float32)
    out_ref[...] = total


def add_far(acc, parts, passing):
    here = pl.BlockSpec(memory_space=pltpu.VMEM)
    anywhere = pl.BlockSpec(memory_space=pl.ANY)
    return pl.pallas_call(
        add_far_kernel,
        in_specs=[here] * (1 + len(parts)) + [anywhere],
        out_specs=[here, anywhere],
        out_shape=[
            jax.ShapeDtypeStruct(acc.shape, jnp.float32),
            jax.ShapeDtypeStruct(passing.shape, passing.dtype),
        ],
        input_output_aliases={1 + len(parts): 1},
        compiler_params=SMALL_PARAMS,
        name="add_far",
    )(acc, *parts, passing)


def add_sums_kernel(total_ref, near_ref, *out_refs):
    total = total_ref[...] + near_ref[...].astype(jnp.float32)
    scaled = jnp.concatenate([total[:, :HD] * SCALE, total[:, HD:]], axis=1).astype(jnp.bfloat16)
    for place, out_ref in enumerate(out_refs):
        out_ref[...] = scaled[place * TILE : (place + 1) * TILE]


def add_sums(total, near):
    return pl.pallas_call(
        add_sums_kernel,
        in_specs=[HERE] * 2,
        out_specs=[HERE] * QUAD,
        out_shape=[jax.ShapeDtypeStruct((TILE, 2 * HD), jnp.bfloat16)] * QUAD,
        compiler_params=SMALL_PARAMS,
        name="add_sums",
    )(total, near)


FLIPS = (0, 2, 1, 3)


def place_queries_kernel(me_ref, *refs):
    for flip, piece in zip(FLIPS, refs[:-1]):
        refs[-1][:, head_columns(own_head(me_ref) ^ flip, ROWS)] = piece[:TILE, :]


def place_queries(me, *pieces):
    return pl.pallas_call(
        place_queries_kernel,
        in_specs=[SCALARS] + [HERE] * 4,
        out_specs=HERE,
        out_shape=jax.ShapeDtypeStruct((TILE, QH * HD), jnp.bfloat16),
        compiler_params=SMALL_PARAMS,
        name="place_queries",
    )(me, *pieces)


def place_keys_kernel(me_ref, *refs):
    dk_ref, dv_ref = refs[-2:]
    for flip, piece in zip(FLIPS, refs[:-2]):
        at = head_columns(own_head(me_ref) ^ flip, HD)
        dk_ref[:, at] = piece[:, :HD]
        dv_ref[:, at] = piece[:, HD:]


def place_keys(me, *pieces):
    return pl.pallas_call(
        place_keys_kernel,
        in_specs=[SCALARS] + [HERE] * 4,
        out_specs=[HERE] * 2,
        out_shape=[jax.ShapeDtypeStruct((TILE, KVH * HD), jnp.bfloat16)] * 2,
        compiler_params=SMALL_PARAMS,
        name="place_keys",
    )(me, *pieces)


def per_device(steps, queries, keys, values, outputs, out_grad, ancestors):
    level, side, core = (lax.axis_index(name) for name in ("level", "side", "core"))
    me = (QUAD * level + 2 * side + core).reshape(1).astype(jnp.int32)

    def to_partner(x, flip):
        return lax.ppermute(x, ("side", "core"), [(t, t ^ flip) for t in range(QUAD)])

    def after(x, done):
        return lax.optimization_barrier((x, done))[0]

    def up(x, shift):
        return lax.ppermute(x, "level", [(z, z + shift) for z in range(steps - shift)])

    def up_all(x):
        return [x] + [up(x, shift) for shift in range(1, steps)]

    def down(x, shift):
        return lax.ppermute(x, "level", [(z + shift, z) for z in range(steps - shift)])

    def exchange(by_head):
        mine, beside, across, corner = by_head
        return [mine, to_partner(across, 1), to_partner(beside, 2), to_partner(corner, 3)]

    kv_quad = exchange(pack_keys(me, keys, values))
    q_sent = pack_queries(me, after(queries, kv_quad[1]))
    q_set = exchange([queries, *q_sent])
    k_level, v_level = join_keys(*after(kv_quad, q_sent))
    k_list = up_all(k_level)
    v_list = up_all(after(v_level, k_list))
    g_set = exchange([out_grad, *pack_queries(me, after(out_grad, q_set[2]))])
    d_set = exchange(row_deltas(me, outputs, out_grad, after(k_list[1], k_list)))

    lse = statistics(me, ancestors, q_set, k_list)
    common = (me, ancestors, q_set, g_set, d_set, lse)
    dq_far, *far = gradients("far", *common, k_list[2:], v_list[2:])
    back = [down(far[shift - 2], shift) for shift in range(2, steps)]
    dq_side, *accs = gradients("side", *common, k_list[:2], v_list[:2], dq_far)
    dq_side = to_partner(dq_side, 2)
    dq_own, dq_core, total, near = gradients(
        "own", *common, k_list[:2], v_list[:2], dq_far, *accs
    )
    total, near = add_far(total, back, near)
    near = down(near, 1)
    dq_core = to_partner(dq_core, 1)

    sums = add_sums(total, near)
    sums = [sums[0]] + [to_partner(sums[flip], flip) for flip in range(1, QUAD)]
    dq_side = after(dq_side, sums)
    dq_corner = to_partner(dq_side[TILE:], 1)
    return (
        place_queries(me, dq_own, dq_core, dq_side, dq_corner),
        *place_keys(me, *sums),
    )


def solution(mesh):
    parts, tok = mesh.shape["parts"], mesh.shape["tok"]
    quads = Mesh(
        mesh.devices.reshape(parts, tok // QUAD, 2, 2), ("parts", "level", "side", "core")
    )
    rows = P(("parts", "level", "side", "core"), None)
    return jax.shard_map(
        functools.partial(per_device, tok // QUAD),
        mesh=quads,
        in_specs=(rows, rows, rows, rows, rows, P("parts", None)),
        out_specs=(rows, rows, rows),
        check_vma=False,
    )
```

```python
import functools
import math

import jax
import jax.numpy as jnp
from jax import lax
from jax.experimental import pallas as pl
from jax.experimental.pallas import tpu as pltpu
from jax.sharding import Mesh
from jax.sharding import PartitionSpec as P

QH = 32
KVH = 4
HD = 128
TILE = 128
GROUP = QH // KVH
ROWS = GROUP * TILE
PAIR = 2 * TILE
QUAD = 4
LEVEL = QUAD * TILE
SCALE = HD ** (-0.5)
SCALE2 = SCALE / math.log(2.0)
MASKED = -1e30
SCALARS = pl.BlockSpec(memory_space=pltpu.SMEM)
HERE = pl.BlockSpec(memory_space=pltpu.VMEM)
NT_DIMS = (((1,), (1,)), ((), ()))
PARAMS = pltpu.CompilerParams(vmem_limit_bytes=28 * 1024 * 1024)
SMALL_PARAMS = pltpu.CompilerParams(vmem_limit_bytes=16 * 1024 * 1024)


def delta_kernel(me_ref, out_ref, grad_ref, after_ref, mine_ref, beside_ref, pair_ref):
    for flip in range(QUAD):
        base = (own_head(me_ref) ^ flip) * ROWS
        delta_ref, row = ((mine_ref, 0), (beside_ref, 0), (pair_ref, 0), (pair_ref, GROUP))[flip]
        for head in range(GROUP):
            cols = pl.ds(pl.multiple_of(base + head * HD, HD), HD)
            product = out_ref[:, cols].astype(jnp.float32) * grad_ref[:, cols].astype(jnp.float32)
            delta_ref[row + head : row + head + 1, :] = jnp.sum(product.T, axis=0, keepdims=True)


def row_deltas(me, outputs, out_grad, after):
    return pl.pallas_call(
        delta_kernel,
        in_specs=[SCALARS, HERE, HERE, pl.BlockSpec(memory_space=pl.ANY)],
        out_specs=[HERE] * 3,
        out_shape=[
            jax.ShapeDtypeStruct((count * GROUP, TILE), jnp.float32) for count in (1, 1, 2)
        ],
        compiler_params=SMALL_PARAMS,
        name="row_deltas",
    )(me, outputs, out_grad, after)


def list_items(items, anc_ref, me, tiles, depth, part):
    tile_of, first_of, second_of, flags_of = items
    cut = ((me >> 2) - 1) * QUAD
    lowest = 2 if part == "far" else 0
    count = jnp.int32(0)
    for place, u in enumerate(tiles):
        tile = me ^ u
        near, live = jnp.int32(1), jnp.int32(1)
        for slot in range(depth):
            entry = anc_ref[tile, slot]
            live += (entry >= 0).astype(jnp.int32)
            near += ((entry >= 0) & (entry >= cut)).astype(jnp.int32)
        start = near if part == "far" else jnp.int32(0)
        stop = near if part == "near" else live
        chunks = (stop - start + 1) // 2

        def slot_of(entry, tile=tile):
            seen = jnp.where(entry == 0, tile, anc_ref[tile, jnp.clip(entry - 1, 0, depth - 1)])
            return ((me >> 2) - (seen >> 2) - lowest) * QUAD + ((seen ^ me) & (QUAD - 1))

        def note(chunk, carry, place=place, start=start, stop=stop, count=count, slot_of=slot_of):
            entry = start + 2 * chunk
            good = entry + 1 < stop
            first = slot_of(entry)
            tile_of[count + chunk] = place
            first_of[count + chunk] = first
            second_of[count + chunk] = jnp.where(good, slot_of(entry + 1), first)
            flags_of[count + chunk] = 1 + 2 * good.astype(jnp.int32) + 4 * (entry == 0).astype(jnp.int32)
            return carry

        lax.fori_loop(0, chunks, note, 0)
        count += chunks
    for extra in range(2):
        tile_of[count + extra] = 0
        first_of[count + extra] = 0
        second_of[count + extra] = 0
        flags_of[count + extra] = 0
    return count


def item_scratch(tiles, depth):
    return [pltpu.SMEM((tiles * ((depth + 2) // 2) + 2,), jnp.int32)] * 4


def slot_rows(slot):
    return pl.ds(pl.multiple_of(slot * TILE, TILE), TILE)


def two_tiles(ref, first, second):
    return jnp.concatenate([ref[slot_rows(first), :], ref[slot_rows(second), :]], axis=0)


def heads_below(ref, u, first, count):
    return jnp.concatenate(
        [ref[u, :, head * HD : (head + 1) * HD] for head in range(first, first + count)], axis=0
    )


def visible_mask(flags):
    key_pos = lax.broadcasted_iota(jnp.int32, (TILE, PAIR), 0)
    query_pos = lax.broadcasted_iota(jnp.int32, (TILE, PAIR), 1) & (TILE - 1)
    return key_pos - query_pos <= jnp.where((flags & 4) != 0, 0, TILE)


def four_tiles(own, peer, side, rows):
    return own, peer, side.at[:rows, :], side.at[rows:, :]


def stats_kernel(depth, steps, me_ref, anc_ref, *rest):
    q_refs, rest = four_tiles(*rest[:3], TILE), rest[3:]
    k_refs = rest[:steps]
    lse_ref, q_all, k_all, item_max, item_sum, *items = rest[steps:]
    me = me_ref[0]
    for u, q_ref in enumerate(q_refs):
        q_all[u] = q_ref[...]
    for shift, k_ref in enumerate(k_refs):
        k_all[shift * LEVEL : (shift + 1) * LEVEL, :] = k_ref[...]
    count = list_items(items, anc_ref, me, range(QUAD), depth, "all")
    tile_of, first_of, second_of, flags_of = items

    def one_item(index):
        u, flags = tile_of[index], flags_of[index]
        good = (flags & 2) != 0
        key_block = two_tiles(k_all, first_of[index], second_of[index])
        mask = visible_mask(flags)
        for pair in range(GROUP // 2):
            rows = slice(pair * PAIR, (pair + 1) * PAIR)
            raw = lax.dot_general(
                key_block,
                heads_below(q_all, u, 2 * pair, 2),
                NT_DIMS,
                preferred_element_type=jnp.float32,
            )
            top, low = jnp.where(mask, raw[:TILE], MASKED), raw[TILE:]
            low_max = jnp.max(low, axis=0, keepdims=True)
            new_max = jnp.maximum(
                jnp.max(top, axis=0, keepdims=True), jnp.where(good, low_max, MASKED)
            )
            low_base = jnp.where(good, new_max, -MASKED)
            item_max[index, :, rows] = new_max
            item_sum[index, :, rows] = jnp.sum(
                jnp.exp2((top - new_max) * SCALE2), axis=0, keepdims=True
            ) + jnp.sum(jnp.exp2((low - low_base) * SCALE2), axis=0, keepdims=True)

    def step(index, carry):
        one_item(2 * index)
        one_item(2 * index + 1)
        return carry

    lax.fori_loop(0, (count + 1) // 2, step, 0)

    lse_ref[...] = jnp.full_like(lse_ref, MASKED)

    def combine(index, carry):
        u = tile_of[index]
        old = lse_ref[u]
        new = item_max[index] * SCALE2 + jnp.log2(item_sum[index])
        top = jnp.maximum(old, new)
        lse_ref[u] = top + jnp.log2(jnp.exp2(old - top) + jnp.exp2(new - top))
        return carry

    lax.fori_loop(0, count, combine, 0)


def grads_kernel(depth, stage, steps, me_ref, anc_ref, *rest):
    q_refs, g_refs = four_tiles(*rest[:3], TILE), four_tiles(*rest[3:6], TILE)
    d_refs, rest = four_tiles(*rest[6:9], GROUP), rest[9:]
    lse_ref, rest = rest[0], rest[1:]
    kv_refs, rest = rest[: 2 * steps], rest[2 * steps :]
    if stage != "far":
        dq_in, rest = rest[0], rest[1:]
    if stage == "own":
        dk_in, dv_in, rest = rest[0], rest[1], rest[2:]
    tiles = {"far": (0, 1, 2, 3), "side": (2, 3), "own": (0, 1)}[stage]
    if stage == "far":
        dq_acc, partial_refs, rest = rest[0], rest[1 : 1 + steps], rest[1 + steps :]
    elif stage == "side":
        dq_refs = (rest[0].at[:TILE, :], rest[0].at[TILE:, :])
        dk_acc, dv_acc, rest = rest[1], rest[2], rest[3:]
    else:
        dq_refs, partial_refs, rest = rest[:2], rest[2 : 2 + steps], rest[2 + steps :]
    items, rest = rest[:4], rest[4:]
    q_all, g_all, delta, k_all, v_all = rest[:5]
    buffers, rest = ((rest[5], rest[6]), (rest[7], rest[8])), rest[9:]
    if stage != "side":
        dk_acc, dv_acc, rest = rest[0], rest[1], rest[2:]
    if stage != "far":
        dq_acc = rest[0]
    me = me_ref[0]
    for place, u in enumerate(tiles):
        q_all[place] = q_refs[u][...]
        g_all[place] = g_refs[u][...]
        for head in range(GROUP):
            cols = slice(head * TILE, (head + 1) * TILE)
            delta[place, :, cols] = d_refs[u][head : head + 1, :]
    for shift in range(steps):
        k_all[shift * LEVEL : (shift + 1) * LEVEL, :] = kv_refs[shift][...]
        v_all[shift * LEVEL : (shift + 1) * LEVEL, :] = kv_refs[steps + shift][...]
    if stage == "own":
        dk_acc[...] = dk_in[...]
        dv_acc[...] = dv_in[...]
    else:
        dk_acc[...] = jnp.zeros_like(dk_acc)
        dv_acc[...] = jnp.zeros_like(dv_acc)
    if stage == "far":
        dq_acc[...] = jnp.zeros_like(dq_acc)
    else:
        dq_acc[...] = dq_in[...]
    for buffer in buffers[1]:
        buffer[...] = jnp.zeros_like(buffer)
    count = list_items(items, anc_ref, me, tiles, depth, "far" if stage == "far" else "near")
    tile_of, first_of, second_of, flags_of = items

    def scores_part(index, low_ref, score_ref):
        place, flags = tile_of[index], flags_of[index]
        first, second = first_of[index], second_of[index]
        key_block = two_tiles(k_all, first, second)
        value_block = two_tiles(v_all, first, second)
        for pair in range(GROUP // 2):
            rows = slice(pair * PAIR, (pair + 1) * PAIR)
            raw = lax.dot_general(
                key_block,
                heads_below(q_all, place, 2 * pair, 2),
                NT_DIMS,
                preferred_element_type=jnp.float32,
            )
            grad_probs = lax.dot_general(
                value_block,
                heads_below(g_all, place, 2 * pair, 2),
                NT_DIMS,
                preferred_element_type=jnp.float32,
            )
            lse = lse_ref[tiles[0] + place, :, rows]
            away = delta[place, :, rows]
            for part in range(2):
                half = slice(part * TILE, (part + 1) * TILE)
                base = jnp.where((flags & (1 + part)) != 0, lse, -MASKED)
                attn = jnp.exp2(raw[half] * SCALE2 - base)
                if stage != "far" and part == 0:
                    attn = jnp.where(visible_mask(flags), attn, 0.0)
                low_ref[half, rows] = attn.astype(jnp.bfloat16)
                score_ref[half, rows] = (attn * (grad_probs[half] - away)).astype(jnp.bfloat16)

    def grads_part(index, low_ref, score_ref):
        index = jnp.maximum(index, 0)
        place, first, second = tile_of[index], first_of[index], second_of[index]
        dv = jnp.dot(
            low_ref[...], heads_below(g_all, place, 0, GROUP), preferred_element_type=jnp.float32
        )
        dk = jnp.dot(
            score_ref[...], heads_below(q_all, place, 0, GROUP), preferred_element_type=jnp.float32
        )
        dq_acc[place] += jnp.dot(
            two_tiles(k_all, first, second).T, score_ref[...], preferred_element_type=jnp.float32
        )
        dk_acc[slot_rows(first), :] += dk[:TILE]
        dk_acc[slot_rows(second), :] += dk[TILE:]
        dv_acc[slot_rows(first), :] += dv[:TILE]
        dv_acc[slot_rows(second), :] += dv[TILE:]

    def step(index, carry):
        scores_part(2 * index, *buffers[0])
        grads_part(2 * index - 1, *buffers[1])
        scores_part(2 * index + 1, *buffers[1])
        grads_part(2 * index, *buffers[0])
        return carry

    lax.fori_loop(0, jnp.where(count > 0, (count + 2) // 2, 0), step, 0)

    if stage != "far":
        for place in range(2):
            for head in range(GROUP):
                cols = slice(head * HD, (head + 1) * HD)
                dq_refs[place][:, cols] = (dq_acc[place, :, cols] * SCALE).T.astype(jnp.bfloat16)
    if stage != "side":
        for shift, out_ref in enumerate(partial_refs):
            rows = slice(shift * LEVEL, (shift + 1) * LEVEL)
            out_ref[:, :HD] = dk_acc[rows, :].astype(out_ref.dtype)
            out_ref[:, HD:] = dv_acc[rows, :].astype(out_ref.dtype)


def work(ancestors, products):
    pairs = QUAD * (ancestors.shape[1] + 1)
    return pl.CostEstimate(
        flops=2 * products * pairs * GROUP * TILE * TILE * 2 * HD,
        transcendentals=pairs * GROUP * TILE * TILE,
        bytes_accessed=16 * 1024 * 1024,
    )


def fixed(shape):
    return pl.BlockSpec(shape, lambda i, *_: (0,) * len(shape))


def own_head(me_ref):
    return ((me_ref[0] & 1) << 1) | ((me_ref[0] >> 1) & 1)


WIDE = pl.BlockSpec((TILE, ROWS), lambda i, me_ref, anc_ref: (0, own_head(me_ref)))
LSE = fixed((QUAD, 1, ROWS))
KEYS = fixed((LEVEL, HD))
SUMS = fixed((LEVEL, 2 * HD))
DQ = fixed((QUAD, HD, ROWS))
PIECE = fixed((TILE, ROWS))
SIDE = fixed((PAIR, ROWS))
DELTA = fixed((GROUP, TILE))
PAIR_DELTA = fixed((2 * GROUP, TILE))


def statistics(me, ancestors, q_set, k_list):
    steps = len(k_list)
    items = item_scratch(QUAD, ancestors.shape[1])
    count = items[0].shape[0]
    return pl.pallas_call(
        functools.partial(stats_kernel, ancestors.shape[1], steps),
        grid_spec=pltpu.PrefetchScalarGridSpec(
            num_scalar_prefetch=2,
            grid=(1,),
            in_specs=[WIDE, WIDE, SIDE] + [KEYS] * steps,
            out_specs=LSE,
            scratch_shapes=[
                pltpu.VMEM((QUAD, TILE, ROWS), jnp.bfloat16),
                pltpu.VMEM((steps * LEVEL, HD), jnp.bfloat16),
                pltpu.VMEM((count, 1, ROWS), jnp.float32),
                pltpu.VMEM((count, 1, ROWS), jnp.float32),
                *items,
            ],
        ),
        out_shape=jax.ShapeDtypeStruct((QUAD, 1, ROWS), jnp.float32),
        compiler_params=PARAMS,
        cost_estimate=work(ancestors, 1),
        name="statistics",
    )(me, ancestors, *q_set, *k_list)


def gradients(stage, me, ancestors, q_set, g_set, d_set, lse, k_list, v_list, *carried):
    steps = len(k_list)
    tiles = QUAD if stage == "far" else 2
    acc = (steps * LEVEL, HD)
    wide = jax.ShapeDtypeStruct((TILE, ROWS), jnp.bfloat16)
    sums = [jax.ShapeDtypeStruct((LEVEL, 2 * HD), jnp.bfloat16)] * steps
    accs = [jax.ShapeDtypeStruct(acc, jnp.float32)] * 2
    dq_half = pl.BlockSpec((2, HD, ROWS), lambda i, *_: (1 if stage == "side" else 0, 0, 0))
    extra_specs = [dq_half, fixed(acc), fixed(acc)][: len(carried)]
    if stage == "far":
        out_specs = [DQ] + [SUMS] * steps
        out_shape = [jax.ShapeDtypeStruct((QUAD, HD, ROWS), jnp.float32)] + sums
    elif stage == "side":
        out_specs = [SIDE, fixed(acc), fixed(acc)]
        out_shape = [jax.ShapeDtypeStruct((PAIR, ROWS), jnp.bfloat16)] + accs
    else:
        sums[0] = jax.ShapeDtypeStruct((LEVEL, 2 * HD), jnp.float32)
        out_specs = [PIECE, PIECE] + [SUMS] * steps
        out_shape = [wide, wide] + sums
    scratch = item_scratch(tiles, ancestors.shape[1]) + [
        pltpu.VMEM((tiles, TILE, ROWS), jnp.bfloat16),
        pltpu.VMEM((tiles, TILE, ROWS), jnp.bfloat16),
        pltpu.VMEM((tiles, 1, ROWS), jnp.float32),
        pltpu.VMEM(acc, jnp.bfloat16),
        pltpu.VMEM(acc, jnp.bfloat16),
    ]
    scratch += [pltpu.VMEM((PAIR, ROWS), jnp.bfloat16)] * 4
    if stage != "side":
        scratch += [pltpu.VMEM(acc, jnp.float32)] * 2
    if stage != "far":
        scratch.append(pltpu.VMEM((tiles, HD, ROWS), jnp.float32))
    return pl.pallas_call(
        functools.partial(grads_kernel, ancestors.shape[1], stage, steps),
        grid_spec=pltpu.PrefetchScalarGridSpec(
            num_scalar_prefetch=2,
            grid=(1,),
            in_specs=[WIDE, WIDE, SIDE] * 2 + [DELTA, PAIR_DELTA, PAIR_DELTA, LSE]
            + [KEYS] * (2 * steps)
            + extra_specs,
            out_specs=out_specs,
            scratch_shapes=scratch,
        ),
        out_shape=out_shape,
        compiler_params=PARAMS,
        cost_estimate=work(ancestors, 5),
        name=stage + "_grads",
    )(me, ancestors, *q_set, *g_set, *d_set, lse, *k_list, *v_list, *carried)


def head_columns(head, width):
    return pl.ds(pl.multiple_of(head * width, width), width)


def pack_keys_kernel(me_ref, keys, values, *out_refs):
    for flip, out_ref in enumerate(out_refs):
        at = head_columns(own_head(me_ref) ^ flip, HD)
        out_ref[:, :HD] = keys[:, at]
        out_ref[:, HD:] = values[:, at]


def pack_keys(me, keys, values):
    return pl.pallas_call(
        pack_keys_kernel,
        in_specs=[SCALARS, HERE, HERE],
        out_specs=[HERE] * QUAD,
        out_shape=[jax.ShapeDtypeStruct((TILE, 2 * HD), jnp.bfloat16)] * QUAD,
        compiler_params=SMALL_PARAMS,
        name="pack_keys",
    )(me, keys, values)


def join_keys_kernel(*refs):
    k_ref, v_ref = refs[-2:]
    for place, ref in enumerate(refs[:-2]):
        rows = slice(place * TILE, (place + 1) * TILE)
        k_ref[rows, :] = ref[:, :HD]
        v_ref[rows, :] = ref[:, HD:]


def join_keys(*pieces):
    return pl.pallas_call(
        join_keys_kernel,
        in_specs=[HERE] * QUAD,
        out_specs=[HERE] * 2,
        out_shape=[jax.ShapeDtypeStruct((LEVEL, HD), jnp.bfloat16)] * 2,
        compiler_params=SMALL_PARAMS,
        name="join_keys",
    )(*pieces)


def pack_queries_kernel(me_ref, own, peer, send_ref):
    at = head_columns(own_head(me_ref) ^ 1, ROWS)
    send_ref[:TILE, :] = own[:, at]
    send_ref[TILE:, :] = peer[:, at]


def pack_queries(me, own, peer):
    return pl.pallas_call(
        pack_queries_kernel,
        in_specs=[SCALARS, HERE, HERE],
        out_specs=HERE,
        out_shape=jax.ShapeDtypeStruct((PAIR, ROWS), jnp.bfloat16),
        compiler_params=SMALL_PARAMS,
        name="pack_queries",
    )(me, own, peer)


def pack_deltas_kernel(own, pair, send_ref):
    send_ref[:GROUP, :] = own[...]
    send_ref[GROUP:, :] = pair[GROUP:, :]


def pack_deltas(own, pair):
    return pl.pallas_call(
        pack_deltas_kernel,
        in_specs=[HERE] * 2,
        out_specs=HERE,
        out_shape=jax.ShapeDtypeStruct((2 * GROUP, TILE), jnp.float32),
        compiler_params=SMALL_PARAMS,
        name="pack_deltas",
    )(own, pair)


def add_far_kernel(total_ref, *refs):
    parts, out_ref = refs[:-3], refs[-2]
    total = total_ref[...]
    for part in parts:
        total += part[...].astype(jnp.float32)
    out_ref[...] = total


def add_far(acc, parts, passing):
    here = pl.BlockSpec(memory_space=pltpu.VMEM)
    anywhere = pl.BlockSpec(memory_space=pl.ANY)
    return pl.pallas_call(
        add_far_kernel,
        in_specs=[here] * (1 + len(parts)) + [anywhere],
        out_specs=[here, anywhere],
        out_shape=[
            jax.ShapeDtypeStruct(acc.shape, jnp.float32),
            jax.ShapeDtypeStruct(passing.shape, passing.dtype),
        ],
        input_output_aliases={1 + len(parts): 1},
        compiler_params=SMALL_PARAMS,
        name="add_far",
    )(acc, *parts, passing)


def add_sums_kernel(total_ref, near_ref, *out_refs):
    total = total_ref[...] + near_ref[...].astype(jnp.float32)
    scaled = jnp.concatenate([total[:, :HD] * SCALE, total[:, HD:]], axis=1).astype(jnp.bfloat16)
    for place, out_ref in enumerate(out_refs):
        out_ref[...] = scaled[place * TILE : (place + 1) * TILE]


def add_sums(total, near):
    return pl.pallas_call(
        add_sums_kernel,
        in_specs=[HERE] * 2,
        out_specs=[HERE] * QUAD,
        out_shape=[jax.ShapeDtypeStruct((TILE, 2 * HD), jnp.bfloat16)] * QUAD,
        compiler_params=SMALL_PARAMS,
        name="add_sums",
    )(total, near)


FLIPS = (0, 2, 1, 3)


def place_queries_kernel(me_ref, *refs):
    for flip, piece in zip(FLIPS, refs[:-1]):
        refs[-1][:, head_columns(own_head(me_ref) ^ flip, ROWS)] = piece[:TILE, :]


def place_queries(me, *pieces):
    return pl.pallas_call(
        place_queries_kernel,
        in_specs=[SCALARS] + [HERE] * 4,
        out_specs=HERE,
        out_shape=jax.ShapeDtypeStruct((TILE, QH * HD), jnp.bfloat16),
        compiler_params=SMALL_PARAMS,
        name="place_queries",
    )(me, *pieces)


def place_keys_kernel(me_ref, *refs):
    dk_ref, dv_ref = refs[-2:]
    for flip, piece in zip(FLIPS, refs[:-2]):
        at = head_columns(own_head(me_ref) ^ flip, HD)
        dk_ref[:, at] = piece[:, :HD]
        dv_ref[:, at] = piece[:, HD:]


def place_keys(me, *pieces):
    return pl.pallas_call(
        place_keys_kernel,
        in_specs=[SCALARS] + [HERE] * 4,
        out_specs=[HERE] * 2,
        out_shape=[jax.ShapeDtypeStruct((TILE, KVH * HD), jnp.bfloat16)] * 2,
        compiler_params=SMALL_PARAMS,
        name="place_keys",
    )(me, *pieces)


def per_device(steps, queries, keys, values, outputs, out_grad, ancestors):
    level, side, core = (lax.axis_index(name) for name in ("level", "side", "core"))
    me = (QUAD * level + 2 * side + core).reshape(1).astype(jnp.int32)

    def to_partner(x, flip):
        return lax.ppermute(x, ("side", "core"), [(t, t ^ flip) for t in range(QUAD)])

    def after(x, done):
        return lax.optimization_barrier((x, done))[0]

    def up(x, shift):
        return lax.ppermute(x, "level", [(z, z + shift) for z in range(steps - shift)])

    def up_all(x):
        return [x] + [up(x, shift) for shift in range(1, steps)]

    def down(x, shift):
        return lax.ppermute(x, "level", [(z + shift, z) for z in range(steps - shift)])

    def exchange(by_head):
        mine, beside, across, corner = by_head
        return [mine, to_partner(across, 1), to_partner(beside, 2), to_partner(corner, 3)]

    kv_quad = exchange(pack_keys(me, keys, values))
    k_level, v_level = join_keys(*kv_quad)
    k_list = up_all(k_level)
    q_peer = to_partner(queries, 1)
    q_set = [queries, q_peer, to_partner(pack_queries(me, queries, after(q_peer, k_level)), 2)]
    g_peer = to_partner(out_grad, 1)
    g_set = [out_grad, g_peer, to_partner(pack_queries(me, out_grad, after(g_peer, k_list)), 2)]
    v_list = up_all(after(v_level, k_list))
    d_own, d_beside, d_pair = row_deltas(me, outputs, out_grad, after(k_level, k_list))
    d_pair = to_partner(d_pair, 1)
    d_set = [d_own, d_pair, to_partner(pack_deltas(d_beside, d_pair), 2)]

    lse = statistics(me, ancestors, q_set, k_list)
    common = (me, ancestors, q_set, g_set, d_set, lse)
    dq_far, *far = gradients("far", *common, k_list[2:], v_list[2:])
    back = [down(far[shift - 2], shift) for shift in range(2, steps)]
    dq_side, *accs = gradients("side", *common, k_list[:2], v_list[:2], dq_far)
    dq_side = to_partner(dq_side, 2)
    dq_own, dq_core, total, near = gradients(
        "own", *common, k_list[:2], v_list[:2], dq_far, *accs
    )
    near = down(near, 1)
    total, dq_core = add_far(total, back, dq_core)
    dq_core = to_partner(dq_core, 1)
    total = after(total, dq_core)

    sums = add_sums(total, near)
    sums = [sums[0]] + [to_partner(sums[flip], flip) for flip in range(1, QUAD)]
    dq_side = after(dq_side, sums)
    dq_corner = to_partner(dq_side[TILE:], 1)
    return (
        place_queries(me, dq_own, dq_core, dq_side, dq_corner),
        *place_keys(me, *sums),
    )


def solution(mesh):
    parts, tok = mesh.shape["parts"], mesh.shape["tok"]
    quads = Mesh(
        mesh.devices.reshape(parts, tok // QUAD, 2, 2), ("parts", "level", "side", "core")
    )
    rows = P(("parts", "level", "side", "core"), None)
    return jax.shard_map(
        functools.partial(per_device, tok // QUAD),
        mesh=quads,
        in_specs=(rows, rows, rows, rows, rows, P("parts", None)),
        out_specs=(rows, rows, rows),
        check_vma=False,
    )
```

```python
import functools
import math

import jax
import jax.numpy as jnp
from jax import lax
from jax.experimental import pallas as pl
from jax.experimental.pallas import tpu as pltpu
from jax.sharding import Mesh
from jax.sharding import PartitionSpec as P

QH = 32
KVH = 4
HD = 128
TILE = 128
GROUP = QH // KVH
ROWS = GROUP * TILE
PAIR = 2 * TILE
QUAD = 4
LEVEL = QUAD * TILE
SCALE = HD ** (-0.5)
SCALE2 = SCALE / math.log(2.0)
MASKED = -1e30
SCALARS = pl.BlockSpec(memory_space=pltpu.SMEM)
HERE = pl.BlockSpec(memory_space=pltpu.VMEM)
NT_DIMS = (((1,), (1,)), ((), ()))
PARAMS = pltpu.CompilerParams(vmem_limit_bytes=28 * 1024 * 1024)
SMALL_PARAMS = pltpu.CompilerParams(vmem_limit_bytes=16 * 1024 * 1024)


def delta_kernel(me_ref, out_ref, grad_ref, after_ref, mine_ref, beside_ref, pair_ref):
    for flip in range(QUAD):
        base = (own_head(me_ref) ^ flip) * ROWS
        delta_ref, row = ((mine_ref, 0), (beside_ref, 0), (pair_ref, 0), (pair_ref, GROUP))[flip]
        for head in range(GROUP):
            cols = pl.ds(pl.multiple_of(base + head * HD, HD), HD)
            product = out_ref[:, cols].astype(jnp.float32) * grad_ref[:, cols].astype(jnp.float32)
            delta_ref[row + head : row + head + 1, :] = jnp.sum(product.T, axis=0, keepdims=True)


def row_deltas(me, outputs, out_grad, after):
    return pl.pallas_call(
        delta_kernel,
        in_specs=[SCALARS, HERE, HERE, pl.BlockSpec(memory_space=pl.ANY)],
        out_specs=[HERE] * 3,
        out_shape=[
            jax.ShapeDtypeStruct((count * GROUP, TILE), jnp.float32) for count in (1, 1, 2)
        ],
        compiler_params=SMALL_PARAMS,
        name="row_deltas",
    )(me, outputs, out_grad, after)


def list_items(items, anc_ref, me, tiles, depth, part):
    tile_of, first_of, second_of, flags_of = items
    cut = ((me >> 2) - 1) * QUAD
    lowest = 2 if part == "far" else 0
    count = jnp.int32(0)
    for place, u in enumerate(tiles):
        tile = me ^ u
        near, live = jnp.int32(1), jnp.int32(1)
        for slot in range(depth):
            entry = anc_ref[tile, slot]
            live += (entry >= 0).astype(jnp.int32)
            near += ((entry >= 0) & (entry >= cut)).astype(jnp.int32)
        start = near if part == "far" else jnp.int32(0)
        stop = near if part == "near" else live
        chunks = (stop - start + 1) // 2

        def slot_of(entry, tile=tile):
            seen = jnp.where(entry == 0, tile, anc_ref[tile, jnp.clip(entry - 1, 0, depth - 1)])
            return ((me >> 2) - (seen >> 2) - lowest) * QUAD + ((seen ^ me) & (QUAD - 1))

        def note(chunk, carry, place=place, start=start, stop=stop, count=count, slot_of=slot_of):
            entry = start + 2 * chunk
            good = entry + 1 < stop
            first = slot_of(entry)
            tile_of[count + chunk] = place
            first_of[count + chunk] = first
            second_of[count + chunk] = jnp.where(good, slot_of(entry + 1), first)
            flags_of[count + chunk] = 1 + 2 * good.astype(jnp.int32) + 4 * (entry == 0).astype(jnp.int32)
            return carry

        lax.fori_loop(0, chunks, note, 0)
        count += chunks
    for extra in range(2):
        tile_of[count + extra] = 0
        first_of[count + extra] = 0
        second_of[count + extra] = 0
        flags_of[count + extra] = 0
    return count


def item_scratch(tiles, depth):
    return [pltpu.SMEM((tiles * ((depth + 2) // 2) + 2,), jnp.int32)] * 4


def slot_rows(slot):
    return pl.ds(pl.multiple_of(slot * TILE, TILE), TILE)


def two_tiles(ref, first, second):
    return jnp.concatenate([ref[slot_rows(first), :], ref[slot_rows(second), :]], axis=0)


def heads_below(ref, u, first, count):
    return jnp.concatenate(
        [ref[u, :, head * HD : (head + 1) * HD] for head in range(first, first + count)], axis=0
    )


def visible_mask(flags):
    key_pos = lax.broadcasted_iota(jnp.int32, (TILE, PAIR), 0)
    query_pos = lax.broadcasted_iota(jnp.int32, (TILE, PAIR), 1) & (TILE - 1)
    return key_pos - query_pos <= jnp.where((flags & 4) != 0, 0, TILE)


def query_tiles(me_ref, own, peer, side):
    at = head_columns(own_head(me_ref), ROWS)
    return four_tiles(own.at[:, at], peer.at[:, at], side, TILE)


def four_tiles(own, peer, side, rows):
    return own, peer, side.at[:rows, :], side.at[rows:, :]


def stats_kernel(depth, steps, me_ref, anc_ref, *rest):
    q_refs, rest = query_tiles(me_ref, *rest[:3]), rest[3:]
    k_refs = rest[:steps]
    lse_ref, q_all, k_all, item_max, item_sum, *items = rest[steps:]
    me = me_ref[0]
    for u, q_ref in enumerate(q_refs):
        q_all[u] = q_ref[...]
    for shift, k_ref in enumerate(k_refs):
        k_all[shift * LEVEL : (shift + 1) * LEVEL, :] = k_ref[...]
    count = list_items(items, anc_ref, me, range(QUAD), depth, "all")
    tile_of, first_of, second_of, flags_of = items

    def one_item(index):
        u, flags = tile_of[index], flags_of[index]
        good = (flags & 2) != 0
        key_block = two_tiles(k_all, first_of[index], second_of[index])
        mask = visible_mask(flags)
        for pair in range(GROUP // 2):
            rows = slice(pair * PAIR, (pair + 1) * PAIR)
            raw = lax.dot_general(
                key_block,
                heads_below(q_all, u, 2 * pair, 2),
                NT_DIMS,
                preferred_element_type=jnp.float32,
            )
            top, low = jnp.where(mask, raw[:TILE], MASKED), raw[TILE:]
            low_max = jnp.max(low, axis=0, keepdims=True)
            new_max = jnp.maximum(
                jnp.max(top, axis=0, keepdims=True), jnp.where(good, low_max, MASKED)
            )
            low_base = jnp.where(good, new_max, -MASKED)
            item_max[index, :, rows] = new_max
            item_sum[index, :, rows] = jnp.sum(
                jnp.exp2((top - new_max) * SCALE2), axis=0, keepdims=True
            ) + jnp.sum(jnp.exp2((low - low_base) * SCALE2), axis=0, keepdims=True)

    def step(index, carry):
        one_item(2 * index)
        one_item(2 * index + 1)
        return carry

    lax.fori_loop(0, (count + 1) // 2, step, 0)

    lse_ref[...] = jnp.full_like(lse_ref, MASKED)

    def combine(index, carry):
        u = tile_of[index]
        old = lse_ref[u]
        new = item_max[index] * SCALE2 + jnp.log2(item_sum[index])
        top = jnp.maximum(old, new)
        lse_ref[u] = top + jnp.log2(jnp.exp2(old - top) + jnp.exp2(new - top))
        return carry

    lax.fori_loop(0, count, combine, 0)


def grads_kernel(depth, stage, steps, me_ref, anc_ref, *rest):
    q_refs, g_refs = query_tiles(me_ref, *rest[:3]), query_tiles(me_ref, *rest[3:6])
    d_refs, rest = four_tiles(*rest[6:9], GROUP), rest[9:]
    lse_ref, rest = rest[0], rest[1:]
    kv_refs, rest = rest[: 2 * steps], rest[2 * steps :]
    if stage != "far":
        dq_in, rest = rest[0], rest[1:]
    if stage == "own":
        dk_in, dv_in, rest = rest[0], rest[1], rest[2:]
    tiles = {"far": (0, 1, 2, 3), "side": (2, 3), "own": (0, 1)}[stage]
    if stage == "far":
        dq_acc, partial_refs, rest = rest[0], rest[1 : 1 + steps], rest[1 + steps :]
    elif stage == "side":
        dq_refs = (rest[0].at[:TILE, :], rest[0].at[TILE:, :])
        dk_acc, dv_acc, rest = rest[1], rest[2], rest[3:]
    else:
        dq_refs, partial_refs, rest = rest[:2], rest[2 : 2 + steps], rest[2 + steps :]
    items, rest = rest[:4], rest[4:]
    q_all, g_all, delta, k_all, v_all = rest[:5]
    buffers, rest = ((rest[5], rest[6]), (rest[7], rest[8])), rest[9:]
    if stage != "side":
        dk_acc, dv_acc, rest = rest[0], rest[1], rest[2:]
    if stage != "far":
        dq_acc = rest[0]
    me = me_ref[0]
    for place, u in enumerate(tiles):
        q_all[place] = q_refs[u][...]
        g_all[place] = g_refs[u][...]
        for head in range(GROUP):
            cols = slice(head * TILE, (head + 1) * TILE)
            delta[place, :, cols] = d_refs[u][head : head + 1, :]
    for shift in range(steps):
        k_all[shift * LEVEL : (shift + 1) * LEVEL, :] = kv_refs[shift][...]
        v_all[shift * LEVEL : (shift + 1) * LEVEL, :] = kv_refs[steps + shift][...]
    if stage == "own":
        dk_acc[...] = dk_in[...]
        dv_acc[...] = dv_in[...]
    else:
        dk_acc[...] = jnp.zeros_like(dk_acc)
        dv_acc[...] = jnp.zeros_like(dv_acc)
    if stage == "far":
        dq_acc[...] = jnp.zeros_like(dq_acc)
    else:
        dq_acc[...] = dq_in[tiles[0] : tiles[0] + 2]
    for buffer in buffers[1]:
        buffer[...] = jnp.zeros_like(buffer)
    count = list_items(items, anc_ref, me, tiles, depth, "far" if stage == "far" else "near")
    tile_of, first_of, second_of, flags_of = items

    def scores_part(index, low_ref, score_ref):
        place, flags = tile_of[index], flags_of[index]
        first, second = first_of[index], second_of[index]
        key_block = two_tiles(k_all, first, second)
        value_block = two_tiles(v_all, first, second)
        for pair in range(GROUP // 2):
            rows = slice(pair * PAIR, (pair + 1) * PAIR)
            raw = lax.dot_general(
                key_block,
                heads_below(q_all, place, 2 * pair, 2),
                NT_DIMS,
                preferred_element_type=jnp.float32,
            )
            grad_probs = lax.dot_general(
                value_block,
                heads_below(g_all, place, 2 * pair, 2),
                NT_DIMS,
                preferred_element_type=jnp.float32,
            )
            lse = lse_ref[tiles[0] + place, :, rows]
            away = delta[place, :, rows]
            for part in range(2):
                half = slice(part * TILE, (part + 1) * TILE)
                base = jnp.where((flags & (1 + part)) != 0, lse, -MASKED)
                attn = jnp.exp2(raw[half] * SCALE2 - base)
                if stage != "far" and part == 0:
                    attn = jnp.where(visible_mask(flags), attn, 0.0)
                low_ref[half, rows] = attn.astype(jnp.bfloat16)
                score_ref[half, rows] = (attn * (grad_probs[half] - away)).astype(jnp.bfloat16)

    def grads_part(index, low_ref, score_ref):
        index = jnp.maximum(index, 0)
        place, first, second = tile_of[index], first_of[index], second_of[index]
        dv = jnp.dot(
            low_ref[...], heads_below(g_all, place, 0, GROUP), preferred_element_type=jnp.float32
        )
        dk = jnp.dot(
            score_ref[...], heads_below(q_all, place, 0, GROUP), preferred_element_type=jnp.float32
        )
        dq_acc[place] += jnp.dot(
            two_tiles(k_all, first, second).T, score_ref[...], preferred_element_type=jnp.float32
        )
        dk_acc[slot_rows(first), :] += dk[:TILE]
        dk_acc[slot_rows(second), :] += dk[TILE:]
        dv_acc[slot_rows(first), :] += dv[:TILE]
        dv_acc[slot_rows(second), :] += dv[TILE:]

    def step(index, carry):
        scores_part(2 * index, *buffers[0])
        grads_part(2 * index - 1, *buffers[1])
        scores_part(2 * index + 1, *buffers[1])
        grads_part(2 * index, *buffers[0])
        return carry

    lax.fori_loop(0, jnp.where(count > 0, (count + 2) // 2, 0), step, 0)

    if stage != "far":
        for place in range(2):
            for head in range(GROUP):
                cols = slice(head * HD, (head + 1) * HD)
                dq_refs[place][:, cols] = (dq_acc[place, :, cols] * SCALE).T.astype(jnp.bfloat16)
    if stage != "side":
        for shift, out_ref in enumerate(partial_refs):
            rows = slice(shift * LEVEL, (shift + 1) * LEVEL)
            out_ref[:, :HD] = dk_acc[rows, :].astype(out_ref.dtype)
            out_ref[:, HD:] = dv_acc[rows, :].astype(out_ref.dtype)


def work(ancestors, products):
    pairs = QUAD * (ancestors.shape[1] + 1)
    return pl.CostEstimate(
        flops=2 * products * pairs * GROUP * TILE * TILE * 2 * HD,
        transcendentals=pairs * GROUP * TILE * TILE,
        bytes_accessed=16 * 1024 * 1024,
    )


def own_head(me_ref):
    return ((me_ref[0] & 1) << 1) | ((me_ref[0] >> 1) & 1)


def statistics(me, ancestors, q_set, k_list):
    steps = len(k_list)
    items = item_scratch(QUAD, ancestors.shape[1])
    count = items[0].shape[0]
    return pl.pallas_call(
        functools.partial(stats_kernel, ancestors.shape[1], steps),
        grid_spec=pltpu.PrefetchScalarGridSpec(
            num_scalar_prefetch=2,
            grid=(1,),
            in_specs=[HERE] * (3 + steps),
            out_specs=HERE,
            scratch_shapes=[
                pltpu.VMEM((QUAD, TILE, ROWS), jnp.bfloat16),
                pltpu.VMEM((steps * LEVEL, HD), jnp.bfloat16),
                pltpu.VMEM((count, 1, ROWS), jnp.float32),
                pltpu.VMEM((count, 1, ROWS), jnp.float32),
                *items,
            ],
        ),
        out_shape=jax.ShapeDtypeStruct((QUAD, 1, ROWS), jnp.float32),
        compiler_params=PARAMS,
        cost_estimate=work(ancestors, 1),
        name="statistics",
    )(me, ancestors, *q_set, *k_list)


def gradients(stage, me, ancestors, q_set, g_set, d_set, lse, k_list, v_list, *carried):
    steps = len(k_list)
    tiles = QUAD if stage == "far" else 2
    acc = (steps * LEVEL, HD)
    wide = jax.ShapeDtypeStruct((TILE, ROWS), jnp.bfloat16)
    sums = [jax.ShapeDtypeStruct((LEVEL, 2 * HD), jnp.bfloat16)] * steps
    accs = [jax.ShapeDtypeStruct(acc, jnp.float32)] * 2
    if stage == "far":
        out_shape = [jax.ShapeDtypeStruct((QUAD, HD, ROWS), jnp.float32)] + sums
    elif stage == "side":
        out_shape = [jax.ShapeDtypeStruct((PAIR, ROWS), jnp.bfloat16)] + accs
    else:
        sums[0] = jax.ShapeDtypeStruct((LEVEL, 2 * HD), jnp.float32)
        out_shape = [wide, wide] + sums
    scratch = item_scratch(tiles, ancestors.shape[1]) + [
        pltpu.VMEM((tiles, TILE, ROWS), jnp.bfloat16),
        pltpu.VMEM((tiles, TILE, ROWS), jnp.bfloat16),
        pltpu.VMEM((tiles, 1, ROWS), jnp.float32),
        pltpu.VMEM(acc, jnp.bfloat16),
        pltpu.VMEM(acc, jnp.bfloat16),
    ]
    scratch += [pltpu.VMEM((PAIR, ROWS), jnp.bfloat16)] * 4
    if stage != "side":
        scratch += [pltpu.VMEM(acc, jnp.float32)] * 2
    if stage != "far":
        scratch.append(pltpu.VMEM((tiles, HD, ROWS), jnp.float32))
    return pl.pallas_call(
        functools.partial(grads_kernel, ancestors.shape[1], stage, steps),
        grid_spec=pltpu.PrefetchScalarGridSpec(
            num_scalar_prefetch=2,
            grid=(1,),
            in_specs=[HERE] * (10 + 2 * steps + len(carried)),
            out_specs=[HERE] * len(out_shape),
            scratch_shapes=scratch,
        ),
        out_shape=out_shape,
        compiler_params=PARAMS,
        cost_estimate=work(ancestors, 5),
        name=stage + "_grads",
    )(me, ancestors, *q_set, *g_set, *d_set, lse, *k_list, *v_list, *carried)


def head_columns(head, width):
    return pl.ds(pl.multiple_of(head * width, width), width)


def pack_keys_kernel(me_ref, keys, values, *out_refs):
    for flip, out_ref in enumerate(out_refs):
        at = head_columns(own_head(me_ref) ^ flip, HD)
        out_ref[:, :HD] = keys[:, at]
        out_ref[:, HD:] = values[:, at]


def pack_keys(me, keys, values):
    return pl.pallas_call(
        pack_keys_kernel,
        in_specs=[SCALARS, HERE, HERE],
        out_specs=[HERE] * QUAD,
        out_shape=[jax.ShapeDtypeStruct((TILE, 2 * HD), jnp.bfloat16)] * QUAD,
        compiler_params=SMALL_PARAMS,
        name="pack_keys",
    )(me, keys, values)


def join_keys_kernel(*refs):
    k_ref, v_ref = refs[-2:]
    for place, ref in enumerate(refs[:-2]):
        rows = slice(place * TILE, (place + 1) * TILE)
        k_ref[rows, :] = ref[:, :HD]
        v_ref[rows, :] = ref[:, HD:]


def join_keys(*pieces):
    return pl.pallas_call(
        join_keys_kernel,
        in_specs=[HERE] * QUAD,
        out_specs=[HERE] * 2,
        out_shape=[jax.ShapeDtypeStruct((LEVEL, HD), jnp.bfloat16)] * 2,
        compiler_params=SMALL_PARAMS,
        name="join_keys",
    )(*pieces)


def pack_queries_kernel(me_ref, own, peer, send_ref):
    at = head_columns(own_head(me_ref) ^ 1, ROWS)
    send_ref[:TILE, :] = own[:, at]
    send_ref[TILE:, :] = peer[:, at]


def pack_queries(me, own, peer):
    return pl.pallas_call(
        pack_queries_kernel,
        in_specs=[SCALARS, HERE, HERE],
        out_specs=HERE,
        out_shape=jax.ShapeDtypeStruct((PAIR, ROWS), jnp.bfloat16),
        compiler_params=SMALL_PARAMS,
        name="pack_queries",
    )(me, own, peer)


def pack_deltas_kernel(own, pair, send_ref):
    send_ref[:GROUP, :] = own[...]
    send_ref[GROUP:, :] = pair[GROUP:, :]


def pack_deltas(own, pair):
    return pl.pallas_call(
        pack_deltas_kernel,
        in_specs=[HERE] * 2,
        out_specs=HERE,
        out_shape=jax.ShapeDtypeStruct((2 * GROUP, TILE), jnp.float32),
        compiler_params=SMALL_PARAMS,
        name="pack_deltas",
    )(own, pair)


def add_far_kernel(total_ref, *refs):
    parts, out_ref = refs[:-3], refs[-2]
    total = total_ref[...]
    for part in parts:
        total += part[...].astype(jnp.float32)
    out_ref[...] = total


def add_far(acc, parts, passing):
    here = pl.BlockSpec(memory_space=pltpu.VMEM)
    anywhere = pl.BlockSpec(memory_space=pl.ANY)
    return pl.pallas_call(
        add_far_kernel,
        in_specs=[here] * (1 + len(parts)) + [anywhere],
        out_specs=[here, anywhere],
        out_shape=[
            jax.ShapeDtypeStruct(acc.shape, jnp.float32),
            jax.ShapeDtypeStruct(passing.shape, passing.dtype),
        ],
        input_output_aliases={1 + len(parts): 1},
        compiler_params=SMALL_PARAMS,
        name="add_far",
    )(acc, *parts, passing)


def add_sums_kernel(total_ref, near_ref, *out_refs):
    total = total_ref[...] + near_ref[...].astype(jnp.float32)
    scaled = jnp.concatenate([total[:, :HD] * SCALE, total[:, HD:]], axis=1).astype(jnp.bfloat16)
    for place, out_ref in enumerate(out_refs):
        out_ref[...] = scaled[place * TILE : (place + 1) * TILE]


def add_sums(total, near):
    return pl.pallas_call(
        add_sums_kernel,
        in_specs=[HERE] * 2,
        out_specs=[HERE] * QUAD,
        out_shape=[jax.ShapeDtypeStruct((TILE, 2 * HD), jnp.bfloat16)] * QUAD,
        compiler_params=SMALL_PARAMS,
        name="add_sums",
    )(total, near)


FLIPS = (0, 2, 1, 3)


def place_queries_kernel(me_ref, *refs):
    for flip, piece in zip(FLIPS, refs[:-1]):
        refs[-1][:, head_columns(own_head(me_ref) ^ flip, ROWS)] = piece[:TILE, :]


def place_queries(me, *pieces):
    return pl.pallas_call(
        place_queries_kernel,
        in_specs=[SCALARS] + [HERE] * 4,
        out_specs=HERE,
        out_shape=jax.ShapeDtypeStruct((TILE, QH * HD), jnp.bfloat16),
        compiler_params=SMALL_PARAMS,
        name="place_queries",
    )(me, *pieces)


def place_keys_kernel(me_ref, *refs):
    dk_ref, dv_ref = refs[-2:]
    for flip, piece in zip(FLIPS, refs[:-2]):
        at = head_columns(own_head(me_ref) ^ flip, HD)
        dk_ref[:, at] = piece[:, :HD]
        dv_ref[:, at] = piece[:, HD:]


def place_keys(me, *pieces):
    return pl.pallas_call(
        place_keys_kernel,
        in_specs=[SCALARS] + [HERE] * 4,
        out_specs=[HERE] * 2,
        out_shape=[jax.ShapeDtypeStruct((TILE, KVH * HD), jnp.bfloat16)] * 2,
        compiler_params=SMALL_PARAMS,
        name="place_keys",
    )(me, *pieces)


def per_device(steps, queries, keys, values, outputs, out_grad, ancestors):
    level, side, core = (lax.axis_index(name) for name in ("level", "side", "core"))
    me = (QUAD * level + 2 * side + core).reshape(1).astype(jnp.int32)

    def to_partner(x, flip):
        return lax.ppermute(x, ("side", "core"), [(t, t ^ flip) for t in range(QUAD)])

    def after(x, done):
        return lax.optimization_barrier((x, done))[0]

    def up(x, shift):
        return lax.ppermute(x, "level", [(z, z + shift) for z in range(steps - shift)])

    def up_all(x):
        return [x] + [up(x, shift) for shift in range(1, steps)]

    def down(x, shift):
        return lax.ppermute(x, "level", [(z + shift, z) for z in range(steps - shift)])

    def exchange(by_head):
        mine, beside, across, corner = by_head
        return [mine, to_partner(across, 1), to_partner(beside, 2), to_partner(corner, 3)]

    kv_quad = exchange(pack_keys(me, keys, values))
    k_level, v_level = join_keys(*kv_quad)
    k_list = up_all(k_level)
    q_peer = to_partner(queries, 1)
    q_set = [queries, q_peer, to_partner(pack_queries(me, queries, after(q_peer, k_level)), 2)]
    g_peer = to_partner(out_grad, 1)
    g_set = [out_grad, g_peer, to_partner(pack_queries(me, out_grad, after(g_peer, k_list)), 2)]
    v_list = up_all(after(v_level, k_list))
    d_own, d_beside, d_pair = row_deltas(me, outputs, out_grad, after(k_level, k_list))
    d_pair = to_partner(d_pair, 1)
    d_set = [d_own, d_pair, to_partner(pack_deltas(d_beside, d_pair), 2)]

    lse = statistics(me, ancestors, q_set, k_list)
    common = (me, ancestors, q_set, g_set, d_set, lse)
    dq_far, *far = gradients("far", *common, k_list[2:], v_list[2:])
    back = [down(far[shift - 2], shift) for shift in range(2, steps)]
    dq_side, *accs = gradients("side", *common, k_list[:2], v_list[:2], dq_far)
    dq_side = to_partner(dq_side, 2)
    dq_own, dq_core, total, near = gradients(
        "own", *common, k_list[:2], v_list[:2], dq_far, *accs
    )
    near = down(near, 1)
    total, dq_core = add_far(total, back, dq_core)
    dq_core = to_partner(dq_core, 1)
    total = after(total, dq_core)

    sums = add_sums(total, near)
    dq_side = after(dq_side, sums)
    sums = [sums[0]] + [to_partner(sums[flip], flip) for flip in range(1, QUAD)]
    dq_corner = to_partner(dq_side[TILE:], 1)
    return (
        place_queries(me, dq_own, dq_core, dq_side, dq_corner),
        *place_keys(me, *sums),
    )


def solution(mesh):
    parts, tok = mesh.shape["parts"], mesh.shape["tok"]
    quads = Mesh(
        mesh.devices.reshape(parts, tok // QUAD, 2, 2), ("parts", "level", "side", "core")
    )
    rows = P(("parts", "level", "side", "core"), None)
    return jax.shard_map(
        functools.partial(per_device, tok // QUAD),
        mesh=quads,
        in_specs=(rows, rows, rows, rows, rows, P("parts", None)),
        out_specs=(rows, rows, rows),
        check_vma=False,
    )
```

```python
import functools
import math

import jax
import jax.numpy as jnp
from jax import lax
from jax.experimental import pallas as pl
from jax.experimental.pallas import tpu as pltpu
from jax.sharding import Mesh
from jax.sharding import PartitionSpec as P

QH = 32
KVH = 4
HD = 128
TILE = 128
GROUP = QH // KVH
ROWS = GROUP * TILE
PAIR = 2 * TILE
QUAD = 4
LEVEL = QUAD * TILE
SCALE = HD ** (-0.5)
SCALE2 = SCALE / math.log(2.0)
MASKED = -1e30
SCALARS = pl.BlockSpec(memory_space=pltpu.SMEM)
HERE = pl.BlockSpec(memory_space=pltpu.VMEM)
NT_DIMS = (((1,), (1,)), ((), ()))
PARAMS = pltpu.CompilerParams(vmem_limit_bytes=28 * 1024 * 1024)
SMALL_PARAMS = pltpu.CompilerParams(vmem_limit_bytes=16 * 1024 * 1024)


def delta_kernel(me_ref, out_ref, grad_ref, after_ref, mine_ref, beside_ref, pair_ref):
    for flip in range(QUAD):
        base = (own_head(me_ref) ^ flip) * ROWS
        delta_ref, row = ((mine_ref, 0), (beside_ref, 0), (pair_ref, 0), (pair_ref, GROUP))[flip]
        for head in range(GROUP):
            cols = pl.ds(pl.multiple_of(base + head * HD, HD), HD)
            product = out_ref[:, cols].astype(jnp.float32) * grad_ref[:, cols].astype(jnp.float32)
            delta_ref[row + head : row + head + 1, :] = jnp.sum(product.T, axis=0, keepdims=True)


def row_deltas(me, outputs, out_grad, after):
    return pl.pallas_call(
        delta_kernel,
        in_specs=[SCALARS, HERE, HERE, pl.BlockSpec(memory_space=pl.ANY)],
        out_specs=[HERE] * 3,
        out_shape=[
            jax.ShapeDtypeStruct((count * GROUP, TILE), jnp.float32) for count in (1, 1, 2)
        ],
        compiler_params=SMALL_PARAMS,
        name="row_deltas",
    )(me, outputs, out_grad, after)


def list_items(items, anc_ref, me, tiles, depth, part):
    tile_of, first_of, second_of, flags_of = items
    cut = ((me >> 2) - 1) * QUAD
    lowest = 2 if part == "far" else 0
    count = jnp.int32(0)
    for place, u in enumerate(tiles):
        tile = me ^ u
        near, live = jnp.int32(1), jnp.int32(1)
        for slot in range(depth):
            entry = anc_ref[tile, slot]
            live += (entry >= 0).astype(jnp.int32)
            near += ((entry >= 0) & (entry >= cut)).astype(jnp.int32)
        start = near if part == "far" else jnp.int32(0)
        stop = near if part == "near" else live
        chunks = (stop - start + 1) // 2

        def slot_of(entry, tile=tile):
            seen = jnp.where(entry == 0, tile, anc_ref[tile, jnp.clip(entry - 1, 0, depth - 1)])
            return ((me >> 2) - (seen >> 2) - lowest) * QUAD + ((seen ^ me) & (QUAD - 1))

        def note(chunk, carry, place=place, start=start, stop=stop, count=count, slot_of=slot_of):
            entry = start + 2 * chunk
            good = entry + 1 < stop
            first = slot_of(entry)
            tile_of[count + chunk] = place
            first_of[count + chunk] = first
            second_of[count + chunk] = jnp.where(good, slot_of(entry + 1), first)
            flags_of[count + chunk] = 1 + 2 * good.astype(jnp.int32) + 4 * (entry == 0).astype(jnp.int32)
            return carry

        lax.fori_loop(0, chunks, note, 0)
        count += chunks
    for extra in range(2):
        tile_of[count + extra] = 0
        first_of[count + extra] = 0
        second_of[count + extra] = 0
        flags_of[count + extra] = 0
    return count


def item_scratch(tiles, depth):
    return [pltpu.SMEM((tiles * ((depth + 2) // 2) + 2,), jnp.int32)] * 4


def slot_rows(slot):
    return pl.ds(pl.multiple_of(slot * TILE, TILE), TILE)


def two_tiles(ref, first, second):
    return jnp.concatenate([ref[slot_rows(first), :], ref[slot_rows(second), :]], axis=0)


def heads_below(ref, u, first, count):
    return jnp.concatenate(
        [ref[u, :, head * HD : (head + 1) * HD] for head in range(first, first + count)], axis=0
    )


def visible_mask(flags):
    key_pos = lax.broadcasted_iota(jnp.int32, (TILE, PAIR), 0)
    query_pos = lax.broadcasted_iota(jnp.int32, (TILE, PAIR), 1) & (TILE - 1)
    return key_pos - query_pos <= jnp.where((flags & 4) != 0, 0, TILE)


def query_tiles(me_ref, own, peer, side):
    at = head_columns(own_head(me_ref), ROWS)
    return four_tiles(own.at[:, at], peer.at[:, at], side, TILE)


def four_tiles(own, peer, side, rows):
    return own, peer, side.at[:rows, :], side.at[rows:, :]


def stats_kernel(depth, steps, me_ref, anc_ref, *rest):
    q_refs, rest = query_tiles(me_ref, *rest[:3]), rest[3:]
    k_refs = rest[:steps]
    lse_ref, q_all, k_all, item_max, item_sum, *items = rest[steps:]
    me = me_ref[0]
    for u, q_ref in enumerate(q_refs):
        q_all[u] = q_ref[...]
    for shift, k_ref in enumerate(k_refs):
        k_all[shift * LEVEL : (shift + 1) * LEVEL, :] = k_ref[...]
    count = list_items(items, anc_ref, me, range(QUAD), depth, "all")
    tile_of, first_of, second_of, flags_of = items

    def one_item(index):
        u, flags = tile_of[index], flags_of[index]
        good = (flags & 2) != 0
        key_block = two_tiles(k_all, first_of[index], second_of[index])
        mask = visible_mask(flags)
        for pair in range(GROUP // 2):
            rows = slice(pair * PAIR, (pair + 1) * PAIR)
            raw = lax.dot_general(
                key_block,
                heads_below(q_all, u, 2 * pair, 2),
                NT_DIMS,
                preferred_element_type=jnp.float32,
            )
            top, low = jnp.where(mask, raw[:TILE], MASKED), raw[TILE:]
            low_max = jnp.max(low, axis=0, keepdims=True)
            new_max = jnp.maximum(
                jnp.max(top, axis=0, keepdims=True), jnp.where(good, low_max, MASKED)
            )
            low_base = jnp.where(good, new_max, -MASKED)
            item_max[index, :, rows] = new_max
            item_sum[index, :, rows] = jnp.sum(
                jnp.exp2((top - new_max) * SCALE2), axis=0, keepdims=True
            ) + jnp.sum(jnp.exp2((low - low_base) * SCALE2), axis=0, keepdims=True)

    def step(index, carry):
        one_item(2 * index)
        one_item(2 * index + 1)
        return carry

    lax.fori_loop(0, (count + 1) // 2, step, 0)

    lse_ref[...] = jnp.full_like(lse_ref, MASKED)

    def combine(index, carry):
        u = tile_of[index]
        old = lse_ref[u]
        new = item_max[index] * SCALE2 + jnp.log2(item_sum[index])
        top = jnp.maximum(old, new)
        lse_ref[u] = top + jnp.log2(jnp.exp2(old - top) + jnp.exp2(new - top))
        return carry

    lax.fori_loop(0, count, combine, 0)


def grads_kernel(depth, stage, steps, me_ref, anc_ref, *rest):
    q_refs, g_refs = query_tiles(me_ref, *rest[:3]), query_tiles(me_ref, *rest[3:6])
    d_refs, rest = four_tiles(*rest[6:9], GROUP), rest[9:]
    lse_ref, rest = rest[0], rest[1:]
    kv_refs, rest = rest[: 2 * steps], rest[2 * steps :]
    if stage != "far":
        dq_in, rest = rest[0], rest[1:]
    if stage == "own":
        dk_in, dv_in, rest = rest[0], rest[1], rest[2:]
    tiles = {"far": (0, 1, 2, 3), "side": (2, 3), "own": (0, 1)}[stage]
    if stage == "far":
        dq_acc, partial_refs, rest = rest[0], rest[1 : 1 + steps], rest[1 + steps :]
    elif stage == "side":
        dq_refs = (rest[0].at[:TILE, :], rest[0].at[TILE:, :])
        dk_acc, dv_acc, rest = rest[1], rest[2], rest[3:]
    else:
        dq_refs, partial_refs, rest = rest[:2], rest[2 : 2 + steps], rest[2 + steps :]
    items, rest = rest[:4], rest[4:]
    q_all, g_all, delta, k_all, v_all = rest[:5]
    buffers, rest = ((rest[5], rest[6]), (rest[7], rest[8])), rest[9:]
    if stage != "side":
        dk_acc, dv_acc, rest = rest[0], rest[1], rest[2:]
    if stage != "far":
        dq_acc = rest[0]
    me = me_ref[0]
    for place, u in enumerate(tiles):
        q_all[place] = q_refs[u][...]
        g_all[place] = g_refs[u][...]
        for head in range(GROUP):
            cols = slice(head * TILE, (head + 1) * TILE)
            delta[place, :, cols] = d_refs[u][head : head + 1, :]
    for shift in range(steps):
        k_all[shift * LEVEL : (shift + 1) * LEVEL, :] = kv_refs[shift][...]
        v_all[shift * LEVEL : (shift + 1) * LEVEL, :] = kv_refs[steps + shift][...]
    if stage == "own":
        dk_acc[...] = dk_in[...]
        dv_acc[...] = dv_in[...]
    else:
        dk_acc[...] = jnp.zeros_like(dk_acc)
        dv_acc[...] = jnp.zeros_like(dv_acc)
    if stage == "far":
        dq_acc[...] = jnp.zeros_like(dq_acc)
    else:
        dq_acc[...] = dq_in[tiles[0] : tiles[0] + 2]
    for buffer in buffers[1]:
        buffer[...] = jnp.zeros_like(buffer)
    count = list_items(items, anc_ref, me, tiles, depth, "far" if stage == "far" else "near")
    tile_of, first_of, second_of, flags_of = items

    def scores_part(index, low_ref, score_ref):
        place, flags = tile_of[index], flags_of[index]
        first, second = first_of[index], second_of[index]
        key_block = two_tiles(k_all, first, second)
        value_block = two_tiles(v_all, first, second)
        for pair in range(GROUP // 2):
            rows = slice(pair * PAIR, (pair + 1) * PAIR)
            raw = lax.dot_general(
                key_block,
                heads_below(q_all, place, 2 * pair, 2),
                NT_DIMS,
                preferred_element_type=jnp.float32,
            )
            grad_probs = lax.dot_general(
                value_block,
                heads_below(g_all, place, 2 * pair, 2),
                NT_DIMS,
                preferred_element_type=jnp.float32,
            )
            lse = lse_ref[tiles[0] + place, :, rows]
            away = delta[place, :, rows]
            for part in range(2):
                half = slice(part * TILE, (part + 1) * TILE)
                base = jnp.where((flags & (1 + part)) != 0, lse, -MASKED)
                attn = jnp.exp2(raw[half] * SCALE2 - base)
                if stage != "far" and part == 0:
                    attn = jnp.where(visible_mask(flags), attn, 0.0)
                low_ref[half, rows] = attn.astype(jnp.bfloat16)
                score_ref[half, rows] = (attn * (grad_probs[half] - away)).astype(jnp.bfloat16)

    def grads_part(index, low_ref, score_ref):
        index = jnp.maximum(index, 0)
        place, first, second = tile_of[index], first_of[index], second_of[index]
        dv = jnp.dot(
            low_ref[...], heads_below(g_all, place, 0, GROUP), preferred_element_type=jnp.float32
        )
        dk = jnp.dot(
            score_ref[...], heads_below(q_all, place, 0, GROUP), preferred_element_type=jnp.float32
        )
        dq_acc[place] += jnp.dot(
            two_tiles(k_all, first, second).T, score_ref[...], preferred_element_type=jnp.float32
        )
        dk_acc[slot_rows(first), :] += dk[:TILE]
        dk_acc[slot_rows(second), :] += dk[TILE:]
        dv_acc[slot_rows(first), :] += dv[:TILE]
        dv_acc[slot_rows(second), :] += dv[TILE:]

    def step(index, carry):
        scores_part(2 * index, *buffers[0])
        grads_part(2 * index - 1, *buffers[1])
        scores_part(2 * index + 1, *buffers[1])
        grads_part(2 * index, *buffers[0])
        return carry

    lax.fori_loop(0, count // 2, step, 0)

    @pl.when((count & 1) == 1)
    def _():
        scores_part(count - 1, *buffers[0])
        grads_part(count - 2, *buffers[1])
        grads_part(count - 1, *buffers[0])

    @pl.when(((count & 1) == 0) & (count > 0))
    def _():
        grads_part(count - 1, *buffers[1])


    if stage != "far":
        for place in range(2):
            for head in range(GROUP):
                cols = slice(head * HD, (head + 1) * HD)
                dq_refs[place][:, cols] = (dq_acc[place, :, cols] * SCALE).T.astype(jnp.bfloat16)
    if stage != "side":
        for shift, out_ref in enumerate(partial_refs):
            rows = slice(shift * LEVEL, (shift + 1) * LEVEL)
            out_ref[:, :HD] = dk_acc[rows, :].astype(out_ref.dtype)
            out_ref[:, HD:] = dv_acc[rows, :].astype(out_ref.dtype)


def work(ancestors, products):
    pairs = QUAD * (ancestors.shape[1] + 1)
    return pl.CostEstimate(
        flops=2 * products * pairs * GROUP * TILE * TILE * 2 * HD,
        transcendentals=pairs * GROUP * TILE * TILE,
        bytes_accessed=16 * 1024 * 1024,
    )


def own_head(me_ref):
    return ((me_ref[0] & 1) << 1) | ((me_ref[0] >> 1) & 1)


def statistics(me, ancestors, q_set, k_list):
    steps = len(k_list)
    items = item_scratch(QUAD, ancestors.shape[1])
    count = items[0].shape[0]
    return pl.pallas_call(
        functools.partial(stats_kernel, ancestors.shape[1], steps),
        grid_spec=pltpu.PrefetchScalarGridSpec(
            num_scalar_prefetch=2,
            grid=(1,),
            in_specs=[HERE] * (3 + steps),
            out_specs=HERE,
            scratch_shapes=[
                pltpu.VMEM((QUAD, TILE, ROWS), jnp.bfloat16),
                pltpu.VMEM((steps * LEVEL, HD), jnp.bfloat16),
                pltpu.VMEM((count, 1, ROWS), jnp.float32),
                pltpu.VMEM((count, 1, ROWS), jnp.float32),
                *items,
            ],
        ),
        out_shape=jax.ShapeDtypeStruct((QUAD, 1, ROWS), jnp.float32),
        compiler_params=PARAMS,
        cost_estimate=work(ancestors, 1),
        name="statistics",
    )(me, ancestors, *q_set, *k_list)


def gradients(stage, me, ancestors, q_set, g_set, d_set, lse, k_list, v_list, *carried):
    steps = len(k_list)
    tiles = QUAD if stage == "far" else 2
    acc = (steps * LEVEL, HD)
    wide = jax.ShapeDtypeStruct((TILE, ROWS), jnp.bfloat16)
    sums = [jax.ShapeDtypeStruct((LEVEL, 2 * HD), jnp.bfloat16)] * steps
    accs = [jax.ShapeDtypeStruct(acc, jnp.float32)] * 2
    if stage == "far":
        out_shape = [jax.ShapeDtypeStruct((QUAD, HD, ROWS), jnp.float32)] + sums
    elif stage == "side":
        out_shape = [jax.ShapeDtypeStruct((PAIR, ROWS), jnp.bfloat16)] + accs
    else:
        sums[0] = jax.ShapeDtypeStruct((LEVEL, 2 * HD), jnp.float32)
        out_shape = [wide, wide] + sums
    scratch = item_scratch(tiles, ancestors.shape[1]) + [
        pltpu.VMEM((tiles, TILE, ROWS), jnp.bfloat16),
        pltpu.VMEM((tiles, TILE, ROWS), jnp.bfloat16),
        pltpu.VMEM((tiles, 1, ROWS), jnp.float32),
        pltpu.VMEM(acc, jnp.bfloat16),
        pltpu.VMEM(acc, jnp.bfloat16),
    ]
    scratch += [pltpu.VMEM((PAIR, ROWS), jnp.bfloat16)] * 4
    if stage != "side":
        scratch += [pltpu.VMEM(acc, jnp.float32)] * 2
    if stage != "far":
        scratch.append(pltpu.VMEM((tiles, HD, ROWS), jnp.float32))
    return pl.pallas_call(
        functools.partial(grads_kernel, ancestors.shape[1], stage, steps),
        grid_spec=pltpu.PrefetchScalarGridSpec(
            num_scalar_prefetch=2,
            grid=(1,),
            in_specs=[HERE] * (10 + 2 * steps + len(carried)),
            out_specs=[HERE] * len(out_shape),
            scratch_shapes=scratch,
        ),
        out_shape=out_shape,
        compiler_params=PARAMS,
        cost_estimate=work(ancestors, 5),
        name=stage + "_grads",
    )(me, ancestors, *q_set, *g_set, *d_set, lse, *k_list, *v_list, *carried)


def head_columns(head, width):
    return pl.ds(pl.multiple_of(head * width, width), width)


def pack_keys_kernel(me_ref, keys, values, *out_refs):
    for flip, out_ref in enumerate(out_refs):
        at = head_columns(own_head(me_ref) ^ flip, HD)
        out_ref[:, :HD] = keys[:, at]
        out_ref[:, HD:] = values[:, at]


def pack_keys(me, keys, values):
    return pl.pallas_call(
        pack_keys_kernel,
        in_specs=[SCALARS, HERE, HERE],
        out_specs=[HERE] * QUAD,
        out_shape=[jax.ShapeDtypeStruct((TILE, 2 * HD), jnp.bfloat16)] * QUAD,
        compiler_params=SMALL_PARAMS,
        name="pack_keys",
    )(me, keys, values)


def join_keys_kernel(*refs):
    k_ref, v_ref = refs[-2:]
    for place, ref in enumerate(refs[:-2]):
        rows = slice(place * TILE, (place + 1) * TILE)
        k_ref[rows, :] = ref[:, :HD]
        v_ref[rows, :] = ref[:, HD:]


def join_keys(*pieces):
    return pl.pallas_call(
        join_keys_kernel,
        in_specs=[HERE] * QUAD,
        out_specs=[HERE] * 2,
        out_shape=[jax.ShapeDtypeStruct((LEVEL, HD), jnp.bfloat16)] * 2,
        compiler_params=SMALL_PARAMS,
        name="join_keys",
    )(*pieces)


def pack_queries_kernel(me_ref, own, peer, send_ref):
    at = head_columns(own_head(me_ref) ^ 1, ROWS)
    send_ref[:TILE, :] = own[:, at]
    send_ref[TILE:, :] = peer[:, at]


def pack_queries(me, own, peer):
    return pl.pallas_call(
        pack_queries_kernel,
        in_specs=[SCALARS, HERE, HERE],
        out_specs=HERE,
        out_shape=jax.ShapeDtypeStruct((PAIR, ROWS), jnp.bfloat16),
        compiler_params=SMALL_PARAMS,
        name="pack_queries",
    )(me, own, peer)


def pack_deltas_kernel(own, pair, send_ref):
    send_ref[:GROUP, :] = own[...]
    send_ref[GROUP:, :] = pair[GROUP:, :]


def pack_deltas(own, pair):
    return pl.pallas_call(
        pack_deltas_kernel,
        in_specs=[HERE] * 2,
        out_specs=HERE,
        out_shape=jax.ShapeDtypeStruct((2 * GROUP, TILE), jnp.float32),
        compiler_params=SMALL_PARAMS,
        name="pack_deltas",
    )(own, pair)


def add_far_kernel(total_ref, *refs):
    parts, out_ref = refs[:-3], refs[-2]
    total = total_ref[...]
    for part in parts:
        total += part[...].astype(jnp.float32)
    out_ref[...] = total


def add_far(acc, parts, passing):
    here = pl.BlockSpec(memory_space=pltpu.VMEM)
    anywhere = pl.BlockSpec(memory_space=pl.ANY)
    return pl.pallas_call(
        add_far_kernel,
        in_specs=[here] * (1 + len(parts)) + [anywhere],
        out_specs=[here, anywhere],
        out_shape=[
            jax.ShapeDtypeStruct(acc.shape, jnp.float32),
            jax.ShapeDtypeStruct(passing.shape, passing.dtype),
        ],
        input_output_aliases={1 + len(parts): 1},
        compiler_params=SMALL_PARAMS,
        name="add_far",
    )(acc, *parts, passing)


def add_sums_kernel(total_ref, near_ref, *out_refs):
    total = total_ref[...] + near_ref[...].astype(jnp.float32)
    scaled = jnp.concatenate([total[:, :HD] * SCALE, total[:, HD:]], axis=1).astype(jnp.bfloat16)
    for place, out_ref in enumerate(out_refs):
        out_ref[...] = scaled[place * TILE : (place + 1) * TILE]


def add_sums(total, near):
    return pl.pallas_call(
        add_sums_kernel,
        in_specs=[HERE] * 2,
        out_specs=[HERE] * QUAD,
        out_shape=[jax.ShapeDtypeStruct((TILE, 2 * HD), jnp.bfloat16)] * QUAD,
        compiler_params=SMALL_PARAMS,
        name="add_sums",
    )(total, near)


FLIPS = (0, 2, 1, 3)


def place_queries_kernel(me_ref, *refs):
    for flip, piece in zip(FLIPS, refs[:-1]):
        refs[-1][:, head_columns(own_head(me_ref) ^ flip, ROWS)] = piece[:TILE, :]


def place_queries(me, *pieces):
    return pl.pallas_call(
        place_queries_kernel,
        in_specs=[SCALARS] + [HERE] * 4,
        out_specs=HERE,
        out_shape=jax.ShapeDtypeStruct((TILE, QH * HD), jnp.bfloat16),
        compiler_params=SMALL_PARAMS,
        name="place_queries",
    )(me, *pieces)


def place_keys_kernel(me_ref, *refs):
    dk_ref, dv_ref = refs[-2:]
    for flip, piece in zip(FLIPS, refs[:-2]):
        at = head_columns(own_head(me_ref) ^ flip, HD)
        dk_ref[:, at] = piece[:, :HD]
        dv_ref[:, at] = piece[:, HD:]


def place_keys(me, *pieces):
    return pl.pallas_call(
        place_keys_kernel,
        in_specs=[SCALARS] + [HERE] * 4,
        out_specs=[HERE] * 2,
        out_shape=[jax.ShapeDtypeStruct((TILE, KVH * HD), jnp.bfloat16)] * 2,
        compiler_params=SMALL_PARAMS,
        name="place_keys",
    )(me, *pieces)


def per_device(steps, queries, keys, values, outputs, out_grad, ancestors):
    level, side, core = (lax.axis_index(name) for name in ("level", "side", "core"))
    me = (QUAD * level + 2 * side + core).reshape(1).astype(jnp.int32)

    def to_partner(x, flip):
        return lax.ppermute(x, ("side", "core"), [(t, t ^ flip) for t in range(QUAD)])

    def after(x, done):
        return lax.optimization_barrier((x, done))[0]

    def up(x, shift):
        return lax.ppermute(x, "level", [(z, z + shift) for z in range(steps - shift)])

    def up_all(x):
        return [x] + [up(x, shift) for shift in range(1, steps)]

    def down(x, shift):
        return lax.ppermute(x, "level", [(z + shift, z) for z in range(steps - shift)])

    def exchange(by_head):
        mine, beside, across, corner = by_head
        return [mine, to_partner(across, 1), to_partner(beside, 2), to_partner(corner, 3)]

    kv_quad = exchange(pack_keys(me, keys, values))
    k_level, v_level = join_keys(*kv_quad)
    k_list = up_all(k_level)
    q_peer = to_partner(queries, 1)
    q_set = [queries, q_peer, to_partner(pack_queries(me, queries, after(q_peer, k_level)), 2)]
    g_peer = to_partner(out_grad, 1)
    g_set = [out_grad, g_peer, to_partner(pack_queries(me, out_grad, after(g_peer, k_list)), 2)]
    v_list = up_all(after(v_level, k_list))
    d_own, d_beside, d_pair = row_deltas(me, outputs, out_grad, after(k_level, k_list))
    d_pair = to_partner(d_pair, 1)
    d_set = [d_own, d_pair, to_partner(pack_deltas(d_beside, d_pair), 2)]

    lse = statistics(me, ancestors, q_set, k_list)
    common = (me, ancestors, q_set, g_set, d_set, lse)
    dq_far, *far = gradients("far", *common, k_list[2:], v_list[2:])
    back = [down(far[shift - 2], shift) for shift in range(2, steps)]
    dq_side, *accs = gradients("side", *common, k_list[:2], v_list[:2], dq_far)
    dq_side = to_partner(dq_side, 2)
    dq_own, dq_core, total, near = gradients(
        "own", *common, k_list[:2], v_list[:2], dq_far, *accs
    )
    near = down(near, 1)
    total, dq_core = add_far(total, back, dq_core)
    dq_core = to_partner(dq_core, 1)
    total = after(total, dq_core)

    sums = add_sums(total, near)
    dq_side = after(dq_side, sums)
    sums = [sums[0]] + [to_partner(sums[flip], flip) for flip in range(1, QUAD)]
    dq_corner = to_partner(dq_side[TILE:], 1)
    return (
        place_queries(me, dq_own, dq_core, dq_side, dq_corner),
        *place_keys(me, *sums),
    )


def solution(mesh):
    parts, tok = mesh.shape["parts"], mesh.shape["tok"]
    quads = Mesh(
        mesh.devices.reshape(parts, tok // QUAD, 2, 2), ("parts", "level", "side", "core")
    )
    rows = P(("parts", "level", "side", "core"), None)
    return jax.shard_map(
        functools.partial(per_device, tok // QUAD),
        mesh=quads,
        in_specs=(rows, rows, rows, rows, rows, P("parts", None)),
        out_specs=(rows, rows, rows),
        check_vma=False,
    )
```

```python
import functools
import math

import jax
import jax.numpy as jnp
from jax import lax
from jax.experimental import pallas as pl
from jax.experimental.pallas import tpu as pltpu
from jax.sharding import Mesh
from jax.sharding import PartitionSpec as P

QH = 32
KVH = 4
HD = 128
TILE = 128
GROUP = QH // KVH
ROWS = GROUP * TILE
PAIR = 2 * TILE
QUAD = 4
LEVEL = QUAD * TILE
SCALE = HD ** (-0.5)
SCALE2 = SCALE / math.log(2.0)
MASKED = -1e30
SCALARS = pl.BlockSpec(memory_space=pltpu.SMEM)
HERE = pl.BlockSpec(memory_space=pltpu.VMEM)
NT_DIMS = (((1,), (1,)), ((), ()))
PARAMS = pltpu.CompilerParams(vmem_limit_bytes=28 * 1024 * 1024)
SMALL_PARAMS = pltpu.CompilerParams(vmem_limit_bytes=16 * 1024 * 1024)


def delta_kernel(me_ref, out_ref, grad_ref, after_ref, mine_ref, beside_ref, pair_ref):
    for flip in range(QUAD):
        base = (own_head(me_ref) ^ flip) * ROWS
        delta_ref, row = ((mine_ref, 0), (beside_ref, 0), (pair_ref, 0), (pair_ref, GROUP))[flip]
        for head in range(GROUP):
            cols = pl.ds(pl.multiple_of(base + head * HD, HD), HD)
            product = out_ref[:, cols].astype(jnp.float32) * grad_ref[:, cols].astype(jnp.float32)
            delta_ref[row + head : row + head + 1, :] = jnp.sum(product.T, axis=0, keepdims=True)


def row_deltas(me, outputs, out_grad, after):
    return pl.pallas_call(
        delta_kernel,
        in_specs=[SCALARS, HERE, HERE, pl.BlockSpec(memory_space=pl.ANY)],
        out_specs=[HERE] * 3,
        out_shape=[
            jax.ShapeDtypeStruct((count * GROUP, TILE), jnp.float32) for count in (1, 1, 2)
        ],
        compiler_params=SMALL_PARAMS,
        name="row_deltas",
    )(me, outputs, out_grad, after)


def list_items(items, anc_ref, me, tiles, depth, part):
    tile_of, first_of, second_of, flags_of = items
    cut = ((me >> 2) - 1) * QUAD
    lowest = 2 if part == "far" else 0
    count = jnp.int32(0)
    for place, u in enumerate(tiles):
        tile = me ^ u
        near, live = jnp.int32(1), jnp.int32(1)
        for slot in range(depth):
            entry = anc_ref[tile, slot]
            live += (entry >= 0).astype(jnp.int32)
            near += ((entry >= 0) & (entry >= cut)).astype(jnp.int32)
        start = near if part == "far" else jnp.int32(0)
        stop = near if part == "near" else live
        chunks = (stop - start + 1) // 2

        def slot_of(entry, tile=tile):
            seen = jnp.where(entry == 0, tile, anc_ref[tile, jnp.clip(entry - 1, 0, depth - 1)])
            return ((me >> 2) - (seen >> 2) - lowest) * QUAD + ((seen ^ me) & (QUAD - 1))

        def note(chunk, carry, place=place, start=start, stop=stop, count=count, slot_of=slot_of):
            entry = start + 2 * chunk
            good = entry + 1 < stop
            first = slot_of(entry)
            tile_of[count + chunk] = place
            first_of[count + chunk] = first
            second_of[count + chunk] = jnp.where(good, slot_of(entry + 1), first)
            flags_of[count + chunk] = 1 + 2 * good.astype(jnp.int32) + 4 * (entry == 0).astype(jnp.int32)
            return carry

        lax.fori_loop(0, chunks, note, 0)
        count += chunks
    for extra in range(2):
        tile_of[count + extra] = 0
        first_of[count + extra] = 0
        second_of[count + extra] = 0
        flags_of[count + extra] = 0
    return count


def item_scratch(tiles, depth):
    return [pltpu.SMEM((tiles * ((depth + 2) // 2) + 2,), jnp.int32)] * 4


def slot_rows(slot):
    return pl.ds(pl.multiple_of(slot * TILE, TILE), TILE)


def two_tiles(ref, first, second):
    return jnp.concatenate([ref[slot_rows(first), :], ref[slot_rows(second), :]], axis=0)


def heads_below(ref, u, first, count):
    return jnp.concatenate(
        [ref[u, :, head * HD : (head + 1) * HD] for head in range(first, first + count)], axis=0
    )


def visible_mask(flags):
    key_pos = lax.broadcasted_iota(jnp.int32, (TILE, PAIR), 0)
    query_pos = lax.broadcasted_iota(jnp.int32, (TILE, PAIR), 1) & (TILE - 1)
    return key_pos - query_pos <= jnp.where((flags & 4) != 0, 0, TILE)


def query_tiles(me_ref, own, peer, side):
    at = head_columns(own_head(me_ref), ROWS)
    return four_tiles(own.at[:, at], peer.at[:, at], side, TILE)


def four_tiles(own, peer, side, rows):
    return own, peer, side.at[:rows, :], side.at[rows:, :]


def stats_kernel(depth, steps, me_ref, anc_ref, *rest):
    q_refs, rest = query_tiles(me_ref, *rest[:3]), rest[3:]
    k_refs = rest[:steps]
    lse_ref, q_all, k_all, item_max, item_sum, *items = rest[steps:]
    me = me_ref[0]
    for u, q_ref in enumerate(q_refs):
        q_all[u] = q_ref[...]
    for shift, k_ref in enumerate(k_refs):
        k_all[shift * LEVEL : (shift + 1) * LEVEL, :] = k_ref[...]
    count = list_items(items, anc_ref, me, range(QUAD), depth, "all")
    tile_of, first_of, second_of, flags_of = items

    def one_item(index):
        u, flags = tile_of[index], flags_of[index]
        good = (flags & 2) != 0
        key_block = two_tiles(k_all, first_of[index], second_of[index])
        mask = visible_mask(flags)
        for pair in range(GROUP // 2):
            rows = slice(pair * PAIR, (pair + 1) * PAIR)
            raw = lax.dot_general(
                key_block,
                heads_below(q_all, u, 2 * pair, 2),
                NT_DIMS,
                preferred_element_type=jnp.float32,
            )
            top, low = jnp.where(mask, raw[:TILE], MASKED), raw[TILE:]
            low_max = jnp.max(low, axis=0, keepdims=True)
            new_max = jnp.maximum(
                jnp.max(top, axis=0, keepdims=True), jnp.where(good, low_max, MASKED)
            )
            low_base = jnp.where(good, new_max, -MASKED)
            item_max[index, :, rows] = new_max
            item_sum[index, :, rows] = jnp.sum(
                jnp.exp2((top - new_max) * SCALE2), axis=0, keepdims=True
            ) + jnp.sum(jnp.exp2((low - low_base) * SCALE2), axis=0, keepdims=True)

    def step(index, carry):
        one_item(2 * index)
        one_item(2 * index + 1)
        return carry

    lax.fori_loop(0, (count + 1) // 2, step, 0)

    lse_ref[...] = jnp.full_like(lse_ref, MASKED)

    def combine(index, carry):
        u = tile_of[index]
        old = lse_ref[u]
        new = item_max[index] * SCALE2 + jnp.log2(item_sum[index])
        top = jnp.maximum(old, new)
        lse_ref[u] = top + jnp.log2(jnp.exp2(old - top) + jnp.exp2(new - top))
        return carry

    lax.fori_loop(0, count, combine, 0)


def grads_kernel(depth, stage, steps, me_ref, anc_ref, *rest):
    q_refs, g_refs = query_tiles(me_ref, *rest[:3]), query_tiles(me_ref, *rest[3:6])
    d_refs, rest = four_tiles(*rest[6:9], GROUP), rest[9:]
    lse_ref, rest = rest[0], rest[1:]
    kv_refs, rest = rest[: 2 * steps], rest[2 * steps :]
    if stage != "far":
        dq_in, rest = rest[0], rest[1:]
    if stage == "own":
        dk_in, dv_in, rest = rest[0], rest[1], rest[2:]
    tiles = {"far": (0, 1, 2, 3), "side": (2, 3), "own": (0, 1)}[stage]
    if stage == "far":
        dq_acc, partial_refs, rest = rest[0], rest[1 : 1 + steps], rest[1 + steps :]
    elif stage == "side":
        dq_refs = (rest[0].at[:TILE, :], rest[0].at[TILE:, :])
        dk_acc, dv_acc, rest = rest[1], rest[2], rest[3:]
    else:
        dq_refs, partial_refs, rest = rest[:2], rest[2 : 2 + steps], rest[2 + steps :]
    items, rest = rest[:4], rest[4:]
    q_all, g_all, delta, k_all, v_all = rest[:5]
    buffers, rest = ((rest[5], rest[6]), (rest[7], rest[8])), rest[9:]
    if stage != "side":
        dk_acc, dv_acc, rest = rest[0], rest[1], rest[2:]
    if stage != "far":
        dq_acc = rest[0]
    me = me_ref[0]
    for place, u in enumerate(tiles):
        q_all[place] = q_refs[u][...]
        g_all[place] = g_refs[u][...]
        for head in range(GROUP):
            cols = slice(head * TILE, (head + 1) * TILE)
            delta[place, :, cols] = d_refs[u][head : head + 1, :]
    for shift in range(steps):
        k_all[shift * LEVEL : (shift + 1) * LEVEL, :] = kv_refs[shift][...]
        v_all[shift * LEVEL : (shift + 1) * LEVEL, :] = kv_refs[steps + shift][...]
    if stage == "own":
        dk_acc[...] = dk_in[...]
        dv_acc[...] = dv_in[...]
    else:
        dk_acc[...] = jnp.zeros_like(dk_acc)
        dv_acc[...] = jnp.zeros_like(dv_acc)
    if stage == "far":
        dq_acc[...] = jnp.zeros_like(dq_acc)
    else:
        dq_acc[...] = dq_in[tiles[0] : tiles[0] + 2]
    for buffer in buffers[1]:
        buffer[...] = jnp.zeros_like(buffer)
    count = list_items(items, anc_ref, me, tiles, depth, "far" if stage == "far" else "near")
    tile_of, first_of, second_of, flags_of = items

    def scores_part(index, low_ref, score_ref):
        place, flags = tile_of[index], flags_of[index]
        first, second = first_of[index], second_of[index]
        key_block = two_tiles(k_all, first, second)
        value_block = two_tiles(v_all, first, second)
        for pair in range(GROUP // 2):
            rows = slice(pair * PAIR, (pair + 1) * PAIR)
            raw = lax.dot_general(
                key_block,
                heads_below(q_all, place, 2 * pair, 2),
                NT_DIMS,
                preferred_element_type=jnp.float32,
            )
            grad_probs = lax.dot_general(
                value_block,
                heads_below(g_all, place, 2 * pair, 2),
                NT_DIMS,
                preferred_element_type=jnp.float32,
            )
            lse = lse_ref[tiles[0] + place, :, rows]
            away = delta[place, :, rows]
            for part in range(2):
                half = slice(part * TILE, (part + 1) * TILE)
                base = jnp.where((flags & (1 + part)) != 0, lse, -MASKED)
                attn = jnp.exp2(raw[half] * SCALE2 - base)
                if stage != "far" and part == 0:
                    attn = jnp.where(visible_mask(flags), attn, 0.0)
                low_ref[half, rows] = attn.astype(jnp.bfloat16)
                score_ref[half, rows] = (attn * (grad_probs[half] - away)).astype(jnp.bfloat16)

    def grads_part(index, low_ref, score_ref):
        index = jnp.maximum(index, 0)
        place, first, second = tile_of[index], first_of[index], second_of[index]
        dv = jnp.dot(
            low_ref[...], heads_below(g_all, place, 0, GROUP), preferred_element_type=jnp.float32
        )
        dk = jnp.dot(
            score_ref[...], heads_below(q_all, place, 0, GROUP), preferred_element_type=jnp.float32
        )
        dq_acc[place] += jnp.dot(
            two_tiles(k_all, first, second).T, score_ref[...], preferred_element_type=jnp.float32
        )
        dk_acc[slot_rows(first), :] += dk[:TILE]
        dk_acc[slot_rows(second), :] += dk[TILE:]
        dv_acc[slot_rows(first), :] += dv[:TILE]
        dv_acc[slot_rows(second), :] += dv[TILE:]

    def step(index, carry):
        scores_part(2 * index, *buffers[0])
        grads_part(2 * index - 1, *buffers[1])
        scores_part(2 * index + 1, *buffers[1])
        grads_part(2 * index, *buffers[0])
        return carry

    lax.fori_loop(0, count // 2, step, 0)

    @pl.when((count & 1) == 1)
    def _():
        scores_part(count - 1, *buffers[0])
        grads_part(count - 2, *buffers[1])
        grads_part(count - 1, *buffers[0])

    @pl.when(((count & 1) == 0) & (count > 0))
    def _():
        grads_part(count - 1, *buffers[1])


    if stage != "far":
        for place in range(2):
            for head in range(GROUP):
                cols = slice(head * HD, (head + 1) * HD)
                dq_refs[place][:, cols] = (dq_acc[place, :, cols] * SCALE).T.astype(jnp.bfloat16)
    if stage != "side":
        for shift, out_ref in enumerate(partial_refs):
            rows = slice(shift * LEVEL, (shift + 1) * LEVEL)
            out_ref[:, :HD] = dk_acc[rows, :].astype(out_ref.dtype)
            out_ref[:, HD:] = dv_acc[rows, :].astype(out_ref.dtype)


def work(ancestors, products):
    pairs = QUAD * (ancestors.shape[1] + 1)
    return pl.CostEstimate(
        flops=2 * products * pairs * GROUP * TILE * TILE * 2 * HD,
        transcendentals=pairs * GROUP * TILE * TILE,
        bytes_accessed=16 * 1024 * 1024,
    )


def own_head(me_ref):
    return ((me_ref[0] & 1) << 1) | ((me_ref[0] >> 1) & 1)


def statistics(me, ancestors, q_set, k_list):
    steps = len(k_list)
    items = item_scratch(QUAD, ancestors.shape[1])
    count = items[0].shape[0]
    return pl.pallas_call(
        functools.partial(stats_kernel, ancestors.shape[1], steps),
        grid_spec=pltpu.PrefetchScalarGridSpec(
            num_scalar_prefetch=2,
            grid=(1,),
            in_specs=[HERE] * (3 + steps),
            out_specs=HERE,
            scratch_shapes=[
                pltpu.VMEM((QUAD, TILE, ROWS), jnp.bfloat16),
                pltpu.VMEM((steps * LEVEL, HD), jnp.bfloat16),
                pltpu.VMEM((count, 1, ROWS), jnp.float32),
                pltpu.VMEM((count, 1, ROWS), jnp.float32),
                *items,
            ],
        ),
        out_shape=jax.ShapeDtypeStruct((QUAD, 1, ROWS), jnp.float32),
        compiler_params=PARAMS,
        cost_estimate=work(ancestors, 1),
        name="statistics",
    )(me, ancestors, *q_set, *k_list)


def gradients(stage, me, ancestors, q_set, g_set, d_set, lse, k_list, v_list, *carried):
    steps = len(k_list)
    tiles = QUAD if stage == "far" else 2
    acc = (steps * LEVEL, HD)
    wide = jax.ShapeDtypeStruct((TILE, ROWS), jnp.bfloat16)
    sums = [jax.ShapeDtypeStruct((LEVEL, 2 * HD), jnp.bfloat16)] * steps
    accs = [jax.ShapeDtypeStruct(acc, jnp.float32)] * 2
    if stage == "far":
        out_shape = [jax.ShapeDtypeStruct((QUAD, HD, ROWS), jnp.float32)] + sums
    elif stage == "side":
        out_shape = [jax.ShapeDtypeStruct((PAIR, ROWS), jnp.bfloat16)] + accs
    else:
        sums[0] = jax.ShapeDtypeStruct((LEVEL, 2 * HD), jnp.float32)
        out_shape = [wide, wide] + sums
    scratch = item_scratch(tiles, ancestors.shape[1]) + [
        pltpu.VMEM((tiles, TILE, ROWS), jnp.bfloat16),
        pltpu.VMEM((tiles, TILE, ROWS), jnp.bfloat16),
        pltpu.VMEM((tiles, 1, ROWS), jnp.float32),
        pltpu.VMEM(acc, jnp.bfloat16),
        pltpu.VMEM(acc, jnp.bfloat16),
    ]
    scratch += [pltpu.VMEM((PAIR, ROWS), jnp.bfloat16)] * 4
    if stage != "side":
        scratch += [pltpu.VMEM(acc, jnp.float32)] * 2
    if stage != "far":
        scratch.append(pltpu.VMEM((tiles, HD, ROWS), jnp.float32))
    return pl.pallas_call(
        functools.partial(grads_kernel, ancestors.shape[1], stage, steps),
        grid_spec=pltpu.PrefetchScalarGridSpec(
            num_scalar_prefetch=2,
            grid=(1,),
            in_specs=[HERE] * (10 + 2 * steps + len(carried)),
            out_specs=[HERE] * len(out_shape),
            scratch_shapes=scratch,
        ),
        out_shape=out_shape,
        compiler_params=PARAMS,
        cost_estimate=work(ancestors, 5),
        name=stage + "_grads",
    )(me, ancestors, *q_set, *g_set, *d_set, lse, *k_list, *v_list, *carried)


def head_columns(head, width):
    return pl.ds(pl.multiple_of(head * width, width), width)


def pack_keys_kernel(me_ref, keys, values, *out_refs):
    for flip, out_ref in enumerate(out_refs):
        at = head_columns(own_head(me_ref) ^ flip, HD)
        out_ref[:, :HD] = keys[:, at]
        out_ref[:, HD:] = values[:, at]


def pack_keys(me, keys, values):
    return pl.pallas_call(
        pack_keys_kernel,
        in_specs=[SCALARS, HERE, HERE],
        out_specs=[HERE] * QUAD,
        out_shape=[jax.ShapeDtypeStruct((TILE, 2 * HD), jnp.bfloat16)] * QUAD,
        compiler_params=SMALL_PARAMS,
        name="pack_keys",
    )(me, keys, values)


def join_keys_kernel(*refs):
    k_ref, v_ref = refs[-2:]
    for place, ref in enumerate(refs[:-2]):
        rows = slice(place * TILE, (place + 1) * TILE)
        k_ref[rows, :] = ref[:, :HD]
        v_ref[rows, :] = ref[:, HD:]


def join_keys(*pieces):
    return pl.pallas_call(
        join_keys_kernel,
        in_specs=[HERE] * QUAD,
        out_specs=[HERE] * 2,
        out_shape=[jax.ShapeDtypeStruct((LEVEL, HD), jnp.bfloat16)] * 2,
        compiler_params=SMALL_PARAMS,
        name="join_keys",
    )(*pieces)


def pack_queries_kernel(me_ref, own, peer, send_ref):
    at = head_columns(own_head(me_ref) ^ 1, ROWS)
    send_ref[:TILE, :] = own[:, at]
    send_ref[TILE:, :] = peer[:, at]


def pack_queries(me, own, peer):
    return pl.pallas_call(
        pack_queries_kernel,
        in_specs=[SCALARS, HERE, HERE],
        out_specs=HERE,
        out_shape=jax.ShapeDtypeStruct((PAIR, ROWS), jnp.bfloat16),
        compiler_params=SMALL_PARAMS,
        name="pack_queries",
    )(me, own, peer)


def pack_deltas_kernel(own, pair, send_ref):
    send_ref[:GROUP, :] = own[...]
    send_ref[GROUP:, :] = pair[GROUP:, :]


def pack_deltas(own, pair):
    return pl.pallas_call(
        pack_deltas_kernel,
        in_specs=[HERE] * 2,
        out_specs=HERE,
        out_shape=jax.ShapeDtypeStruct((2 * GROUP, TILE), jnp.float32),
        compiler_params=SMALL_PARAMS,
        name="pack_deltas",
    )(own, pair)


def add_far_kernel(total_ref, *refs):
    parts, out_ref = refs[:-3], refs[-2]
    total = total_ref[...]
    for part in parts:
        total += part[...].astype(jnp.float32)
    out_ref[...] = total


def add_far(acc, parts, passing):
    here = pl.BlockSpec(memory_space=pltpu.VMEM)
    anywhere = pl.BlockSpec(memory_space=pl.ANY)
    return pl.pallas_call(
        add_far_kernel,
        in_specs=[here] * (1 + len(parts)) + [anywhere],
        out_specs=[here, anywhere],
        out_shape=[
            jax.ShapeDtypeStruct(acc.shape, jnp.float32),
            jax.ShapeDtypeStruct(passing.shape, passing.dtype),
        ],
        input_output_aliases={1 + len(parts): 1},
        compiler_params=SMALL_PARAMS,
        name="add_far",
    )(acc, *parts, passing)


def add_sums_kernel(total_ref, near_ref, *out_refs):
    total = total_ref[...] + near_ref[...].astype(jnp.float32)
    scaled = jnp.concatenate([total[:, :HD] * SCALE, total[:, HD:]], axis=1).astype(jnp.bfloat16)
    for place, out_ref in enumerate(out_refs):
        out_ref[...] = scaled[place * TILE : (place + 1) * TILE]


def add_sums(total, near):
    return pl.pallas_call(
        add_sums_kernel,
        in_specs=[HERE] * 2,
        out_specs=[HERE] * QUAD,
        out_shape=[jax.ShapeDtypeStruct((TILE, 2 * HD), jnp.bfloat16)] * QUAD,
        compiler_params=SMALL_PARAMS,
        name="add_sums",
    )(total, near)


FLIPS = (0, 2, 1, 3)


def place_queries_kernel(me_ref, *refs):
    for flip, piece in zip(FLIPS, refs[:-1]):
        refs[-1][:, head_columns(own_head(me_ref) ^ flip, ROWS)] = piece[:TILE, :]


def place_queries(me, *pieces):
    return pl.pallas_call(
        place_queries_kernel,
        in_specs=[SCALARS] + [HERE] * 4,
        out_specs=HERE,
        out_shape=jax.ShapeDtypeStruct((TILE, QH * HD), jnp.bfloat16),
        compiler_params=SMALL_PARAMS,
        name="place_queries",
    )(me, *pieces)


def place_keys_kernel(me_ref, *refs):
    dk_ref, dv_ref = refs[-2:]
    for flip, piece in zip(FLIPS, refs[:-2]):
        at = head_columns(own_head(me_ref) ^ flip, HD)
        dk_ref[:, at] = piece[:, :HD]
        dv_ref[:, at] = piece[:, HD:]


def place_keys(me, *pieces):
    return pl.pallas_call(
        place_keys_kernel,
        in_specs=[SCALARS] + [HERE] * 4,
        out_specs=[HERE] * 2,
        out_shape=[jax.ShapeDtypeStruct((TILE, KVH * HD), jnp.bfloat16)] * 2,
        compiler_params=SMALL_PARAMS,
        name="place_keys",
    )(me, *pieces)


def per_device(steps, queries, keys, values, outputs, out_grad, ancestors):
    level, side, core = (lax.axis_index(name) for name in ("level", "side", "core"))
    me = (QUAD * level + 2 * side + core).reshape(1).astype(jnp.int32)

    def to_partner(x, flip):
        return lax.ppermute(x, ("side", "core"), [(t, t ^ flip) for t in range(QUAD)])

    def after(x, done):
        return lax.optimization_barrier((x, done))[0]

    def up(x, shift):
        return lax.ppermute(x, "level", [(z, z + shift) for z in range(steps - shift)])

    def up_all(x):
        return [x] + [up(x, shift) for shift in range(1, steps)]

    def down(x, shift):
        return lax.ppermute(x, "level", [(z + shift, z) for z in range(steps - shift)])

    def exchange(by_head):
        mine, beside, across, corner = by_head
        return [mine, to_partner(across, 1), to_partner(beside, 2), to_partner(corner, 3)]

    kv_quad = exchange(pack_keys(me, keys, values))
    k_level, v_level = join_keys(*kv_quad)
    k_list = up_all(k_level)
    q_peer = to_partner(queries, 1)
    q_set = [queries, q_peer, to_partner(pack_queries(me, queries, after(q_peer, k_level)), 2)]
    g_peer = to_partner(out_grad, 1)
    g_set = [out_grad, g_peer, to_partner(pack_queries(me, out_grad, after(g_peer, k_list)), 2)]
    v_list = up_all(after(v_level, k_list))
    d_own, d_beside, d_pair = row_deltas(me, outputs, out_grad, after(k_level, k_list))
    d_pair = to_partner(d_pair, 1)
    d_set = [d_own, d_pair, to_partner(pack_deltas(d_beside, d_pair), 2)]

    lse = statistics(me, ancestors, q_set, k_list)
    common = (me, ancestors, q_set, g_set, d_set, lse)
    dq_far, *far = gradients("far", *common, k_list[2:], v_list[2:])
    back = [down(far[shift - 2], shift) for shift in range(2, steps)]
    dq_side, *accs = gradients("side", *common, k_list[:2], v_list[:2], dq_far)
    dq_side = to_partner(dq_side, 2)
    dq_own, dq_core, total, near = gradients(
        "own", *common, k_list[:2], v_list[:2], dq_far, *accs
    )
    near = down(near, 1)
    total, dq_core = add_far(total, back, dq_core)
    dq_core = to_partner(dq_core, 1)
    total = after(total, dq_core)

    sums = add_sums(total, near)
    dq_side = after(dq_side, sums)
    sums = [sums[0]] + [to_partner(sums[flip], flip) for flip in range(1, QUAD)]
    dq_corner = to_partner(dq_side[TILE:], 1)
    query_grad = place_queries(me, dq_own, dq_core, dq_side, dq_corner)
    return (query_grad, *place_keys(me, *after(sums, query_grad)))


def solution(mesh):
    parts, tok = mesh.shape["parts"], mesh.shape["tok"]
    quads = Mesh(
        mesh.devices.reshape(parts, tok // QUAD, 2, 2), ("parts", "level", "side", "core")
    )
    rows = P(("parts", "level", "side", "core"), None)
    return jax.shard_map(
        functools.partial(per_device, tok // QUAD),
        mesh=quads,
        in_specs=(rows, rows, rows, rows, rows, P("parts", None)),
        out_specs=(rows, rows, rows),
        check_vma=False,
    )
```
